32 devices in a mesh: blk: 4 (over y, core), docs: 8 (over z, x).
Axes of the slice: x: 2, y: 2, z: 4, core: 2. Of those that a mesh axis runs over, the one named last changes fastest.
Arguments:
- tokens: bfloat16 [8, 1024, 768], P('docs', 'blk'), may hold values from -6 to 6
- box_corners: int32 [4, 8, 1024], P(None, 'docs', 'blk'), may hold values from 0 to 999
- cotangent: bfloat16 [8, 1024, 768], P('docs', 'blk'), may hold values from -6 to 6
- w_query: bfloat16 [768, 768], replicated, may hold values from -0.21875 to 0.21875
- b_query: float32 [768], replicated, may hold values from -1.75 to 1.75
- w_key: bfloat16 [768, 768], replicated, may hold values from -0.21875 to 0.21875
- w_value: bfloat16 [768, 768], replicated, may hold values from -0.21875 to 0.21875
- b_value: float32 [768], replicated, may hold values from -1.75 to 1.75
- w_out: bfloat16 [768, 768], replicated, may hold values from -0.875 to 0.875
- b_out: float32 [768], replicated, may hold values from -1.75 to 1.75
- gain_first: float32 [768], replicated, may hold values from 0.25 to 1.75
- shift_first: float32 [768], replicated, may hold values from -1.75 to 1.75
- w_up: bfloat16 [768, 3072], replicated, may hold values from -0.21875 to 0.21875
- b_up: float32 [3072], replicated, may hold values from -3 to 3
- w_down: bfloat16 [3072, 768], replicated, may hold values from -0.109375 to 0.109375
- b_down: float32 [768], replicated, may hold values from -1.75 to 1.75
- gain_second: float32 [768], replicated, may hold values from 0.25 to 1.75
- shift_second: float32 [768], replicated, may hold values from -1.75 to 1.75
- table_order: float32 [32, 12], replicated, may hold values from -5 to 5
- table_horizontal: float32 [32, 12], replicated, may hold values from -5 to 5
- table_vertical: float32 [32, 12], replicated, may hold values from -5 to 5
Outputs:
- output: bfloat16 [8, 1024, 768], P('docs', 'blk')
- grad_tokens: bfloat16 [8, 1024, 768], P('docs', 'blk')
- grad_w_query: float32 [768, 768], P('blk')
- grad_b_query: float32 [768], P('blk')
- grad_w_key: float32 [768, 768], P('blk')
- grad_w_value: float32 [768, 768], P('blk')
- grad_b_value: float32 [768], P('blk')
- grad_w_out: float32 [768, 768], P('blk')
- grad_b_out: float32 [768], P('blk')
- grad_gain_first: float32 [768], P('blk')
- grad_shift_first: float32 [768], P('blk')
- grad_w_up: float32 [768, 3072], P('blk')
- grad_b_up: float32 [3072], P('blk')
- grad_w_down: float32 [3072, 768], P('blk')
- grad_b_down: float32 [768], P('blk')
- grad_gain_second: float32 [768], P('blk')
- grad_shift_second: float32 [768], P('blk')
- grad_table_order: float32 [32, 12], P('blk')
- grad_table_horizontal: float32 [32, 12], P('blk')
- grad_table_vertical: float32 [32, 12], P('blk')
The draws below stay inside these ranges and needn't reach their ends.
All inputs are finite; a program needn't handle non-finite values.
Results may differ from the reference program's by a relative error of at most 0.025.
Values may be sent and summed in bfloat16 or wider, within the bound.
No kernel may reach another device: no remote copies, remote signals or barrier semaphores. Data moves between devices by JAX's collectives and lax.ppermute only.
A program may use at most 256 MiB of HBM per device.

```python
import math
import jax
import jax.numpy as jnp
from jax import lax

D = 768
H = 12
HD = 64
FF = 3072
NB = 32
SEQ = 1024
DOCS = 8


def set_ends(entries, stream_key, smallest, high):
    longest = entries.shape.index(max(entries.shape))
    spots = []
    for shift in (0, 1):
        where = [jax.random.randint(jax.random.fold_in(stream_key, axis), (), 0, length) for axis, length in enumerate(entries.shape)]
        where[longest] = (where[longest] + shift) % entries.shape[longest]
        spots.append(tuple(where))
    return entries.at[spots[0]].set(smallest).at[spots[1]].set(high)


def level_of(own_key, shape, pieces, least, high):
    def one(position, shards_of):
        steps = jax.random.uniform(jax.random.fold_in(jax.random.fold_in(own_key, 6), position), (shards_of,), jnp.float32, least / len(pieces), high / len(pieces))
        return jnp.repeat(jnp.exp(steps), shape[position] // shards_of).reshape((-1,) + (1,) * (len(shape) - position - 1))

    level = one(*pieces[0])
    for cut in pieces[1:]:
        level = level * one(*cut)
    return level


def bell_draw(rng, dims, scale, limit, cuts=(), held_as=jnp.bfloat16):
    loudness = level_of(rng, dims, cuts, -0.22, 0.18) if cuts else 1.0
    entries = jax.random.normal(rng, dims, jnp.float32) * scale * loudness
    return jnp.minimum(jnp.maximum(entries, -limit), limit).astype(held_as)


def setup_inputs(seed: int = 0) -> dict:
    key_of = jax.random.split(jax.random.key(seed), 22)
    return {
        "tokens": bell_draw(key_of[0], (DOCS, SEQ, D), 1.0, 6.0, ((0, 8), (1, 4))),
        "box_corners": set_ends(jax.random.randint(key_of[1], (4, DOCS, SEQ), 0, 1000), jax.random.fold_in(key_of[1], 1), 0, 999).astype(jnp.int32),
        "cotangent": bell_draw(key_of[2], (DOCS, SEQ, D), 1.0, 6.0, ((0, 8), (1, 4))),
        "w_query": bell_draw(key_of[3], (D, D), D ** -0.5, 0.21875),
        "b_query": bell_draw(key_of[4], (D,), 0.3, 1.75, (), jnp.float32),
        "w_key": bell_draw(key_of[5], (D, D), D ** -0.5, 0.21875),
        "w_value": bell_draw(key_of[6], (D, D), D ** -0.5, 0.21875),
        "b_value": bell_draw(key_of[7], (D,), 0.3, 1.75, (), jnp.float32),
        "w_out": bell_draw(key_of[8], (D, D), (D // 16) ** -0.5, 0.875),
        "b_out": bell_draw(key_of[9], (D,), 0.3, 1.75, (), jnp.float32),
        "gain_first": jnp.clip(1.0 + 0.15 * jax.random.normal(key_of[10], (D,), jnp.float32), 0.25, 1.75),
        "shift_first": bell_draw(key_of[11], (D,), 0.3, 1.75, (), jnp.float32),
        "w_up": bell_draw(key_of[12], (D, FF), D ** -0.5, 0.21875),
        "b_up": bell_draw(key_of[13], (FF,), 0.5, 3.0, (), jnp.float32),
        "w_down": bell_draw(key_of[14], (FF, D), FF ** -0.5, 0.109375),
        "b_down": bell_draw(key_of[15], (D,), 0.3, 1.75, (), jnp.float32),
        "gain_second": jnp.clip(1.0 + 0.15 * jax.random.normal(key_of[16], (D,), jnp.float32), 0.25, 1.75),
        "shift_second": bell_draw(key_of[17], (D,), 0.3, 1.75, (), jnp.float32),
        "table_order": bell_draw(key_of[18], (NB, H), 0.8, 5.0, (), jnp.float32),
        "table_horizontal": bell_draw(key_of[19], (NB, H), 0.8, 5.0, (), jnp.float32),
        "table_vertical": bell_draw(key_of[20], (NB, H), 0.8, 5.0, (), jnp.float32),
    }


@jax.custom_vjp
def low(v):
    return lax.optimization_barrier(v.astype(jnp.bfloat16)).astype(jnp.float32)

@jax.custom_vjp
def low_back(v):
    return v

def low_keep(v):
    return (low(v), None)

def low_pass(kept, grad):
    return (grad,)

def back_keep(v):
    return (v, None)

def back_low(kept, grad):
    return (low(grad),)
low.defvjp(low_keep, low_pass)
low_back.defvjp(back_keep, back_low)
ORDER_LIMITS = (1, 2, 3, 4, 5, 6, 7, 8, 12, 16, 23, 32, 45, 64, 91)
BOX_LIMITS = (2, 4, 6, 8, 12, 16, 24, 32, 48, 64, 96, 128, 192, 256, 384)
EPSILON = 1e-05

def bucketize(offsets, limits):
    magnitude = jnp.abs(offsets)
    bucket_id = jnp.zeros(offsets.shape, jnp.int32)
    for threshold in limits:
        bucket_id = bucket_id + (magnitude >= threshold).astype(jnp.int32)
    return bucket_id + 16 * (offsets > 0).astype(jnp.int32)

def normalize(summed, gain, shift):
    centred = summed - lax.optimization_barrier(jnp.mean(summed, axis=-1, keepdims=True))
    spread = lax.optimization_barrier(jnp.mean(centred * centred, axis=-1, keepdims=True))
    return centred * lax.rsqrt(spread + EPSILON) * gain + shift

def matmul(left, right):
    return jnp.einsum('bsd,df->bsf', left, right, precision=lax.Precision.HIGHEST)

def layer(params, inputs, centre_x, centre_y):
    w_query, b_query, w_key, w_value, b_value, w_out, b_out, gain_first, shift_first, w_up, b_up, w_down, b_down, gain_second, shift_second, table_order, table_horizontal, table_vertical = params
    doc_count, doc_length, model_width = inputs.shape

    def split_heads(flat):
        return flat.reshape(doc_count, doc_length, H, HD)
    queries = low(low_back(matmul(inputs, w_query) + b_query))
    key_rows = low(low_back(matmul(inputs, w_key)))
    value_rows = low(low_back(matmul(inputs, w_value) + b_value))
    positions = jnp.arange(doc_length, dtype=jnp.int32)
    order_bucket = bucketize(positions[None, :] - positions[:, None], ORDER_LIMITS)
    across_bucket = bucketize(centre_x[:, None, :] - centre_x[:, :, None], BOX_LIMITS)
    down_bucket = bucketize(centre_y[:, None, :] - centre_y[:, :, None], BOX_LIMITS)
    bias = jnp.transpose(table_order[order_bucket], (2, 0, 1))[None]
    bias = bias + jnp.transpose(table_horizontal[across_bucket], (0, 3, 1, 2))
    bias = bias + jnp.transpose(table_vertical[down_bucket], (0, 3, 1, 2))
    raw = jnp.einsum('bqhe,bkhe->bhqk', split_heads(queries), split_heads(key_rows), precision=lax.Precision.HIGHEST)
    scores = low_back(raw * HD ** (-0.5) + bias)
    shifted = scores - lax.optimization_barrier(jnp.max(scores, axis=-1, keepdims=True))
    raised = jnp.exp(shifted)
    chances = low(raised / lax.optimization_barrier(jnp.sum(raised, axis=-1, keepdims=True)))
    mixed_out = jnp.einsum('bhqk,bkhe->bqhe', chances, split_heads(value_rows), precision=lax.Precision.HIGHEST).reshape(doc_count, doc_length, model_width)
    mixed_out = low(low_back(mixed_out))
    branch = low_back(matmul(mixed_out, w_out) + b_out)
    first_norm = normalize(inputs + branch, gain_first, shift_first)
    hidden = low_back(matmul(low(first_norm), w_up) + b_up)
    active = low(jax.nn.gelu(hidden, approximate=False))
    second = low_back(matmul(active, w_down) + b_down)
    return normalize(first_norm + second, gain_second, shift_second)

def reference(tokens, box_corners, cotangent, w_query, b_query, w_key, w_value, b_value, w_out, b_out, gain_first, shift_first, w_up, b_up, w_down, b_down, gain_second, shift_second, table_order, table_horizontal, table_vertical):
    params = (w_query.astype(jnp.float32), b_query, w_key.astype(jnp.float32), w_value.astype(jnp.float32), b_value, w_out.astype(jnp.float32), b_out, gain_first, shift_first, w_up.astype(jnp.float32), b_up, w_down.astype(jnp.float32), b_down, gain_second, shift_second, table_order, table_horizontal, table_vertical)
    centre_x = box_corners[0] + box_corners[2]
    centre_y = box_corners[1] + box_corners[3]
    group_size = math.gcd(DOCS, 4)
    group_count = DOCS // group_size

    def by_group(array):
        return array.reshape((group_count, group_size) + array.shape[1:])
    group_data = (by_group(tokens.astype(jnp.float32)), by_group(centre_x), by_group(centre_y), by_group(cotangent.astype(jnp.float32)))
    grad_start = jax.tree.map(jnp.zeros_like, params)

    def one_group(grad_total, group_item):
        tokens_in, across_in, down_in, upstream = group_item
        layer_out, pull_back = jax.vjp(lambda weights_in, rows_in: layer(weights_in, rows_in, across_in, down_in), params, tokens_in)
        grad_params, grad_rows = pull_back(upstream)
        grad_total = jax.tree.map(jnp.add, grad_total, grad_params)
        return (grad_total, (layer_out, grad_rows))
    grad_total, (layer_out, grad_rows) = lax.scan(one_group, grad_start, group_data)
    output = layer_out.reshape(tokens.shape).astype(jnp.bfloat16)
    grad_tokens = grad_rows.reshape(tokens.shape).astype(jnp.bfloat16)
    return (output, grad_tokens, grad_total[0], grad_total[1], grad_total[2], grad_total[3], grad_total[4], grad_total[5], grad_total[6], grad_total[7], grad_total[8], grad_total[9], grad_total[10], grad_total[11], grad_total[12], grad_total[13], grad_total[14], grad_total[15], grad_total[16], grad_total[17])
```

```python
import functools

import jax
import jax.numpy as jnp
from jax import lax
from jax.experimental import pallas as pl
from jax.experimental.pallas import tpu as pltpu
from jax.sharding import PartitionSpec as P

ORDER_LIMITS = (1, 2, 3, 4, 5, 6, 7, 8, 12, 16, 23, 32, 45, 64, 91)
BOX_LIMITS = (2, 4, 6, 8, 12, 16, 24, 32, 48, 64, 96, 128, 192, 256, 384)
EPSILON = 1e-05
LANES = 128
PAIR = 128
VMEM_LIMIT = 56 * 1024 * 1024


def forward_kernel(table_ref, order_ref, across_ref, down_ref, query_ref, key_ref, value_ref,
                   raised_ref, mixed_ref, inverse_ref, score_ref, value_sums_ref):
    keys, queries = order_ref.shape
    head_size = PAIR // 2
    rows = lax.broadcasted_iota(jnp.int32, (PAIR, queries), 0)
    query_pair = query_ref[...]
    zero = jnp.zeros_like(query_pair)
    both = jnp.concatenate(
        [jnp.where(rows < head_size, query_pair, zero), jnp.where(rows >= head_size, query_pair, zero)], axis=1
    )
    step = 128
    peak = jnp.full((8, 2 * queries), -jnp.inf, jnp.float32)

    def first(block, peak):
        at = pl.multiple_of(block * step, step)
        raw = jnp.dot(key_ref[pl.ds(at, step), :], both, preferred_element_type=jnp.float32)
        peaks = []
        for lane in range(0, queries, LANES):
            picks = [ref[pl.ds(at, step), lane : lane + LANES] for ref in (order_ref, across_ref, down_ref)]
            for head in range(2):
                table = jnp.broadcast_to(table_ref[0, head : head + 1, :], (step, LANES))
                score = raw[:, head * queries + lane : head * queries + lane + LANES]
                for pick in picks:
                    score = score + jnp.take_along_axis(table, pick, axis=1, mode="promise_in_bounds")
                score_ref[pl.ds(at, step), head * queries + lane : head * queries + lane + LANES] = score
                peaks.append((head * queries + lane, jnp.max(score.reshape(step // 8, 8, LANES), axis=0)))
        peaks = jnp.concatenate([p for _, p in sorted(peaks, key=lambda item: item[0])], axis=1)
        return jnp.maximum(peak, peaks)

    peak = lax.fori_loop(0, keys // step, first, peak)
    peak = jnp.max(peak, axis=0, keepdims=True)
    value_sums_ref[0, :head_size, :] = value_ref[:head_size, :]
    value_sums_ref[1, :head_size, :] = value_ref[head_size:, :]
    value_sums_ref[:, head_size:, :] = jnp.ones((2, 16, keys), jnp.bfloat16)

    for head in range(2):
        for at in range(0, keys, step):
            lanes = slice(head * queries, (head + 1) * queries)
            raised = jnp.exp(score_ref[at : at + step, lanes] - peak[:, lanes]).astype(jnp.bfloat16)
            raised_ref[head, at : at + step, :] = raised
        sums = jnp.dot(value_sums_ref[head], raised_ref[head], preferred_element_type=jnp.float32)
        inverse = 1.0 / sums[head_size : head_size + 1, :]
        mixed_ref[head * head_size : (head + 1) * head_size, :] = sums[:head_size, :] * inverse
        inverse_ref[head] = inverse


def attention_forward(tables, order, across, down, query_t, keys, value_t):
    width, queries = query_t.shape
    length = keys.shape[0]
    pairs = width // PAIR
    whole = pl.BlockSpec((length, queries), lambda p: (0, 0))
    return pl.pallas_call(
        forward_kernel,
        grid=(pairs,),
        in_specs=[
            pl.BlockSpec((1, 2, LANES), lambda p: (p, 0, 0)),
            whole, whole, whole,
            pl.BlockSpec((PAIR, queries), lambda p: (p, 0)),
            pl.BlockSpec((length, PAIR), lambda p: (0, p)),
            pl.BlockSpec((PAIR, length), lambda p: (p, 0)),
        ],
        out_specs=[
            pl.BlockSpec((2, length, queries), lambda p: (p, 0, 0)),
            pl.BlockSpec((PAIR, queries), lambda p: (p, 0)),
            pl.BlockSpec((2, 1, queries), lambda p: (p, 0, 0)),
        ],
        out_shape=[
            jax.ShapeDtypeStruct((2 * pairs, length, queries), jnp.bfloat16),
            jax.ShapeDtypeStruct((width, queries), jnp.float32),
            jax.ShapeDtypeStruct((2 * pairs, 1, queries), jnp.float32),
        ],
        scratch_shapes=[
            pltpu.VMEM((length, 2 * queries), jnp.float32),
            pltpu.VMEM((2, PAIR // 2 + 16, length), jnp.bfloat16),
        ],
        compiler_params=pltpu.CompilerParams(vmem_limit_bytes=VMEM_LIMIT),
        cost_estimate=pl.CostEstimate(flops=4 * width * queries * length, bytes_accessed=16 << 20, transcendentals=0),
        name="attention_forward",
    )(tables, order, across, down, query_t, keys, value_t)


def backward_kernel(order_ref, across_ref, down_ref, raised_ref, query_ref, mixed_ref, dot_ref, value_ref, key_ref,
                    grad_query_ref, grad_key_ref, grad_value_ref, table_ref,
                    sum_ref, grad_ref, count_ref, *, heads, scale):
    slot = pl.program_id(0)
    keys, queries = order_ref.shape
    head_size = PAIR // 2
    group = 16
    per_super = 4
    supers = keys // (group * per_super)
    buckets = count_ref.shape[1] // group

    @pl.when(slot == 0)
    def _():
        sum_ref[...] = jnp.zeros_like(sum_ref)
        count_ref[...] = jnp.zeros_like(count_ref)

    rows = lax.broadcasted_iota(jnp.int32, (PAIR, queries), 0)
    for pair in range(heads // 2):
        at = slice(pair * PAIR, (pair + 1) * PAIR)
        query_pair = query_ref[at, :]
        mixed_pair = mixed_ref[at, :]
        zero = jnp.zeros_like(query_pair)
        query_both = [jnp.where(rows < head_size, query_pair, zero), jnp.where(rows >= head_size, query_pair, zero)]
        mixed_both = [jnp.where(rows < head_size, mixed_pair, zero), jnp.where(rows >= head_size, mixed_pair, zero)]
        query_both = jnp.concatenate(query_both, axis=1)
        mixed_both = jnp.concatenate(mixed_both, axis=1)
        grad_probs = jnp.dot(value_ref[:, at], mixed_both, preferred_element_type=jnp.float32)
        raised = jnp.concatenate([raised_ref[2 * pair], raised_ref[2 * pair + 1]], axis=1)
        dots = jnp.concatenate([dot_ref[2 * pair], dot_ref[2 * pair + 1]], axis=1)
        grad = (raised.astype(jnp.float32) * (grad_probs - dots)).astype(jnp.bfloat16)
        nt = (((1,), (1,)), ((), ()))
        grad_value_ref[:, at] = lax.dot_general(raised, mixed_both, nt, preferred_element_type=jnp.float32).astype(jnp.bfloat16)
        grad_key_ref[:, at] = lax.dot_general(grad, query_both, nt, preferred_element_type=jnp.float32).astype(jnp.bfloat16)
        for one in range(2):
            head = 2 * pair + one
            mine = grad[:, one * queries : (one + 1) * queries]
            feature = slice(head * head_size, (head + 1) * head_size)
            sum_ref[feature, :] += jnp.dot(key_ref[feature, :], mine, preferred_element_type=jnp.float32)
            for g in range(keys // group):
                grad_ref[g // per_super, head * group : (head + 1) * group, (g % per_super) * queries : (g % per_super + 1) * queries] = mine[g * group : (g + 1) * group, :]

    def tally(sup, _):
        grads = grad_ref[sup]
        for number, ref in enumerate((order_ref, across_ref, down_ref)):
            parts = []
            for sub in range(per_super):
                at = pl.multiple_of(sup * (group * per_super) + sub * group, group)
                ids = ref[pl.ds(at, group), :]
                parts.append(jnp.concatenate([jnp.where(ids == b, 1.0, 0.0).astype(jnp.bfloat16) for b in range(buckets)], axis=0))
            hot = jnp.concatenate(parts, axis=1)
            count_ref[number] += lax.dot_general(hot, grads, (((1,), (1,)), ((), ())), preferred_element_type=jnp.float32)
        return 0

    lax.fori_loop(0, supers, tally, 0)

    @pl.when(slot == pl.num_programs(0) - 1)
    def _():
        grad_query_ref[...] = (sum_ref[...] * scale).astype(jnp.bfloat16)
        place = lax.broadcasted_iota(jnp.int32, (buckets * group, heads * group), 0) % group
        other = lax.broadcasted_iota(jnp.int32, (buckets * group, heads * group), 1) % group
        for number in range(3):
            kept = jnp.where(place == other, count_ref[number], 0.0)
            table_ref[number] = jnp.sum(kept.reshape(buckets, group, heads * group), axis=1)


def attention_backward(order, across, down, raised, query_t, mixed_t, dots, values, key_t, scale, slots):
    width, queries = query_t.shape
    heads = raised.shape[0]
    length = values.shape[0]
    keys = length // slots
    buckets = 32
    group = 16
    ids = pl.BlockSpec((keys, queries), lambda s: (s, 0))
    full = pl.BlockSpec((width, queries), lambda s: (0, 0))
    rows = pl.BlockSpec((keys, width), lambda s: (s, 0))
    return pl.pallas_call(
        functools.partial(backward_kernel, heads=heads, scale=scale),
        grid=(slots,),
        in_specs=[
            ids, ids, ids,
            pl.BlockSpec((heads, keys, queries), lambda s: (0, s, 0)),
            full, full,
            pl.BlockSpec((heads, 1, queries), lambda s: (0, 0, 0)),
            rows,
            pl.BlockSpec((width, keys), lambda s: (0, s)),
        ],
        out_specs=[
            full, rows, rows,
            pl.BlockSpec((3, buckets, heads * group), lambda s: (0, 0, 0)),
        ],
        out_shape=[
            jax.ShapeDtypeStruct((width, queries), jnp.bfloat16),
            jax.ShapeDtypeStruct((length, width), jnp.bfloat16),
            jax.ShapeDtypeStruct((length, width), jnp.bfloat16),
            jax.ShapeDtypeStruct((3, buckets, heads * group), jnp.float32),
        ],
        scratch_shapes=[
            pltpu.VMEM((width, queries), jnp.float32),
            pltpu.VMEM((keys // (group * 4), heads * group, 4 * queries), jnp.bfloat16),
            pltpu.VMEM((3, buckets * group, heads * group), jnp.float32),
        ],
        compiler_params=pltpu.CompilerParams(vmem_limit_bytes=VMEM_LIMIT),
        cost_estimate=pl.CostEstimate(flops=8 * width * queries * length, bytes_accessed=16 << 20, transcendentals=0),
        name="attention_backward",
    )(order, across, down, raised, query_t, mixed_t, dots, values, key_t)


def bucketize(offsets, limits):
    magnitude = jnp.abs(offsets)
    bucket_id = jnp.zeros(offsets.shape, jnp.int32)
    for threshold in limits:
        bucket_id = bucket_id + (magnitude >= threshold).astype(jnp.int32)
    return bucket_id + 16 * (offsets > 0).astype(jnp.int32)


def normalize(summed, gain, shift):
    centred = summed - jnp.mean(summed, axis=-1, keepdims=True)
    spread = jnp.mean(centred * centred, axis=-1, keepdims=True)
    return centred * lax.rsqrt(spread + EPSILON) * gain + shift


def gelu_exact(values):
    return jax.nn.gelu(values, approximate=False)


def einsum(spec, left, right):
    return jnp.einsum(spec, left, right, preferred_element_type=jnp.float32)


def exchange(array, axis_name, distance):
    pairs = [(i, i ^ distance) for i in range(lax.axis_size(axis_name))]
    return lax.ppermute(array, axis_name, pairs)


def add_low(left, right):
    return (left.astype(jnp.float32) + right.astype(jnp.float32)).astype(jnp.bfloat16)


def half_of(array, dimension, which):
    length = array.shape[dimension] // 2
    return lax.dynamic_slice_in_dim(array, which * length, length, dimension)


def split_dimension(shape):
    if shape[0] % 32 == 0:
        return 0
    if shape[1] % 256 == 0:
        return 1
    return 0 if shape[0] % 2 == 0 else 1


def weight_grad_parts(left, right, spec):
    me = lax.axis_index("blk")
    rows = left.shape[1] // lax.axis_size("blk")

    def part(distance):
        return lax.dynamic_slice_in_dim(left, (me ^ distance) * rows, rows, 1)

    sent = einsum(spec, jnp.concatenate([part(1), part(3)], axis=1), right).astype(jnp.bfloat16)
    kept = einsum(spec, jnp.concatenate([part(0), part(2)], axis=1), right).astype(jnp.bfloat16)
    return (sent, kept)


def reduce_weight(parts):
    sent, kept = parts
    rows = kept.shape[0] // 2
    got = exchange(sent, "blk", 1)
    far = add_low(kept[rows:], got[rows:])
    near = add_low(kept[:rows], got[:rows])
    data = add_low(near, exchange(far, "blk", 2))
    here = lax.axis_index("docs")
    steps = []
    distance = 1
    while distance < lax.axis_size("docs"):
        dimension = split_dimension(data.shape)
        side = (here // distance) % 2
        got = exchange(half_of(data, dimension, 1 - side), "docs", distance)
        data = add_low(half_of(data, dimension, side), got)
        steps.append((dimension, side, distance))
        distance = distance * 2
    for dimension, side, distance in reversed(steps):
        got = exchange(data, "docs", distance)
        data = jnp.where(
            side == 0,
            jnp.concatenate([data, got], axis=dimension),
            jnp.concatenate([got, data], axis=dimension),
        )
    return data.astype(jnp.float32)


def body(
    tokens,
    box_corners,
    cotangent,
    w_query,
    b_query,
    w_key,
    w_value,
    b_value,
    w_out,
    b_out,
    gain_first,
    shift_first,
    w_up,
    b_up,
    w_down,
    b_down,
    gain_second,
    shift_second,
    table_order,
    table_horizontal,
    table_vertical,
):
    docs_here, doc_length, model_width = tokens.shape
    bucket_total, head_count = table_order.shape
    head_size = model_width // head_count
    score_scale = head_size ** (-0.5)
    blk_count = lax.axis_size("blk")
    me = lax.axis_index("blk")
    rows_in = tokens.reshape(doc_length, model_width)

    centres = jnp.stack([box_corners[0, 0] + box_corners[2, 0], box_corners[1, 0] + box_corners[3, 0]])
    centres = centres.astype(jnp.float32)
    centre_slots = [centres] + [exchange(centres, "blk", s) for s in range(1, blk_count)]
    core_rows = exchange(rows_in, "blk", 1)
    far_rows = exchange(rows_in, "blk", 2)
    rows_all = jnp.concatenate([rows_in, core_rows, far_rows, exchange(far_rows, "blk", 1)], axis=0)
    centres_all = jnp.concatenate(centre_slots, axis=1).astype(jnp.int32)
    centres_own = centres.astype(jnp.int32)

    inside = jnp.arange(doc_length, dtype=jnp.int32)
    key_place = jnp.concatenate([(me ^ s) * doc_length + inside for s in range(blk_count)])
    query_place = me * doc_length + inside
    order = bucketize(key_place[:, None] - query_place[None, :], ORDER_LIMITS)
    across = bucketize(centres_all[0][:, None] - centres_own[0][None, :], BOX_LIMITS)
    down = bucketize(centres_all[1][:, None] - centres_own[1][None, :], BOX_LIMITS)
    tables = jnp.concatenate([table_order, table_horizontal, table_vertical], axis=0).T
    tables = jnp.pad(tables, ((0, 0), (0, LANES - 3 * bucket_total))).reshape(head_count // 2, 2, LANES)

    query_t = (einsum("df,td->ft", w_query, rows_in) + b_query[:, None]).astype(jnp.bfloat16)
    query_t = query_t * jnp.bfloat16(score_scale)
    keys = einsum("td,df->tf", rows_all, w_key).astype(jnp.bfloat16)
    key_t = einsum("df,td->ft", w_key, rows_all).astype(jnp.bfloat16)
    values = (einsum("td,df->tf", rows_all, w_value) + b_value).astype(jnp.bfloat16)
    value_t = (einsum("df,td->ft", w_value, rows_all) + b_value[:, None]).astype(jnp.bfloat16)

    raised, mixed_t, inverse = attention_forward(
        tables, order, across + bucket_total, down + 2 * bucket_total, query_t, keys, value_t
    )

    mixed_low = mixed_t.astype(jnp.bfloat16)
    branch = einsum("ft,fd->td", mixed_low, w_out) + b_out
    inputs = rows_in.astype(jnp.float32)
    first_norm, pull_first = jax.vjp(normalize, inputs + branch, gain_first, shift_first)
    first_low = first_norm.astype(jnp.bfloat16)
    hidden = einsum("td,df->tf", first_low, w_up) + b_up
    active_full, pull_gelu = jax.vjp(gelu_exact, hidden)
    active = active_full.astype(jnp.bfloat16)
    second = einsum("td,df->tf", active, w_down) + b_down
    result, pull_second = jax.vjp(normalize, first_norm + second, gain_second, shift_second)
    output = result.astype(jnp.bfloat16).reshape(tokens.shape)
    upstream = cotangent.reshape(doc_length, model_width).astype(jnp.float32)
    grad_pre2, grad_gain_second, grad_shift_second = pull_second(upstream)
    grad_second = grad_pre2.astype(jnp.bfloat16)
    parts_down = weight_grad_parts(active, grad_second, "td,tf->df")
    grad_b_down = jnp.sum(grad_second.astype(jnp.float32), axis=0)
    grad_active = einsum("tf,df->td", grad_second, w_down)
    grad_hidden = pull_gelu(grad_active)[0].astype(jnp.bfloat16)
    parts_up = weight_grad_parts(first_low, grad_hidden, "td,tf->df")
    grad_b_up = jnp.sum(grad_hidden.astype(jnp.float32), axis=0)
    grad_first = grad_pre2 + einsum("tf,df->td", grad_hidden, w_up)
    grad_pre1, grad_gain_first, grad_shift_first = pull_first(grad_first)
    grad_branch = grad_pre1.astype(jnp.bfloat16)
    parts_out = weight_grad_parts(mixed_low.T, grad_branch, "td,tf->df")
    grad_b_out = jnp.sum(grad_branch.astype(jnp.float32), axis=0)

    heads_shape = (head_count, head_size, doc_length)
    grad_mixed_t = einsum("df,tf->dt", w_out, grad_branch).astype(jnp.bfloat16).astype(jnp.float32)
    scaled_t = (grad_mixed_t.reshape(heads_shape) * inverse).astype(jnp.bfloat16)
    dots = jnp.sum(scaled_t.astype(jnp.float32) * mixed_t.reshape(heads_shape), axis=1, keepdims=True)
    scaled_t = scaled_t.reshape(model_width, doc_length)

    grad_query_t, grad_keys, grad_values, tallies = attention_backward(
        order, across, down, raised, query_t, scaled_t, dots, values, key_t, score_scale, blk_count
    )
    table_sums = jnp.sum(tallies.reshape(3, bucket_total, head_count, -1), axis=-1)

    parts_value = weight_grad_parts(rows_all, grad_values, "td,tf->df")
    parts_key = weight_grad_parts(rows_all, grad_keys, "td,tf->df")
    parts_query = weight_grad_parts(rows_in, grad_query_t, "td,ft->df")
    grad_b_query = jnp.sum(grad_query_t.astype(jnp.float32), axis=1)
    grad_b_value = jnp.sum(grad_values.astype(jnp.float32), axis=0)

    shared = einsum("tf,df->td", grad_keys, w_key) + einsum("tf,df->td", grad_values, w_value)
    shared = shared.reshape(blk_count, doc_length, model_width)
    near = exchange(jnp.concatenate([shared[1], shared[3]]).astype(jnp.bfloat16), "blk", 1).astype(jnp.float32)
    far = exchange((shared[2] + near[doc_length:]).astype(jnp.bfloat16), "blk", 2).astype(jnp.float32)
    grad_inputs = grad_pre1 + einsum("ft,df->td", grad_query_t, w_query) + shared[0] + near[:doc_length] + far
    grad_tokens = grad_inputs.astype(jnp.bfloat16).reshape(tokens.shape)

    small = [
        grad_b_query,
        grad_b_value,
        grad_b_out,
        grad_gain_first,
        grad_shift_first,
        grad_b_up,
        grad_b_down,
        grad_gain_second,
        grad_shift_second,
        table_sums[0],
        table_sums[1],
        table_sums[2],
    ]
    packed = jnp.concatenate([piece.reshape(blk_count, -1) for piece in small], axis=1)
    packed = lax.psum(packed, ("blk", "docs"))
    mine = lax.dynamic_slice_in_dim(packed, me, 1, 0)[0]
    small_out = []
    cursor = 0
    for piece in small:
        length = piece.size // blk_count
        small_out.append(mine[cursor : cursor + length].reshape((piece.shape[0] // blk_count,) + piece.shape[1:]))
        cursor = cursor + length

    grad_w_down = reduce_weight(parts_down)
    grad_w_up = reduce_weight(parts_up)
    grad_w_out = reduce_weight(parts_out)
    grad_w_value = reduce_weight(parts_value)
    grad_w_key = reduce_weight(parts_key)
    grad_w_query = reduce_weight(parts_query)
    return (
        output,
        grad_tokens,
        grad_w_query,
        small_out[0],
        grad_w_key,
        grad_w_value,
        small_out[1],
        grad_w_out,
        small_out[2],
        small_out[3],
        small_out[4],
        grad_w_up,
        small_out[5],
        grad_w_down,
        small_out[6],
        small_out[7],
        small_out[8],
        small_out[9],
        small_out[10],
        small_out[11],
    )


def solution(mesh):
    return jax.shard_map(
        body,
        mesh=mesh,
        in_specs=(
            P("docs", "blk", None),
            P(None, "docs", "blk"),
            P("docs", "blk", None),
            P(),
            P(),
            P(),
            P(),
            P(),
            P(),
            P(),
            P(),
            P(),
            P(),
            P(),
            P(),
            P(),
            P(),
            P(),
            P(),
            P(),
            P(),
        ),
        out_specs=(
            P("docs", "blk", None),
            P("docs", "blk", None),
            P("blk", None),
            P("blk"),
            P("blk", None),
            P("blk", None),
            P("blk"),
            P("blk", None),
            P("blk"),
            P("blk"),
            P("blk"),
            P("blk", None),
            P("blk"),
            P("blk", None),
            P("blk"),
            P("blk"),
            P("blk"),
            P("blk", None),
            P("blk", None),
            P("blk", None),
        ),
        check_vma=False,
    )
```

```python
import functools
import math

import jax
import jax.numpy as jnp
from jax import lax
from jax.experimental import pallas as pl
from jax.experimental.pallas import tpu as pltpu
from jax.sharding import PartitionSpec as P

ORDER_LIMITS = (1, 2, 3, 4, 5, 6, 7, 8, 12, 16, 23, 32, 45, 64, 91)
BOX_LIMITS = (2, 4, 6, 8, 12, 16, 24, 32, 48, 64, 96, 128, 192, 256, 384)
EPSILON = 1e-05
LANES = 128
PAIR = 128
VMEM_LIMIT = 60 * 1024 * 1024
FIELD = 65536
LOG2E = 1.4426950408889634
UNIT = 2048.0

def forward_kernel(tile_ref, table_ref, near_ref, across_ref, down_ref, query_ref, key_ref, value_ref,
                   raised_ref, mixed_ref, inverse_ref, mixed_low_ref, score_ref, order_ref, value_sums_ref):
    keys, queries = across_ref.shape
    head_size = PAIR // 2
    rows = lax.broadcasted_iota(jnp.int32, (PAIR, queries), 0)
    query_pair = query_ref[...]
    zero = jnp.zeros_like(query_pair)
    both = jnp.concatenate(
        [jnp.where(rows < head_size, query_pair, zero), jnp.where(rows >= head_size, query_pair, zero)], axis=1
    )
    step = 16
    numbers = lax.GatherDimensionNumbers(
        offset_dims=(), collapsed_slice_dims=(1,), start_index_map=(1,),
        operand_batching_dims=(0,), start_indices_batching_dims=(0,),
    )

    def pick(places):
        table = jnp.broadcast_to(table_ref[0], places.shape)
        return lax.gather(table, places[..., None], numbers, (1, 1), mode=lax.GatherScatterMode.PROMISE_IN_BOUNDS)

    for at in range(0, near_ref.shape[0], step):
        order_ref[at : at + step, :] = pick(near_ref[at : at + step, :])
    value_sums_ref[0, :head_size, :] = value_ref[:head_size, :]
    value_sums_ref[1, :head_size, :] = value_ref[head_size:, :]
    value_sums_ref[:, head_size:, :] = jnp.ones((2, 16, keys), jnp.bfloat16)

    peaks = [jnp.full((8, LANES), -jnp.inf, jnp.float32) for _ in range(2 * queries // LANES)]
    for at in range(0, keys, step):
        raw = jnp.dot(key_ref[at : at + step, :], both, preferred_element_type=jnp.float32)
        for lane in range(0, queries, LANES):
            lanes = slice(lane, lane + LANES)
            start = pl.multiple_of(tile_ref[at // LANES, lane // LANES] + at % LANES, step)
            code = order_ref[pl.ds(start, step), :]
            code = code + pick(across_ref[at : at + step, lanes]) + pick(down_ref[at : at + step, lanes])
            for head, field in enumerate((lax.bitwise_and(code, FIELD - 1), lax.shift_right_logical(code, 16))):
                place = head * queries + lane
                score = raw[:, place : place + LANES] + field.astype(jnp.float32)
                score_ref[at : at + step, place : place + LANES] = score
                peaks[place // LANES] = jnp.maximum(peaks[place // LANES], jnp.max(score.reshape(step // 8, 8, LANES), axis=0))
    peak = jnp.max(jnp.concatenate(peaks, axis=1), axis=0, keepdims=True)
    for head in range(2):
        lanes = slice(head * queries, (head + 1) * queries)
        for at in range(0, keys, step):
            raised = jnp.exp2((score_ref[at : at + step, lanes] - peak[:, lanes]) * (LOG2E / UNIT)).astype(jnp.bfloat16)
            raised_ref[head, at : at + step, :] = raised
        sums = jnp.dot(value_sums_ref[head], raised_ref[head], preferred_element_type=jnp.float32)
        inverse = 1.0 / sums[head_size : head_size + 1, :]
        mixed = sums[:head_size, :] * inverse
        mixed_ref[head * head_size : (head + 1) * head_size, :] = mixed
        mixed_low_ref[head * head_size : (head + 1) * head_size, :] = mixed.astype(jnp.bfloat16)
        inverse_ref[head * head_size : (head + 1) * head_size, :] = jnp.broadcast_to(inverse, (head_size, queries))


def attention_forward(tiles, tables, near, across, down, query_t, keys, value_t):
    width, queries = query_t.shape
    length = keys.shape[0]
    pairs = width // PAIR
    whole = pl.BlockSpec((length, queries), lambda p: (0, 0))
    return pl.pallas_call(
        forward_kernel,
        grid=(pairs,),
        in_specs=[
            pl.BlockSpec(memory_space=pltpu.SMEM),
            pl.BlockSpec((1, 1, LANES), lambda p: (p, 0, 0)),
            pl.BlockSpec(near.shape, lambda p: (0, 0)),
            whole, whole,
            pl.BlockSpec((PAIR, queries), lambda p: (p, 0)),
            pl.BlockSpec((length, PAIR), lambda p: (0, p)),
            pl.BlockSpec((PAIR, length), lambda p: (p, 0)),
        ],
        out_specs=[
            pl.BlockSpec((2, length, queries), lambda p: (p, 0, 0)),
            pl.BlockSpec((PAIR, queries), lambda p: (p, 0)),
            pl.BlockSpec((PAIR, queries), lambda p: (p, 0)),
            pl.BlockSpec((PAIR, queries), lambda p: (p, 0)),
        ],
        out_shape=[
            jax.ShapeDtypeStruct((2 * pairs, length, queries), jnp.bfloat16),
            jax.ShapeDtypeStruct((width, queries), jnp.float32),
            jax.ShapeDtypeStruct((width, queries), jnp.float32),
            jax.ShapeDtypeStruct((width, queries), jnp.bfloat16),
        ],
        scratch_shapes=[
            pltpu.VMEM((length, 2 * queries), jnp.float32),
            pltpu.VMEM(near.shape, jnp.int32),
            pltpu.VMEM((2, PAIR // 2 + 16, length), jnp.bfloat16),
        ],
        compiler_params=pltpu.CompilerParams(vmem_limit_bytes=VMEM_LIMIT),
        cost_estimate=pl.CostEstimate(flops=4 * width * queries * length, bytes_accessed=16 << 20, transcendentals=0),
        name="attention_forward",
    )(tiles, tables, near, across, down, query_t, keys, value_t)


def backward_kernel(order_ref, across_ref, down_ref, raised_ref, query_ref, upstream_ref, inverse_ref, mixed_ref,
                    value_ref, key_ref, grad_query_ref, grad_key_ref, grad_value_ref, table_ref, bias_ref,
                    sum_ref, grad_ref, count_ref, scaled_ref, dot_ref, value_sum_ref, *, heads, scale, key_scale):
    slot = pl.program_id(0)
    keys, queries = order_ref.shape
    head_size = PAIR // 2
    group = 16
    per_super = 4
    supers = keys // (group * per_super)
    buckets = count_ref.shape[1] // group
    nt = (((1,), (1,)), ((), ()))

    @pl.when(slot == 0)
    def _():
        sum_ref[...] = jnp.zeros_like(sum_ref)
        count_ref[...] = jnp.zeros_like(count_ref)
        value_sum_ref[...] = jnp.zeros_like(value_sum_ref)
        for head in range(heads):
            feature = slice(head * head_size, (head + 1) * head_size)
            scaled = (upstream_ref[feature, :].astype(jnp.float32) * inverse_ref[feature, :]).astype(jnp.bfloat16)
            scaled_ref[feature, :] = scaled
            dot_ref[head : head + 1, :] = jnp.sum(scaled.astype(jnp.float32) * mixed_ref[feature, :], axis=0, keepdims=True)

    rows = lax.broadcasted_iota(jnp.int32, (PAIR, queries), 0)
    for pair in range(heads // 2):
        at = slice(pair * PAIR, (pair + 1) * PAIR)
        query_pair = query_ref[at, :]
        mixed_pair = scaled_ref[at, :]
        zero = jnp.zeros_like(query_pair)
        query_both = [jnp.where(rows < head_size, query_pair, zero), jnp.where(rows >= head_size, query_pair, zero)]
        mixed_both = [jnp.where(rows < head_size, mixed_pair, zero), jnp.where(rows >= head_size, mixed_pair, zero)]
        query_both = jnp.concatenate(query_both, axis=1)
        mixed_both = jnp.concatenate(mixed_both, axis=1)
        grad_probs = jnp.dot(value_ref[:, at], mixed_both, preferred_element_type=jnp.float32)
        raised = jnp.concatenate([raised_ref[2 * pair], raised_ref[2 * pair + 1]], axis=1)
        dots = jnp.concatenate([dot_ref[2 * pair : 2 * pair + 1, :], dot_ref[2 * pair + 1 : 2 * pair + 2, :]], axis=1)
        grad = (raised.astype(jnp.float32) * (grad_probs - dots)).astype(jnp.bfloat16)
        grad_values = lax.dot_general(raised, mixed_both, nt, preferred_element_type=jnp.float32).astype(jnp.bfloat16)
        grad_value_ref[:, at] = grad_values
        value_sum_ref[:, at] += jnp.sum(grad_values.astype(jnp.float32).reshape(keys // 8, 8, PAIR), axis=0)
        grad_keys = lax.dot_general(grad, query_both, nt, preferred_element_type=jnp.float32)
        grad_key_ref[:, at] = (grad_keys * key_scale).astype(jnp.bfloat16)
        for one in range(2):
            head = 2 * pair + one
            mine = grad[:, one * queries : (one + 1) * queries]
            feature = slice(head * head_size, (head + 1) * head_size)
            sum_ref[feature, :] += jnp.dot(key_ref[feature, :], mine, preferred_element_type=jnp.float32)
            for g in range(keys // group):
                lanes = slice((g % per_super) * queries, (g % per_super + 1) * queries)
                grad_ref[g // per_super, head * group : (head + 1) * group, lanes] = mine[g * group : (g + 1) * group, :]

    def tally(sup, _):
        grads = grad_ref[sup]
        for number, ref in enumerate((order_ref, across_ref, down_ref)):
            parts = []
            for sub in range(per_super):
                at = pl.multiple_of(sup * (group * per_super) + sub * group, group)
                ids = ref[pl.ds(at, group), :]
                hot = [jnp.where(ids == b + number * buckets, 1.0, 0.0).astype(jnp.bfloat16) for b in range(buckets)]
                parts.append(jnp.concatenate(hot, axis=0))
            hot = jnp.concatenate(parts, axis=1)
            count_ref[number] += lax.dot_general(hot, grads, nt, preferred_element_type=jnp.float32)
        return 0

    lax.fori_loop(0, supers, tally, 0)

    @pl.when(slot == pl.num_programs(0) - 1)
    def _():
        grad_queries = (sum_ref[...] * scale).astype(jnp.bfloat16)
        grad_query_ref[...] = grad_queries
        ones = jnp.ones((8, queries), jnp.bfloat16)
        bias_ref[:8, :] = value_sum_ref[...]
        bias_ref[8:, :] = lax.dot_general(ones, grad_queries, nt, preferred_element_type=jnp.float32)
        place = lax.broadcasted_iota(jnp.int32, (buckets * group, heads * group), 0) % group
        other = lax.broadcasted_iota(jnp.int32, (buckets * group, heads * group), 1) % group
        owner = lax.broadcasted_iota(jnp.int32, (heads * group, LANES), 0) // group
        column = lax.broadcasted_iota(jnp.int32, (heads * group, LANES), 1)
        gather = jnp.where(owner == column, 1.0, 0.0)
        for number in range(3):
            kept = jnp.where(place == other, count_ref[number], 0.0)
            kept = jnp.sum(kept.reshape(buckets, group, heads * group), axis=1)
            table_ref[number] = jnp.dot(kept, gather, preferred_element_type=jnp.float32, precision=lax.Precision.HIGHEST)


def attention_backward(order, across, down, raised, query_t, upstream_t, inverse_t, mixed_t, values, key_t, scale, key_scale, slots):
    width, queries = query_t.shape
    heads = raised.shape[0]
    length = values.shape[0]
    keys = length // slots
    buckets = 32
    group = 16
    ids = pl.BlockSpec((keys, queries), lambda s: (s, 0))
    full = pl.BlockSpec((width, queries), lambda s: (0, 0))
    rows = pl.BlockSpec((keys, width), lambda s: (s, 0))
    return pl.pallas_call(
        functools.partial(backward_kernel, heads=heads, scale=scale, key_scale=key_scale),
        grid=(slots,),
        in_specs=[
            ids, ids, ids,
            pl.BlockSpec((heads, keys, queries), lambda s: (0, s, 0)),
            full, full, full, full,
            rows,
            pl.BlockSpec((width, keys), lambda s: (0, s)),
        ],
        out_specs=[
            full, rows, rows,
            pl.BlockSpec((3, buckets, LANES), lambda s: (0, 0, 0)),
            pl.BlockSpec((16, width), lambda s: (0, 0)),
        ],
        out_shape=[
            jax.ShapeDtypeStruct((width, queries), jnp.bfloat16),
            jax.ShapeDtypeStruct((length, width), jnp.bfloat16),
            jax.ShapeDtypeStruct((length, width), jnp.bfloat16),
            jax.ShapeDtypeStruct((3, buckets, LANES), jnp.float32),
            jax.ShapeDtypeStruct((16, width), jnp.float32),
        ],
        scratch_shapes=[
            pltpu.VMEM((width, queries), jnp.float32),
            pltpu.VMEM((keys // (group * 4), heads * group, 4 * queries), jnp.bfloat16),
            pltpu.VMEM((3, buckets * group, heads * group), jnp.float32),
            pltpu.VMEM((width, queries), jnp.bfloat16),
            pltpu.VMEM((16, queries), jnp.float32),
            pltpu.VMEM((8, width), jnp.float32),
        ],
        compiler_params=pltpu.CompilerParams(vmem_limit_bytes=VMEM_LIMIT),
        cost_estimate=pl.CostEstimate(flops=0, bytes_accessed=0, transcendentals=0),
        name="attention_backward",
    )(order, across, down, raised, query_t, upstream_t, inverse_t, mixed_t, values, key_t)


ERF_P = 0.3275911
ERF_A = (0.254829592, -0.284496736, 1.421413741, -1.453152027, 1.061405429)
TN = (((0,), (0,)), ((), ()))
NT = (((1,), (1,)), ((), ()))


def dot(left, right, numbers=(((1,), (0,)), ((), ()))):
    return lax.dot_general(left, right, numbers, preferred_element_type=jnp.float32)


def gelu_and_slope(values):
    size = jnp.abs(values) * (0.5**0.5)
    near = 1.0 / (1.0 + ERF_P * size)
    series = ERF_A[4]
    for term in ERF_A[3::-1]:
        series = series * near + term
    bell = jnp.exp(-(size * size))
    tail = 0.5 * (series * near) * bell
    share = jnp.where(values >= 0, 1.0 - tail, tail)
    return (values * share, share + values * bell * (0.5 / math.pi) ** 0.5)


def normalized(values):
    centred = values - jnp.mean(values, axis=1, keepdims=True)
    scale = lax.rsqrt(jnp.mean(centred * centred, axis=1, keepdims=True) + EPSILON)
    return (centred * scale, scale)


def norm_back(normal, scale, grad, gain):
    scaled = grad * gain
    inner = jnp.mean(scaled * normal, axis=1, keepdims=True)
    return scale * (scaled - jnp.mean(scaled, axis=1, keepdims=True) - normal * inner)


def column_sum(values):
    return jnp.sum(values, axis=0, keepdims=True)


def upper_kernel(me_ref, mixed_ref, tokens_ref, cotangent_ref, w_out_ref, w_up_ref, w_down_ref, b_out_ref, gain_first_ref,
                 shift_first_ref, b_up_ref, b_down_ref, gain_second_ref, shift_second_ref,
                 output_ref, grad_ref, normal_ref, scale_ref, low_ref, slope_ref, sent_ref, kept_ref, sums_ref,
                 active_ref):
    me = me_ref[0]
    width = tokens_ref.shape[1]
    hidden = w_up_ref.shape[1]
    step = width
    branch = dot(mixed_ref[...], w_out_ref[...], TN) + b_out_ref[...]
    normal, scale = normalized(tokens_ref[...].astype(jnp.float32) + branch)
    normal_ref[...] = normal
    scale_ref[...] = jnp.broadcast_to(scale, scale_ref.shape)
    first_norm = normal * gain_first_ref[...] + shift_first_ref[...]
    first_low = first_norm.astype(jnp.bfloat16)
    low_ref[...] = first_low.T
    second = first_norm + b_down_ref[...]
    for at in range(0, hidden, step):
        columns = slice(at, at + step)
        active, slope = gelu_and_slope(dot(first_low, w_up_ref[:, columns]) + b_up_ref[:, columns])
        slope_ref[:, columns] = slope.astype(jnp.bfloat16)
        active = active.astype(jnp.bfloat16)
        active_ref[:, columns] = active
        second = second + dot(active, w_down_ref[columns, :])
    normal, scale = normalized(second)
    output_ref[...] = (normal * gain_second_ref[...] + shift_second_ref[...]).astype(jnp.bfloat16)
    upstream = cotangent_ref[...].astype(jnp.float32)
    grad = norm_back(normal, scale, upstream, gain_second_ref[...])
    grad_ref[...] = grad
    grad_second = grad.astype(jnp.bfloat16)
    sums_ref[...] = jnp.zeros_like(sums_ref)
    sums_ref[0:1, :] = column_sum(upstream * normal)
    sums_ref[1:2, :] = column_sum(upstream)
    sums_ref[2:3, :] = column_sum(grad_second.astype(jnp.float32))
    rows = hidden // 4
    for distance, out in ((1, sent_ref.at[0]), (3, sent_ref.at[1]), (0, kept_ref.at[0]), (2, kept_ref.at[1])):
        place = pl.multiple_of(lax.bitwise_xor(me, distance) * rows, LANES)
        out[...] = dot(active_ref[:, pl.ds(place, rows)], grad_second, TN).astype(jnp.bfloat16)


def upper(me, mixed_low, tokens, cotangent, w_out, w_up, w_down, *vectors):
    length, width = tokens.shape
    hidden = w_up.shape[1]
    bf16, f32 = jnp.bfloat16, jnp.float32
    shapes = [
        ((length, width), bf16),
        ((length, width), f32),
        ((length, width), f32),
        ((length, LANES), f32),
        ((width, length), bf16),
        ((length, hidden), bf16),
        ((2, hidden // 4, width), bf16),
        ((2, hidden // 4, width), bf16),
        ((8, width), f32),
    ]
    return pl.pallas_call(
        upper_kernel,
        in_specs=[pl.BlockSpec(memory_space=pltpu.SMEM)] + [pl.BlockSpec(memory_space=pltpu.VMEM)] * (6 + len(vectors)),
        out_shape=[jax.ShapeDtypeStruct(shape, dtype) for shape, dtype in shapes],
        scratch_shapes=[pltpu.VMEM((length, hidden), bf16)],
        compiler_params=pltpu.CompilerParams(vmem_limit_bytes=VMEM_LIMIT),
        cost_estimate=pl.CostEstimate(flops=8 * length * width * hidden, bytes_accessed=24 << 20, transcendentals=0),
        name="upper",
    )(me, mixed_low, tokens, cotangent, w_out, w_up, w_down, *[v[None, :] for v in vectors])


def lower_kernel(me_ref, grad_ref, normal_ref, scale_ref, low_ref, slope_ref, mixed_ref, w_out_ref, w_up_ref, w_down_ref, gain_ref,
                 sent_up_ref, kept_up_ref, sent_out_ref, kept_out_ref, grad_first_ref, upstream_ref, sums_ref, up_sums_ref,
                 hidden_ref):
    me = me_ref[0]
    width = grad_ref.shape[1]
    hidden = w_up_ref.shape[1]
    step = width
    rows = width // 4
    grad_first = grad_ref[...]
    grad_second = grad_first.astype(jnp.bfloat16)
    up_sums_ref[...] = jnp.zeros_like(up_sums_ref)
    for at in range(0, hidden, step):
        columns = slice(at, at + step)
        grad_hidden = dot(grad_second, w_down_ref[columns, :], NT) * slope_ref[:, columns].astype(jnp.float32)
        grad_hidden = grad_hidden.astype(jnp.bfloat16)
        hidden_ref[:, columns] = grad_hidden
        up_sums_ref[at // step : at // step + 1, :] = column_sum(grad_hidden.astype(jnp.float32))
        grad_first = grad_first + dot(grad_hidden, w_up_ref[:, columns], NT)

    def places(sent, kept):
        for distance, out in ((1, sent.at[0]), (3, sent.at[1]), (0, kept.at[0]), (2, kept.at[1])):
            place = lax.bitwise_xor(me, distance) * rows
            yield (pl.ds(pl.multiple_of(place, rows), rows), out)

    for place, out in places(sent_up_ref, kept_up_ref):
        out[...] = dot(low_ref[place, :], hidden_ref[...]).astype(jnp.bfloat16)
    normal = normal_ref[...]
    grad = norm_back(normal, scale_ref[:, :1], grad_first, gain_ref[...])
    grad_first_ref[...] = grad
    grad_branch = grad.astype(jnp.bfloat16)
    sums_ref[...] = jnp.zeros_like(sums_ref)
    sums_ref[0:1, :] = column_sum(grad_first * normal)
    sums_ref[1:2, :] = column_sum(grad_first)
    sums_ref[2:3, :] = column_sum(grad_branch.astype(jnp.float32))
    upstream_ref[...] = dot(w_out_ref[...], grad_branch, NT).astype(jnp.bfloat16)
    for place, out in places(sent_out_ref, kept_out_ref):
        out[...] = dot(mixed_ref[place, :], grad_branch).astype(jnp.bfloat16)


def lower(me, grad, normal, scale, low_t, slope, mixed_low, w_out, w_up, w_down, gain):
    length, width = grad.shape
    hidden = w_up.shape[1]
    bf16, f32 = jnp.bfloat16, jnp.float32
    shapes = [
        ((2, width // 4, hidden), bf16),
        ((2, width // 4, hidden), bf16),
        ((2, width // 4, width), bf16),
        ((2, width // 4, width), bf16),
        ((length, width), f32),
        ((width, length), bf16),
        ((8, width), f32),
        ((8, width), f32),
    ]
    return pl.pallas_call(
        lower_kernel,
        in_specs=[pl.BlockSpec(memory_space=pltpu.SMEM)] + [pl.BlockSpec(memory_space=pltpu.VMEM)] * 10,
        out_shape=[jax.ShapeDtypeStruct(shape, dtype) for shape, dtype in shapes],
        scratch_shapes=[pltpu.VMEM((length, hidden), bf16)],
        compiler_params=pltpu.CompilerParams(vmem_limit_bytes=VMEM_LIMIT),
        cost_estimate=pl.CostEstimate(flops=8 * length * width * hidden, bytes_accessed=24 << 20, transcendentals=0),
        name="lower",
    )(me, grad, normal, scale, low_t, slope, mixed_low, w_out, w_up, w_down, gain[None, :])


def last_kernel(me_ref, rows_ref, own_ref, query_ref, key_ref, value_ref, upper_sums_ref, lower_sums_ref, up_sums_ref, bias_ref, table_ref,
                sent_ref, kept_ref, small_ref):
    me = me_ref[0]
    width = rows_ref.shape[1]
    rows = width // 4
    ups = rows_ref.shape[0]
    sums = jnp.concatenate([upper_sums_ref[:3, :], lower_sums_ref[:3, :], column_sum(bias_ref[:8, :]), bias_ref[8:9, :]], axis=0)
    for number, part in enumerate((sums, up_sums_ref[...])):
        for at in range(0, width, LANES):
            place = (number * width + at) // LANES * 8
            small_ref[place : place + 8, :] = part[:, at : at + LANES].astype(jnp.bfloat16).astype(jnp.float32)
    used = 2 * width // LANES * 8
    for number in range(3):
        size = table_ref.shape[1]
        small_ref[used + number * size : used + (number + 1) * size, :] = table_ref[number]
    small = small_ref[...].astype(jnp.bfloat16)
    for side in range(2):
        for out in (sent_ref, kept_ref):
            out[side, :, 3 * width :] = small
    for number, (left, right, numbers) in enumerate(
        ((own_ref, query_ref, (((0,), (1,)), ((), ()))), (rows_ref, key_ref, TN), (rows_ref, value_ref, TN))
    ):
        columns = slice(number * width, (number + 1) * width)
        full = dot(left[...], right[...], numbers).astype(jnp.bfloat16)
        for quarter in range(4):
            distance = lax.bitwise_xor(me, quarter)
            part = full[quarter * rows : (quarter + 1) * rows, :]

            @pl.when(distance % 2 == 1)
            def _():
                sent_ref[distance // 2, :, columns] = part

            @pl.when(distance % 2 == 0)
            def _():
                kept_ref[distance // 2, :, columns] = part


def last_grads(me, rows_all, rows_in, grad_query_t, grad_keys, grad_values, *small):
    width = rows_in.shape[1]
    rows = width // 4
    out = jax.ShapeDtypeStruct((2, rows, 3 * width + LANES), jnp.bfloat16)
    return pl.pallas_call(
        last_kernel,
        in_specs=[pl.BlockSpec(memory_space=pltpu.SMEM)] + [pl.BlockSpec(memory_space=pltpu.VMEM)] * (5 + len(small)),
        out_shape=[out, out],
        scratch_shapes=[pltpu.VMEM((rows, LANES), jnp.float32)],
        compiler_params=pltpu.CompilerParams(vmem_limit_bytes=VMEM_LIMIT),
        cost_estimate=pl.CostEstimate(flops=0, bytes_accessed=0, transcendentals=0),
        name="last_grads",
    )(me, rows_all, rows_in, grad_query_t, grad_keys, grad_values, *small)


MARK_FLOPS = 20_000_000_000


def bucketize(offsets, limits):
    magnitude = jnp.abs(offsets)
    bucket_id = jnp.zeros(offsets.shape, jnp.int32)
    for threshold in limits:
        bucket_id = bucket_id + (magnitude >= threshold).astype(jnp.int32)
    return bucket_id + 16 * (offsets > 0).astype(jnp.int32)


def einsum(spec, left, right):
    return jnp.einsum(spec, left, right, preferred_element_type=jnp.float32)


def exchange(array, axis_name, distance):
    pairs = [(i, i ^ distance) for i in range(lax.axis_size(axis_name))]
    return lax.ppermute(array, axis_name, pairs)


def in_blocks(sent, kept):
    got = exchange(sent, "blk", 1)
    shape = (2, 2, 2, -1, sent.shape[-1])
    return (kept.reshape(shape), got.reshape(shape))


def mark_kernel(array_ref, out_ref):
    out_ref[...] = jnp.zeros_like(out_ref)


def mark_of(array):
    return pl.pallas_call(
        mark_kernel,
        in_specs=[pl.BlockSpec(memory_space=pl.ANY)],
        out_specs=pl.BlockSpec(memory_space=pltpu.VMEM),
        out_shape=jax.ShapeDtypeStruct((8, LANES), jnp.float32),
        compiler_params=pltpu.CompilerParams(has_side_effects=True),
        cost_estimate=pl.CostEstimate(flops=MARK_FLOPS, bytes_accessed=4096, transcendentals=0),
        name="mark",
    )(array)


BITS = {"y": 0, "x": 1, "a": 2}


def add_low(left, right):
    return (left.astype(jnp.float32) + right.astype(jnp.float32)).astype(jnp.bfloat16)


def reduce_rows(kept, got, widths, order, back, sides):
    distances = {"y": ("blk", 2), "x": ("docs", 1), "a": ("docs", 2)}

    def half(array, letter, sent):
        side = sides[letter]
        if sent:
            side = 1 - side
        return lax.dynamic_slice_in_dim(array, side, 1, BITS[letter])

    for letter in order:
        pairs = list(zip(kept, got))
        sent = [add_low(half(one, letter, True), half(two, letter, True)) for one, two in pairs]
        sent = sent[0] if len(sent) == 1 else jnp.concatenate(sent, axis=4)
        result = yield (sent, *distances[letter])
        kept = [add_low(half(one, letter, False), half(two, letter, False)) for one, two in pairs]
        kept = [kept[0] if len(kept) == 1 else jnp.concatenate(kept, axis=4)]
        got = [result]
    data = add_low(kept[0], got[0])
    distance = 4
    while distance < lax.axis_size("docs"):
        got = yield (data, "docs", distance)
        data = add_low(data, got)
        distance = distance * 2
    for letter in back:
        got = yield (data, *distances[letter])
        halves = [jnp.where(sides[letter] == 0, data, got), jnp.where(sides[letter] == 0, got, data)]
        data = jnp.concatenate(halves, axis=BITS[letter])
    data = data.reshape(-1, data.shape[4])
    outs = []
    column = 0
    for width in widths:
        outs.append(data[:, column : column + width].astype(jnp.float32))
        column = column + width
    return outs


class Line:
    def __init__(self):
        self.last = None
        self.waiting = {}
        self.steps = {}
        self.results = {}

    def after(self, *arrays):
        if self.last is None:
            return arrays
        return lax.optimization_barrier((*arrays, self.last))[:-1]

    def mark(self, array):
        self.last = array

    def send(self, name):
        array, axis_name, distance = self.waiting[name]
        self.waiting[name] = exchange(array, axis_name, distance)
        self.mark(mark_of(array))

    def begin(self, name, steps):
        self.steps[name] = steps
        array, axis_name, distance = next(steps)
        self.waiting[name] = exchange(array, axis_name, distance)
        self.mark(array)

    def go(self, names):
        for name in names:
            if name in self.results:
                continue
            (got,) = self.after(self.waiting[name])
            try:
                self.waiting[name] = self.steps[name].send(got)
            except StopIteration as stop:
                self.results[name] = stop.value
                continue
            self.send(name)

    def finish(self, names):
        while any(name not in self.results for name in names):
            self.go(names)


def body(
    tokens,
    box_corners,
    cotangent,
    w_query,
    b_query,
    w_key,
    w_value,
    b_value,
    w_out,
    b_out,
    gain_first,
    shift_first,
    w_up,
    b_up,
    w_down,
    b_down,
    gain_second,
    shift_second,
    table_order,
    table_horizontal,
    table_vertical,
):
    docs_here, doc_length, model_width = tokens.shape
    bucket_total, head_count = table_order.shape
    head_size = model_width // head_count
    score_scale = head_size ** (-0.5)
    blk_count = lax.axis_size("blk")
    me = lax.axis_index("blk")
    rows_in = tokens.reshape(doc_length, model_width)

    centres = jnp.stack([box_corners[0, 0] + box_corners[2, 0], box_corners[1, 0] + box_corners[3, 0]])
    centres = centres.astype(jnp.float32)
    centre_slots = [centres] + [exchange(centres, "blk", s) for s in range(1, blk_count)]
    core_rows = exchange(rows_in, "blk", 1)
    far_rows = exchange(rows_in, "blk", 2)
    rows_all = jnp.concatenate([rows_in, core_rows, far_rows, exchange(far_rows, "blk", 1)], axis=0)
    centres_all = jnp.concatenate(centre_slots, axis=1).astype(jnp.int32)
    centres_own = centres.astype(jnp.int32)

    inside = jnp.arange(doc_length, dtype=jnp.int32)
    key_place = jnp.concatenate([(me ^ s) * doc_length + inside for s in range(blk_count)])
    query_place = me * doc_length + inside
    order = bucketize(key_place[:, None] - query_place[None, :], ORDER_LIMITS)
    across = bucketize(centres_all[0][:, None] - centres_own[0][None, :], BOX_LIMITS) + bucket_total
    down = bucketize(centres_all[1][:, None] - centres_own[1][None, :], BOX_LIMITS) + 2 * bucket_total
    tile = jnp.arange(LANES, dtype=jnp.int32)
    near = [bucketize(t * LANES + tile[:, None] - tile[None, :], ORDER_LIMITS) for t in range(-2, 3)]
    near = jnp.concatenate(near, axis=0)
    tiles = (key_place[::LANES, None] - query_place[None, ::LANES]) // LANES
    tiles = (jnp.clip(tiles, -2, 2) + 2) * LANES
    tables = jnp.concatenate([table_order, table_horizontal, table_vertical], axis=0).T
    tables = jnp.round((tables + 5.0) * UNIT).astype(jnp.int32)
    tables = tables[0::2] + FIELD * tables[1::2]
    tables = jnp.pad(tables, ((0, 0), (0, LANES - 3 * bucket_total)))[:, None, :]

    query_t = (einsum("df,td->ft", w_query, rows_in) + b_query[:, None]).astype(jnp.bfloat16)
    query_t = query_t * jnp.bfloat16(score_scale * UNIT)
    keys = einsum("td,df->tf", rows_all, w_key).astype(jnp.bfloat16)
    key_t = einsum("df,td->ft", w_key, rows_all).astype(jnp.bfloat16)
    values = (einsum("td,df->tf", rows_all, w_value) + b_value).astype(jnp.bfloat16)
    value_t = (einsum("df,td->ft", w_value, rows_all) + b_value[:, None]).astype(jnp.bfloat16)

    raised, mixed_t, inverse_t, mixed_low = attention_forward(
        tiles, tables, near, across, down, query_t, keys, value_t
    )

    place = me.reshape(1).astype(jnp.int32)
    cotangents = cotangent.reshape(doc_length, model_width)
    output, grad_pre2, normal, scale, low_t, slope, sent_down, kept_down, upper_sums = upper(
        place, mixed_low, rows_in, cotangents, w_out, w_up, w_down,
        b_out, gain_first, shift_first, b_up, b_down, gain_second, shift_second
    )
    parts_down = in_blocks(sent_down, kept_down)
    sent_up, kept_up, sent_out, kept_out, grad_pre1, upstream_t, lower_sums, up_sums = lower(
        place, grad_pre2, normal, scale, low_t, slope, mixed_low, w_out, w_up, w_down, gain_first
    )
    parts_up = in_blocks(sent_up, kept_up)
    parts_out = in_blocks(sent_out, kept_out)
    output = output.reshape(tokens.shape)

    here = lax.axis_index("docs")
    sides = {"y": 0, "x": here % 2, "a": (here // 2) % 2}
    line = Line()
    line.mark(upstream_t)
    def begin(name, parts, order, back):
        kept = [part[0] for part in parts]
        got = list(line.after(*[part[1] for part in parts]))
        widths = [kept[0].shape[4]]
        if name == "last":
            widths = [model_width] * 3 + [LANES]
        line.begin(name, reduce_rows(kept, got, widths, order, back, sides))

    begin("out", [parts_out], "yxa", "xa")
    begin("up", [parts_up], "xya", "ax")
    begin("down", [parts_down], "axy", "xa")
    (upstream_t,) = line.after(upstream_t)
    grad_query_t, grad_keys, grad_values, table_sums, bias_sums = attention_backward(
        order, across, down, raised, query_t, upstream_t, inverse_t, mixed_t, values, key_t,
        score_scale, 1.0 / UNIT, blk_count
    )
    line.mark(grad_values)
    line.go(["up"])
    grad_query_t, grad_keys, grad_values = line.after(grad_query_t, grad_keys, grad_values)
    sent_last, kept_last = last_grads(
        place, rows_all, rows_in, grad_query_t, grad_keys, grad_values, upper_sums, lower_sums, up_sums, bias_sums, table_sums
    )
    parts_last = in_blocks(sent_last, kept_last)
    line.mark(sent_last)
    line.go(["down", "out"])
    begin("last", [parts_last], "yax", "ax")
    line.go(["up"])

    grad_query_t, grad_keys, grad_values = line.after(grad_query_t, grad_keys, grad_values)
    shared = einsum("tf,df->td", grad_keys, w_key) + einsum("tf,df->td", grad_values, w_value)
    shared = shared.reshape(blk_count, doc_length, model_width)
    shared_sent = jnp.concatenate([shared[1], shared[3]]).astype(jnp.bfloat16)
    line.mark(shared_sent)
    near = exchange(shared_sent, "blk", 1)
    line.go(["up", "out", "down"])
    (near,) = line.after(near)
    near = near.astype(jnp.float32)
    far_sent = (shared[2] + near[doc_length:]).astype(jnp.bfloat16)
    line.mark(far_sent)
    far = exchange(far_sent, "blk", 2)
    line.go(["last", "out", "down", "up", "last", "out", "last", "out", "down", "up", "out", "last"])
    grad_query_t, far = line.after(grad_query_t, far)
    grad_inputs = grad_pre1 + einsum("ft,df->td", grad_query_t, w_query) + shared[0] + near[:doc_length]
    grad_tokens = (grad_inputs + far.astype(jnp.float32)).astype(jnp.bfloat16).reshape(tokens.shape)
    line.mark(grad_tokens)
    line.go(["down", "last", "up", "down", "last"])
    line.finish(["down", "last", "up", "out"])

    (grad_w_down,) = line.results["down"]
    (grad_w_up,) = line.results["up"]
    (grad_w_out,) = line.results["out"]
    grad_w_query, grad_w_key, grad_w_value, flat = line.results["last"]
    tiles_each = model_width // LANES
    rows = model_width // blk_count

    def vectors(first):
        block = flat[first : first + 8 * tiles_each].reshape(tiles_each, 8, LANES)
        return jnp.transpose(block, (1, 0, 2)).reshape(8, model_width)

    each = lax.dynamic_slice_in_dim(vectors(0), me * rows, rows, 1)
    grad_b_up = lax.dynamic_slice_in_dim(vectors(8 * tiles_each), me, 1, 0)[0]
    table_rows = bucket_total // blk_count
    table_out = []
    for number in range(3):
        first = 16 * tiles_each + number * bucket_total + me * table_rows
        table_out.append(lax.dynamic_slice_in_dim(flat, first, table_rows, 0)[:, :head_count])
    small_out = [each[7], each[6], each[5], each[3], each[4], grad_b_up, each[2], each[0], each[1], *table_out]
    return (
        output,
        grad_tokens,
        grad_w_query,
        small_out[0],
        grad_w_key,
        grad_w_value,
        small_out[1],
        grad_w_out,
        small_out[2],
        small_out[3],
        small_out[4],
        grad_w_up,
        small_out[5],
        grad_w_down,
        small_out[6],
        small_out[7],
        small_out[8],
        small_out[9],
        small_out[10],
        small_out[11],
    )


def solution(mesh):
    return jax.shard_map(
        body,
        mesh=mesh,
        in_specs=(
            P("docs", "blk", None),
            P(None, "docs", "blk"),
            P("docs", "blk", None),
            P(),
            P(),
            P(),
            P(),
            P(),
            P(),
            P(),
            P(),
            P(),
            P(),
            P(),
            P(),
            P(),
            P(),
            P(),
            P(),
            P(),
            P(),
        ),
        out_specs=(
            P("docs", "blk", None),
            P("docs", "blk", None),
            P("blk", None),
            P("blk"),
            P("blk", None),
            P("blk", None),
            P("blk"),
            P("blk", None),
            P("blk"),
            P("blk"),
            P("blk"),
            P("blk", None),
            P("blk"),
            P("blk", None),
            P("blk"),
            P("blk"),
            P("blk"),
            P("blk", None),
            P("blk", None),
            P("blk", None),
        ),
        check_vma=False,
    )
```

```python
import functools
import math

import jax
import jax.numpy as jnp
from jax import lax
from jax.experimental import pallas as pl
from jax.experimental.pallas import tpu as pltpu
from jax.sharding import PartitionSpec as P

ORDER_LIMITS = (1, 2, 3, 4, 5, 6, 7, 8, 12, 16, 23, 32, 45, 64, 91)
BOX_LIMITS = (2, 4, 6, 8, 12, 16, 24, 32, 48, 64, 96, 128, 192, 256, 384)
EPSILON = 1e-05
LANES = 128
PAIR = 128
VMEM_LIMIT = 60 * 1024 * 1024
FIELD = 65536
LOG2E = 1.4426950408889634
UNIT = 2048.0

def forward_kernel(tile_ref, table_ref, near_ref, across_ref, down_ref, query_ref, key_ref, value_ref,
                   raised_ref, mixed_ref, inverse_ref, mixed_low_ref, score_ref, order_ref, value_sums_ref):
    keys, queries = across_ref.shape
    head_size = PAIR // 2
    rows = lax.broadcasted_iota(jnp.int32, (PAIR, queries), 0)
    query_pair = query_ref[...]
    zero = jnp.zeros_like(query_pair)
    both = jnp.concatenate(
        [jnp.where(rows < head_size, query_pair, zero), jnp.where(rows >= head_size, query_pair, zero)], axis=1
    )
    step = 16
    numbers = lax.GatherDimensionNumbers(
        offset_dims=(), collapsed_slice_dims=(1,), start_index_map=(1,),
        operand_batching_dims=(0,), start_indices_batching_dims=(0,),
    )

    def pick(places):
        table = jnp.broadcast_to(table_ref[0], places.shape)
        return lax.gather(table, places[..., None], numbers, (1, 1), mode=lax.GatherScatterMode.PROMISE_IN_BOUNDS)

    for at in range(0, near_ref.shape[0], step):
        order_ref[at : at + step, :] = pick(near_ref[at : at + step, :])
    value_sums_ref[0, :head_size, :] = value_ref[:head_size, :]
    value_sums_ref[1, :head_size, :] = value_ref[head_size:, :]
    value_sums_ref[:, head_size:, :] = jnp.ones((2, 16, keys), jnp.bfloat16)

    peaks = [jnp.full((8, LANES), -jnp.inf, jnp.float32) for _ in range(2 * queries // LANES)]
    for at in range(0, keys, step):
        raw = jnp.dot(key_ref[at : at + step, :], both, preferred_element_type=jnp.float32)
        for lane in range(0, queries, LANES):
            lanes = slice(lane, lane + LANES)
            start = pl.multiple_of(tile_ref[at // LANES, lane // LANES] + at % LANES, step)
            code = order_ref[pl.ds(start, step), :]
            code = code + pick(across_ref[at : at + step, lanes]) + pick(down_ref[at : at + step, lanes])
            for head, field in enumerate((lax.bitwise_and(code, FIELD - 1), lax.shift_right_logical(code, 16))):
                place = head * queries + lane
                score = raw[:, place : place + LANES] + field.astype(jnp.float32)
                score_ref[at : at + step, place : place + LANES] = score
                peaks[place // LANES] = jnp.maximum(peaks[place // LANES], jnp.max(score.reshape(step // 8, 8, LANES), axis=0))
    peak = jnp.max(jnp.concatenate(peaks, axis=1), axis=0, keepdims=True)
    for head in range(2):
        lanes = slice(head * queries, (head + 1) * queries)
        for at in range(0, keys, step):
            raised = jnp.exp2((score_ref[at : at + step, lanes] - peak[:, lanes]) * (LOG2E / UNIT)).astype(jnp.bfloat16)
            raised_ref[head, at : at + step, :] = raised
        sums = jnp.dot(value_sums_ref[head], raised_ref[head], preferred_element_type=jnp.float32)
        inverse = 1.0 / sums[head_size : head_size + 1, :]
        mixed = sums[:head_size, :] * inverse
        mixed_ref[head * head_size : (head + 1) * head_size, :] = mixed
        mixed_low_ref[head * head_size : (head + 1) * head_size, :] = mixed.astype(jnp.bfloat16)
        inverse_ref[head * head_size : (head + 1) * head_size, :] = jnp.broadcast_to(inverse, (head_size, queries))


def attention_forward(tiles, tables, near, across, down, query_t, keys, value_t):
    width, queries = query_t.shape
    length = keys.shape[0]
    pairs = width // PAIR
    whole = pl.BlockSpec((length, queries), lambda p: (0, 0))
    return pl.pallas_call(
        forward_kernel,
        grid=(pairs,),
        in_specs=[
            pl.BlockSpec(memory_space=pltpu.SMEM),
            pl.BlockSpec((1, 1, LANES), lambda p: (p, 0, 0)),
            pl.BlockSpec(near.shape, lambda p: (0, 0)),
            whole, whole,
            pl.BlockSpec((PAIR, queries), lambda p: (p, 0)),
            pl.BlockSpec((length, PAIR), lambda p: (0, p)),
            pl.BlockSpec((PAIR, length), lambda p: (p, 0)),
        ],
        out_specs=[
            pl.BlockSpec((2, length, queries), lambda p: (p, 0, 0)),
            pl.BlockSpec((PAIR, queries), lambda p: (p, 0)),
            pl.BlockSpec((PAIR, queries), lambda p: (p, 0)),
            pl.BlockSpec((PAIR, queries), lambda p: (p, 0)),
        ],
        out_shape=[
            jax.ShapeDtypeStruct((2 * pairs, length, queries), jnp.bfloat16),
            jax.ShapeDtypeStruct((width, queries), jnp.float32),
            jax.ShapeDtypeStruct((width, queries), jnp.float32),
            jax.ShapeDtypeStruct((width, queries), jnp.bfloat16),
        ],
        scratch_shapes=[
            pltpu.VMEM((length, 2 * queries), jnp.float32),
            pltpu.VMEM(near.shape, jnp.int32),
            pltpu.VMEM((2, PAIR // 2 + 16, length), jnp.bfloat16),
        ],
        compiler_params=pltpu.CompilerParams(vmem_limit_bytes=VMEM_LIMIT),
        cost_estimate=pl.CostEstimate(flops=4 * width * queries * length, bytes_accessed=16 << 20, transcendentals=0),
        name="attention_forward",
    )(tiles, tables, near, across, down, query_t, keys, value_t)


ERF_P = 0.3275911
ERF_A = (0.254829592, -0.284496736, 1.421413741, -1.453152027, 1.061405429)
TN = (((0,), (0,)), ((), ()))
NT = (((1,), (1,)), ((), ()))


def dot(left, right, numbers=(((1,), (0,)), ((), ()))):
    return lax.dot_general(left, right, numbers, preferred_element_type=jnp.float32)


def gelu_and_slope(values):
    size = jnp.abs(values) * (0.5**0.5)
    near = 1.0 / (1.0 + ERF_P * size)
    series = ERF_A[4]
    for term in ERF_A[3::-1]:
        series = series * near + term
    bell = jnp.exp(-(size * size))
    tail = 0.5 * (series * near) * bell
    share = jnp.where(values >= 0, 1.0 - tail, tail)
    return (values * share, share + values * bell * (0.5 / math.pi) ** 0.5)


def normalized(values):
    centred = values - jnp.mean(values, axis=1, keepdims=True)
    scale = lax.rsqrt(jnp.mean(centred * centred, axis=1, keepdims=True) + EPSILON)
    return (centred * scale, scale)


def norm_back(normal, scale, grad, gain):
    scaled = grad * gain
    inner = jnp.mean(scaled * normal, axis=1, keepdims=True)
    return scale * (scaled - jnp.mean(scaled, axis=1, keepdims=True) - normal * inner)


def column_sum(values):
    return jnp.sum(values, axis=0, keepdims=True)


def put_rows(out, me_ref, full):
    rows = full.shape[0] // 4
    for x in range(2):
        for a in range(2):
            part = full[(2 * x + a) * rows : (2 * x + a + 1) * rows, :]
            out[lax.bitwise_xor(me_ref[1], x), lax.bitwise_xor(me_ref[2], a), :, : full.shape[1]] = part


def upper_kernel(me_ref, mixed_ref, tokens_ref, cotangent_ref, w_out_ref, w_up_ref, w_down_ref, vectors_ref, b_up_ref,
                 output_ref, grad_ref, normal_ref, scale_ref, low_ref, slope_ref, sent_ref, kept_ref, sums_ref,
                 active_ref):
    me = me_ref[0]
    width = tokens_ref.shape[1]
    hidden = w_up_ref.shape[1]
    step = width
    b_out, gain_first, shift_first, b_down, gain_second, shift_second = [vectors_ref[n : n + 1, :] for n in range(6)]
    branch = dot(mixed_ref[...], w_out_ref[...], TN) + b_out
    normal, scale = normalized(tokens_ref[...].astype(jnp.float32) + branch)
    normal_ref[...] = normal
    scale_ref[...] = jnp.broadcast_to(scale, scale_ref.shape)
    first_norm = normal * gain_first + shift_first
    first_low = first_norm.astype(jnp.bfloat16)
    low_ref[...] = first_low.T
    second = first_norm + b_down
    for at in range(0, hidden, step):
        columns = slice(at, at + step)
        active, slope = gelu_and_slope(dot(first_low, w_up_ref[:, columns]) + b_up_ref[:, columns])
        slope_ref[:, columns] = slope.astype(jnp.bfloat16)
        active = active.astype(jnp.bfloat16)
        active_ref[:, columns] = active
        second = second + dot(active, w_down_ref[columns, :])
    normal, scale = normalized(second)
    output_ref[...] = (normal * gain_second + shift_second).astype(jnp.bfloat16)
    upstream = cotangent_ref[...].astype(jnp.float32)
    grad = norm_back(normal, scale, upstream, gain_second)
    grad_ref[...] = grad
    grad_second = grad.astype(jnp.bfloat16)
    sums_ref[...] = jnp.zeros_like(sums_ref)
    sums_ref[0:1, :] = column_sum(upstream * normal)
    sums_ref[1:2, :] = column_sum(upstream)
    sums_ref[2:3, :] = column_sum(grad_second.astype(jnp.float32))
    rows = hidden // 4
    for distance, out in ((1, sent_ref.at[0]), (3, sent_ref.at[1]), (0, kept_ref.at[0]), (2, kept_ref.at[1])):
        place = pl.multiple_of(lax.bitwise_xor(me, distance) * rows, LANES)
        put_rows(out, me_ref, dot(active_ref[:, pl.ds(place, rows)], grad_second, TN).astype(jnp.bfloat16))


def upper(me, mixed_low, tokens, cotangent, w_out, w_up, w_down, vectors, b_up):
    length, width = tokens.shape
    hidden = w_up.shape[1]
    bf16, f32 = jnp.bfloat16, jnp.float32
    shapes = [
        ((length, width), bf16),
        ((length, width), f32),
        ((length, width), f32),
        ((length, LANES), f32),
        ((width, length), bf16),
        ((length, hidden), bf16),
        ((2, 2, 2, hidden // 16, width), bf16),
        ((2, 2, 2, hidden // 16, width), bf16),
        ((8, width), f32),
    ]
    return pl.pallas_call(
        upper_kernel,
        in_specs=[pl.BlockSpec(memory_space=pltpu.SMEM)]
        + [pl.BlockSpec(memory_space=pltpu.VMEM)] * 3
        + [pl.BlockSpec(memory_space=pltpu.VMEM)] * 3
        + [pl.BlockSpec(memory_space=pltpu.VMEM)] * 2,
        out_shape=[jax.ShapeDtypeStruct(shape, dtype) for shape, dtype in shapes],
        scratch_shapes=[pltpu.VMEM((length, hidden), bf16)],
        compiler_params=pltpu.CompilerParams(vmem_limit_bytes=VMEM_LIMIT),
        cost_estimate=pl.CostEstimate(flops=8 * length * width * hidden, bytes_accessed=24 << 20, transcendentals=0),
        name="upper",
    )(me, mixed_low, tokens, cotangent, w_out, w_up, w_down, vectors, b_up[None, :])


def lower_kernel(me_ref, grad_ref, normal_ref, scale_ref, low_ref, slope_ref, mixed_ref, w_out_ref, w_up_ref, w_down_ref, vectors_ref,
                 sent_up_ref, kept_up_ref, sent_out_ref, kept_out_ref, grad_first_ref, upstream_ref, sums_ref, up_sums_ref,
                 hidden_ref):
    me = me_ref[0]
    width = grad_ref.shape[1]
    hidden = w_up_ref.shape[1]
    step = width
    rows = width // 4
    grad_first = grad_ref[...]
    grad_second = grad_first.astype(jnp.bfloat16)
    up_sums_ref[...] = jnp.zeros_like(up_sums_ref)
    for at in range(0, hidden, step):
        columns = slice(at, at + step)
        grad_hidden = dot(grad_second, w_down_ref[columns, :], NT) * slope_ref[:, columns].astype(jnp.float32)
        grad_hidden = grad_hidden.astype(jnp.bfloat16)
        hidden_ref[:, columns] = grad_hidden
        up_sums_ref[at // step : at // step + 1, :] = column_sum(grad_hidden.astype(jnp.float32))
        grad_first = grad_first + dot(grad_hidden, w_up_ref[:, columns], NT)

    def places(sent, kept):
        for distance, out in ((1, sent.at[0]), (3, sent.at[1]), (0, kept.at[0]), (2, kept.at[1])):
            place = lax.bitwise_xor(me, distance) * rows
            yield (pl.ds(pl.multiple_of(place, rows), rows), out)

    for place, out in places(sent_up_ref, kept_up_ref):
        put_rows(out, me_ref, dot(low_ref[place, :], hidden_ref[...]).astype(jnp.bfloat16))
    normal = normal_ref[...]
    grad = norm_back(normal, scale_ref[:, :1], grad_first, vectors_ref[1:2, :])
    grad_first_ref[...] = grad
    grad_branch = grad.astype(jnp.bfloat16)
    sums_ref[...] = jnp.zeros_like(sums_ref)
    sums_ref[0:1, :] = column_sum(grad_first * normal)
    sums_ref[1:2, :] = column_sum(grad_first)
    sums_ref[2:3, :] = column_sum(grad_branch.astype(jnp.float32))
    upstream_ref[...] = dot(w_out_ref[...], grad_branch, NT).astype(jnp.bfloat16)
    for place, out in places(sent_out_ref, kept_out_ref):
        put_rows(out, me_ref, dot(mixed_ref[place, :], grad_branch).astype(jnp.bfloat16))


def lower(me, grad, normal, scale, low_t, slope, mixed_low, w_out, w_up, w_down, vectors):
    length, width = grad.shape
    hidden = w_up.shape[1]
    bf16, f32 = jnp.bfloat16, jnp.float32
    shapes = [
        ((2, 2, 2, width // 16, hidden), bf16),
        ((2, 2, 2, width // 16, hidden), bf16),
        ((2, 2, 2, width // 16, width), bf16),
        ((2, 2, 2, width // 16, width), bf16),
        ((length, width), f32),
        ((width, length), bf16),
        ((8, width), f32),
        ((8, width), f32),
    ]
    return pl.pallas_call(
        lower_kernel,
        in_specs=[pl.BlockSpec(memory_space=pltpu.SMEM)]
        + [pl.BlockSpec(memory_space=pltpu.VMEM)] * 6
        + [pl.BlockSpec(memory_space=pltpu.VMEM)] * 3
        + [pl.BlockSpec(memory_space=pltpu.VMEM)],
        out_shape=[jax.ShapeDtypeStruct(shape, dtype) for shape, dtype in shapes],
        scratch_shapes=[pltpu.VMEM((length, hidden), bf16)],
        compiler_params=pltpu.CompilerParams(vmem_limit_bytes=VMEM_LIMIT),
        cost_estimate=pl.CostEstimate(flops=8 * length * width * hidden, bytes_accessed=24 << 20, transcendentals=0),
        name="lower",
    )(me, grad, normal, scale, low_t, slope, mixed_low, w_out, w_up, w_down, vectors)


def project_kernel(*refs):
    one_ref, two_ref, w_key_ref, w_value_ref, b_value_ref = refs[:5]
    keys_ref, value_ref = refs[-2:]
    keys = one_ref.shape[0]
    for number, ref in enumerate((one_ref, two_ref)):
        at = slice(number * keys, (number + 1) * keys)
        keys_ref[at, :] = dot(ref[...], w_key_ref[...]).astype(jnp.bfloat16)
        values = dot(w_value_ref[...], ref[...], (((0,), (1,)), ((), ())))
        value_ref[:, at] = (values + b_value_ref[:, :1]).astype(jnp.bfloat16)


def project(one, two, w_key, w_value, b_value, before=()):
    length, width = one.shape
    half = 1 if before else 0
    return pl.pallas_call(
        project_kernel,
        grid=(1,),
        in_specs=[
            pl.BlockSpec((length, width), lambda i: (0, 0)),
            pl.BlockSpec((length, width), lambda i: (0, 0)),
            pl.BlockSpec((width, width), lambda i: (0, 0)),
            pl.BlockSpec((width, width), lambda i: (0, 0)),
            pl.BlockSpec((width, LANES), lambda i: (0, 0)),
        ]
        + [pl.BlockSpec(memory_space=pl.ANY)] * len(before),
        out_specs=[
            pl.BlockSpec((2 * length, width), lambda i: (half, 0)),
            pl.BlockSpec((width, 2 * length), lambda i: (0, half)),
        ],
        out_shape=[
            jax.ShapeDtypeStruct((4 * length, width), jnp.bfloat16),
            jax.ShapeDtypeStruct((width, 4 * length), jnp.bfloat16),
        ],
        input_output_aliases={5: 0, 6: 1} if before else {},
        compiler_params=pltpu.CompilerParams(vmem_limit_bytes=VMEM_LIMIT),
        cost_estimate=pl.CostEstimate(flops=8 * length * width * width, bytes_accessed=6 << 20, transcendentals=0),
        name="project",
    )(one, two, w_key, w_value, b_value, *before)


def project_back_kernel(grad_key_ref, grad_value_ref, w_key_ref, w_value_ref, sent_ref, near_ref, far_ref):
    keys = near_ref.shape[0]
    for slot, out in enumerate((near_ref, sent_ref.at[:keys], far_ref, sent_ref.at[keys:])):
        at = slice(slot * keys, (slot + 1) * keys)
        total = dot(grad_key_ref[at, :], w_key_ref[...], NT) + dot(grad_value_ref[at, :], w_value_ref[...], NT)
        out[...] = total.astype(jnp.bfloat16)


def project_back(grad_keys, grad_values, w_key, w_value):
    length, width = grad_keys.shape
    sizes = (length // 2, length // 4, length // 4)
    return pl.pallas_call(
        project_back_kernel,
        out_shape=[jax.ShapeDtypeStruct((size, width), jnp.bfloat16) for size in sizes],
        compiler_params=pltpu.CompilerParams(vmem_limit_bytes=VMEM_LIMIT),
        cost_estimate=pl.CostEstimate(flops=0, bytes_accessed=0, transcendentals=0),
        name="project_back",
    )(grad_keys, grad_values, w_key, w_value)


def backward_kernel(me_ref, far_ref, order_ref, across_ref, down_ref, raised_ref, query_ref, upstream_ref, inverse_ref, mixed_ref,
                    value_ref, key_ref, rows_a, rows_b, rows_c, rows_d, upper_sums_ref, lower_sums_ref, up_sums_ref,
                    grad_query_ref, grad_key_ref, grad_value_ref, sent_ref, kept_ref,
                    sum_ref, grad_ref, count_ref, scaled_ref, dot_ref, value_sum_ref, all_pairs_ref, all_rows_ref, small_ref,
                    *, heads, scale, key_scale):
    slot = pl.program_id(0)
    keys, queries = order_ref.shape
    width = query_ref.shape[0]
    head_size = PAIR // 2
    group = 16
    per_super = 4
    supers = keys // (group * per_super)
    buckets = count_ref.shape[1] // group

    @pl.when(slot == 0)
    def _():
        sum_ref[...] = jnp.zeros_like(sum_ref)
        count_ref[...] = jnp.zeros_like(count_ref)
        value_sum_ref[...] = jnp.zeros_like(value_sum_ref)
        for index, ref in enumerate((rows_a, rows_b, rows_c, rows_d)):
            all_rows_ref[index * keys : (index + 1) * keys, :] = ref[...]
        for head in range(heads):
            feature = slice(head * head_size, (head + 1) * head_size)
            scaled = (upstream_ref[feature, :].astype(jnp.float32) * inverse_ref[feature, :]).astype(jnp.bfloat16)
            scaled_ref[feature, :] = scaled
            dot_ref[head : head + 1, :] = jnp.sum(scaled.astype(jnp.float32) * mixed_ref[feature, :], axis=0, keepdims=True)

    rows = lax.broadcasted_iota(jnp.int32, (PAIR, queries), 0)
    here = pl.ds(pl.multiple_of(slot * keys, keys), keys)
    for pair in range(heads // 2):
        at = slice(pair * PAIR, (pair + 1) * PAIR)
        query_pair = query_ref[at, :]
        mixed_pair = scaled_ref[at, :]
        zero = jnp.zeros_like(query_pair)
        query_both = [jnp.where(rows < head_size, query_pair, zero), jnp.where(rows >= head_size, query_pair, zero)]
        mixed_both = [jnp.where(rows < head_size, mixed_pair, zero), jnp.where(rows >= head_size, mixed_pair, zero)]
        query_both = jnp.concatenate(query_both, axis=1)
        mixed_both = jnp.concatenate(mixed_both, axis=1)
        grad_probs = dot(value_ref[at, :], mixed_both, TN)
        raised = jnp.concatenate([raised_ref[2 * pair], raised_ref[2 * pair + 1]], axis=1)
        dots = jnp.concatenate([dot_ref[2 * pair : 2 * pair + 1, :], dot_ref[2 * pair + 1 : 2 * pair + 2, :]], axis=1)
        grad = (raised.astype(jnp.float32) * (grad_probs - dots)).astype(jnp.bfloat16)
        grad_values = dot(raised, mixed_both, NT).astype(jnp.bfloat16)
        grad_value_ref[:, at] = grad_values
        all_pairs_ref[here, width + pair * PAIR : width + (pair + 1) * PAIR] = grad_values
        value_sum_ref[:, at] += jnp.sum(grad_values.astype(jnp.float32).reshape(keys // 8, 8, PAIR), axis=0)
        grad_keys = (dot(grad, query_both, NT) * key_scale).astype(jnp.bfloat16)
        grad_key_ref[:, at] = grad_keys
        all_pairs_ref[here, at] = grad_keys
        both = dot(key_ref[:, at], grad, TN)
        sum_ref[at.start : at.start + head_size, :] += both[:head_size, :queries]
        sum_ref[at.start + head_size : at.stop, :] += both[head_size:, queries:]
        for one in range(2):
            head = 2 * pair + one
            mine = grad[:, one * queries : (one + 1) * queries]
            for g in range(keys // group):
                lanes = slice((g % per_super) * queries, (g % per_super + 1) * queries)
                grad_ref[g // per_super, head * group : (head + 1) * group, lanes] = mine[g * group : (g + 1) * group, :]

    def add_counts(number, ref, sup, grads):
        parts = []
        for sub in range(per_super):
            at = pl.multiple_of(sup * (group * per_super) + sub * group, group)
            ids = ref[pl.ds(at, group), :]
            hot = [jnp.where(ids == b + number * buckets, 1.0, 0.0).astype(jnp.bfloat16) for b in range(buckets)]
            parts.append(jnp.concatenate(hot, axis=0))
        count_ref[number] += dot(jnp.concatenate(parts, axis=1), grads, NT)

    def tally(sup, _):
        grads = grad_ref[sup]
        add_counts(1, across_ref, sup, grads)
        add_counts(2, down_ref, sup, grads)
        far = far_ref[slot * supers + sup]

        @pl.when(far == 0)
        def _():
            add_counts(0, order_ref, sup, grads)

        @pl.when(far > 0)
        def _():
            at = pl.ds(pl.multiple_of(far * group, group), group)
            count_ref[0, at, :] += dot(jnp.ones((group, per_super * queries), jnp.bfloat16), grads, NT)

        return 0

    lax.fori_loop(0, supers, tally, 0)

    @pl.when(slot == pl.num_programs(0) - 1)
    def _():
        grad_queries = (sum_ref[...] * scale).astype(jnp.bfloat16)
        grad_query_ref[...] = grad_queries
        bias_query = dot(jnp.ones((8, queries), jnp.bfloat16), grad_queries, NT)[:1]
        sums = [upper_sums_ref[:3, :], lower_sums_ref[:3, :], column_sum(value_sum_ref[...]), bias_query]
        for number, part in enumerate((jnp.concatenate(sums, axis=0), up_sums_ref[...])):
            for at in range(0, width, LANES):
                place = (number * width + at) // LANES * 8
                small_ref[place : place + 8, :] = part[:, at : at + LANES]
        used = 2 * width // LANES * 8
        place = lax.broadcasted_iota(jnp.int32, (buckets * group, heads * group), 0) % group
        other = lax.broadcasted_iota(jnp.int32, (buckets * group, heads * group), 1) % group
        owner = lax.broadcasted_iota(jnp.int32, (heads * group, LANES), 0) // group
        column = lax.broadcasted_iota(jnp.int32, (heads * group, LANES), 1)
        gather = jnp.where(owner == column, 1.0, 0.0)
        for number in range(3):
            kept = jnp.where(place == other, count_ref[number], 0.0)
            kept = jnp.sum(kept.reshape(buckets, group, heads * group), axis=1)
            table = jnp.dot(kept, gather, preferred_element_type=jnp.float32, precision=lax.Precision.HIGHEST)
            small_ref[used + number * buckets : used + (number + 1) * buckets, :] = table
        small = small_ref[...].astype(jnp.bfloat16)
        each = width // 4
        for side in range(2):
            for out in (sent_ref, kept_ref):
                for x in range(2):
                    for a in range(2):
                        part = small[(2 * x + a) * each // 4 : (2 * x + a + 1) * each // 4, :]
                        out[side, lax.bitwise_xor(me_ref[1], x), lax.bitwise_xor(me_ref[2], a), :, 3 * width :] = part
        parts = (
            (slice(0, width), dot(rows_a[...], grad_queries, (((0,), (1,)), ((), ())))),
            (slice(width, 3 * width), dot(all_rows_ref[...], all_pairs_ref[...], TN)),
        )
        for columns, full in parts:
            full = full.astype(jnp.bfloat16)
            for quarter in range(4):
                distance = lax.bitwise_xor(me_ref[0], quarter)
                for x in range(2):
                    for a in range(2):
                        first = quarter * each + (2 * x + a) * each // 4
                        part = full[first : first + each // 4, :]
                        at_x, at_a = lax.bitwise_xor(me_ref[1], x), lax.bitwise_xor(me_ref[2], a)

                        @pl.when(distance % 2 == 1)
                        def _():
                            sent_ref[distance // 2, at_x, at_a, :, columns] = part

                        @pl.when(distance % 2 == 0)
                        def _():
                            kept_ref[distance // 2, at_x, at_a, :, columns] = part


def attention_backward(me, far, order, across, down, raised, query_t, upstream_t, inverse_t, mixed_t, value_t, keys_in, row_slots,
                       small_sums, scale, key_scale):
    width, queries = query_t.shape
    heads = raised.shape[0]
    length = keys_in.shape[0]
    slots = len(row_slots)
    keys = length // slots
    buckets = 32
    group = 16
    ids = pl.BlockSpec((keys, queries), lambda s: (s, 0))
    full = pl.BlockSpec((width, queries), lambda s: (0, 0))
    rows = pl.BlockSpec((keys, width), lambda s: (s, 0))
    last = (2, 2, 2, width // 16, 3 * width + LANES)
    return pl.pallas_call(
        functools.partial(backward_kernel, heads=heads, scale=scale, key_scale=key_scale),
        grid=(slots,),
        in_specs=[
            pl.BlockSpec(memory_space=pltpu.SMEM),
            pl.BlockSpec(memory_space=pltpu.SMEM),
            ids, ids, ids,
            pl.BlockSpec((heads, keys, queries), lambda s: (0, s, 0)),
            full, full, full, full,
            pl.BlockSpec((width, keys), lambda s: (0, s)),
            rows,
        ]
        + [pl.BlockSpec((keys, width), lambda s: (0, 0))] * slots
        + [pl.BlockSpec((8, width), lambda s: (0, 0))] * len(small_sums),
        out_specs=[full, rows, rows] + [pl.BlockSpec(last, lambda s: (0, 0, 0, 0, 0))] * 2,
        out_shape=[
            jax.ShapeDtypeStruct((width, queries), jnp.bfloat16),
            jax.ShapeDtypeStruct((length, width), jnp.bfloat16),
            jax.ShapeDtypeStruct((length, width), jnp.bfloat16),
            jax.ShapeDtypeStruct(last, jnp.bfloat16),
            jax.ShapeDtypeStruct(last, jnp.bfloat16),
        ],
        scratch_shapes=[
            pltpu.VMEM((width, queries), jnp.float32),
            pltpu.VMEM((keys // (group * 4), heads * group, 4 * queries), jnp.bfloat16),
            pltpu.VMEM((3, buckets * group, heads * group), jnp.float32),
            pltpu.VMEM((width, queries), jnp.bfloat16),
            pltpu.VMEM((16, queries), jnp.float32),
            pltpu.VMEM((8, width), jnp.float32),
            pltpu.VMEM((length, 2 * width), jnp.bfloat16),
            pltpu.VMEM((length, width), jnp.bfloat16),
            pltpu.VMEM((width // slots, LANES), jnp.float32),
        ],
        compiler_params=pltpu.CompilerParams(vmem_limit_bytes=VMEM_LIMIT),
        cost_estimate=pl.CostEstimate(flops=0, bytes_accessed=0, transcendentals=0),
        name="attention_backward",
    )(me, far, order, across, down, raised, query_t, upstream_t, inverse_t, mixed_t, value_t, keys_in, *row_slots, *small_sums)


MARK_FLOPS = 20000000000


def bucketize(offsets, limits):
    magnitude = jnp.abs(offsets)

    def pick(bits, first, size):
        if not bits:
            return limits[first + size // 2]
        half = size // 2
        return jnp.where(bits[0], pick(bits[1:], first + half + 1, half), pick(bits[1:], first, half))

    bits = []
    total = 16 * (offsets > 0).astype(jnp.int32)
    weight = (len(limits) + 1) // 2
    while weight:
        bit = magnitude >= pick(bits, 0, len(limits))
        bits.append(bit)
        total = total + jnp.where(bit, weight, 0)
        weight = weight // 2
    return total


def einsum(spec, left, right):
    return jnp.einsum(spec, left, right, preferred_element_type=jnp.float32)


def exchange(array, axis_name, distance):
    pairs = [(i, i ^ distance) for i in range(lax.axis_size(axis_name))]
    return lax.ppermute(array, axis_name, pairs)


def in_blocks(sent, kept):
    return (kept, exchange(sent, "blk", 1))


def mark_kernel(array_ref, out_ref):
    out_ref[...] = jnp.zeros_like(out_ref)


def mark_of(array, flops):
    return pl.pallas_call(
        mark_kernel,
        in_specs=[pl.BlockSpec(memory_space=pl.ANY)],
        out_specs=pl.BlockSpec(memory_space=pltpu.VMEM),
        out_shape=jax.ShapeDtypeStruct((8, LANES), jnp.float32),
        compiler_params=pltpu.CompilerParams(has_side_effects=True),
        cost_estimate=pl.CostEstimate(flops=flops, bytes_accessed=4096, transcendentals=0),
        name="mark",
    )(array)


BITS = {"y": 0, "x": 1, "a": 2}


def add_low(left, right):
    return (left.astype(jnp.float32) + right.astype(jnp.float32)).astype(jnp.bfloat16)


def reduce_rows(kept, got, order, back, sides):
    distances = {"y": ("blk", 2), "x": ("docs", 1), "a": ("docs", 2)}
    for letter in order:
        bit = BITS[letter]
        near = [lax.slice_in_dim(array, 0, 1, axis=bit) for array in (kept, got)]
        away = [lax.slice_in_dim(array, 1, 2, axis=bit) for array in (kept, got)]
        got = yield (add_low(*away), *distances[letter])
        kept = add_low(*near)
    data = add_low(kept, got)
    distance = 4
    while distance < lax.axis_size("docs"):
        got = yield (data, "docs", distance)
        data = add_low(data, got)
        distance = distance * 2
    for letter in back:
        got = yield (data, *distances[letter])
        data = jnp.concatenate([data, got], axis=BITS[letter])
    for letter in back:
        bit = BITS[letter]
        near = lax.slice_in_dim(data, 0, 1, axis=bit)
        away = lax.slice_in_dim(data, 1, 2, axis=bit)
        halves = [jnp.where(sides[letter] == 0, near, away), jnp.where(sides[letter] == 0, away, near)]
        data = jnp.concatenate(halves, axis=bit)
    return data.reshape(-1, data.shape[4])


class Line:
    def __init__(self):
        self.last = None
        self.waiting = {}
        self.steps = {}
        self.results = {}

    def after(self, *arrays):
        if self.last is None:
            return arrays
        return lax.optimization_barrier((*arrays, self.last))[:-1]

    def mark(self, array):
        self.last = array

    def send(self, name):
        array, axis_name, distance = self.waiting[name]
        self.waiting[name] = exchange(array, axis_name, distance)
        self.mark(array)

    def begin(self, name, steps, marked):
        self.steps[name] = steps
        array, axis_name, distance = next(steps)
        self.waiting[name] = exchange(array, axis_name, distance)
        self.mark(mark_of(array, 20_000_000_000) if marked else array)

    def go(self, names):
        for name in names:
            if name in self.results:
                continue
            (got,) = self.after(self.waiting[name])
            try:
                self.waiting[name] = self.steps[name].send(got)
            except StopIteration as stop:
                self.results[name] = stop.value
                continue
            self.send(name)

    def finish(self, names):
        while any(name not in self.results for name in names):
            self.go(names)


def body(
    tokens,
    box_corners,
    cotangent,
    w_query,
    b_query,
    w_key,
    w_value,
    b_value,
    w_out,
    b_out,
    gain_first,
    shift_first,
    w_up,
    b_up,
    w_down,
    b_down,
    gain_second,
    shift_second,
    table_order,
    table_horizontal,
    table_vertical,
):
    docs_here, doc_length, model_width = tokens.shape
    bucket_total, head_count = table_order.shape
    head_size = model_width // head_count
    score_scale = head_size ** (-0.5)
    blk_count = lax.axis_size("blk")
    me = lax.axis_index("blk")
    rows_in = tokens.reshape(doc_length, model_width)

    centres = jnp.stack([box_corners[0, 0] + box_corners[2, 0], box_corners[1, 0] + box_corners[3, 0]])
    centres = centres.astype(jnp.float32)
    centre_slots = [centres] + [exchange(centres, "blk", s) for s in range(1, blk_count)]
    core_rows = exchange(rows_in, "blk", 1)
    far_rows = exchange(rows_in, "blk", 2)
    row_slots = [rows_in, core_rows, far_rows, exchange(far_rows, "blk", 1)]
    centres_all = jnp.concatenate(centre_slots, axis=1).astype(jnp.int32)
    centres_own = centres.astype(jnp.int32)

    inside = jnp.arange(doc_length, dtype=jnp.int32)
    key_place = jnp.concatenate([(me ^ s) * doc_length + inside for s in range(blk_count)])
    query_place = me * doc_length + inside
    order = bucketize(key_place[:, None] - query_place[None, :], ORDER_LIMITS)
    across = bucketize(centres_all[0][:, None] - centres_own[0][None, :], BOX_LIMITS) + bucket_total
    down = bucketize(centres_all[1][:, None] - centres_own[1][None, :], BOX_LIMITS) + 2 * bucket_total
    tile = jnp.arange(LANES, dtype=jnp.int32)
    near = [bucketize(t * LANES + tile[:, None] - tile[None, :], ORDER_LIMITS) for t in range(-2, 3)]
    near = jnp.concatenate(near, axis=0)
    tiles = (key_place[::LANES, None] - query_place[None, ::LANES]) // LANES
    tiles = (jnp.clip(tiles, -2, 2) + 2) * LANES
    first_key = key_place[::64]
    beyond = jnp.where(first_key > query_place[-1], first_key - query_place[-1], query_place[0] - (first_key + 63))
    far_order = jnp.where(beyond >= ORDER_LIMITS[-1], 15 + 16 * (first_key > query_place[-1]), 0).astype(jnp.int32)
    tables = jnp.concatenate([table_order, table_horizontal, table_vertical], axis=0).T
    tables = jnp.round((tables + 5.0) * UNIT).astype(jnp.int32)
    tables = tables[0::2] + FIELD * tables[1::2]
    tables = jnp.pad(tables, ((0, 0), (0, LANES - 3 * bucket_total)))[:, None, :]

    query_t = (einsum("df,td->ft", w_query, rows_in) + b_query[:, None]).astype(jnp.bfloat16)
    query_t = query_t * jnp.bfloat16(score_scale * UNIT)
    bias_column = jnp.broadcast_to(b_value[:, None], (model_width, LANES))
    vectors_in = jnp.stack([b_out, gain_first, shift_first, b_down, gain_second, shift_second, b_out, b_out])
    projected = project(rows_in, core_rows, w_key, w_value, bias_column)
    keys, value_t = project(row_slots[2], row_slots[3], w_key, w_value, bias_column, projected)
    keys, order, vectors_in, far_order = lax.optimization_barrier((keys, order, vectors_in, far_order))
    raised, mixed_t, inverse_t, mixed_low = attention_forward(
        tiles, tables, near, across, down, query_t, keys, value_t
    )

    here = lax.axis_index("docs")
    place = jnp.stack([me, here % 2, (here // 2) % 2]).astype(jnp.int32)
    cotangents = cotangent.reshape(doc_length, model_width)
    output, grad_pre2, normal, scale, low_t, slope, sent_down, kept_down, upper_sums = upper(
        place, mixed_low, rows_in, cotangents, w_out, w_up, w_down, vectors_in, b_up
    )
    parts_down = in_blocks(sent_down, kept_down)
    sent_up, kept_up, sent_out, kept_out, grad_pre1, upstream_t, lower_sums, up_sums = lower(
        place, grad_pre2, normal, scale, low_t, slope, mixed_low, w_out, w_up, w_down, vectors_in
    )
    parts_up = in_blocks(sent_up, kept_up)
    parts_out = in_blocks(sent_out, kept_out)
    output = output.reshape(tokens.shape)

    sides = {"y": 0, "x": here % 2, "a": (here // 2) % 2}
    line = Line()
    line.mark(upstream_t)
    def begin(name, parts, order, back):
        kept, got = parts
        (got,) = line.after(got)
        line.begin(name, reduce_rows(kept, got, order, back, sides), name == "last")

    begin("down", parts_down, "axy", "xa")
    begin("up", parts_up, "xay", "ax")
    begin("out", parts_out, "yxa", "xa")
    (upstream_t,) = line.after(upstream_t)
    grad_query_t, grad_keys, grad_values, sent_last, kept_last = attention_backward(
        place, far_order, order, across, down, raised, query_t, upstream_t, inverse_t, mixed_t, value_t, keys, row_slots,
        (upper_sums, lower_sums, up_sums), score_scale, 1.0 / UNIT
    )
    parts_last = in_blocks(sent_last, kept_last)
    line.mark(sent_last)
    line.mark(mark_of(line.last, 20000000000))
    line.go(["up"])
    begin("last", parts_last, "ayx", "ax")
    line.mark(mark_of(line.last, 20000000000))
    line.go(["down", "out", "up"])
    grad_keys, grad_values = line.after(grad_keys, grad_values)
    shared_sent, shared_near, shared_far = project_back(grad_keys, grad_values, w_key, w_value)
    line.mark(shared_sent)
    near = exchange(shared_sent, "blk", 1)
    line.mark(mark_of(line.last, 5000000000))
    line.go(["up", "out", "down"])
    line.mark(mark_of(line.last, 20000000000))
    line.go(["last", "out", "down", "up"])
    (near,) = line.after(near)
    near = near.astype(jnp.float32)
    far_sent = (shared_far.astype(jnp.float32) + near[doc_length:]).astype(jnp.bfloat16)
    line.mark(far_sent)
    far = exchange(far_sent, "blk", 2)
    line.go(["last", "out"])
    line.mark(mark_of(line.last, 20000000000))
    line.go(["last", "out", "down", "up", "out"])
    line.go(["last", "down"])
    line.mark(mark_of(line.last, 20000000000))
    grad_query_t, far = line.after(grad_query_t, far)
    grad_inputs = grad_pre1 + einsum("ft,df->td", grad_query_t, w_query) + shared_near.astype(jnp.float32) + near[:doc_length]
    grad_tokens = (grad_inputs + far.astype(jnp.float32)).astype(jnp.bfloat16).reshape(tokens.shape)
    line.mark(grad_tokens)
    line.go(["last", "up", "down", "last"])
    line.finish(["down", "last", "up", "out"])

    (grad_w_down, grad_w_up, grad_w_out) = [line.results[name].astype(jnp.float32) for name in ("down", "up", "out")]
    last = line.results["last"]
    grads = [last[:, n * model_width : (n + 1) * model_width].astype(jnp.float32) for n in range(3)]
    grad_w_query, grad_w_key, grad_w_value = grads
    flat = last[:, 3 * model_width :].astype(jnp.float32)
    tiles_each = model_width // LANES
    rows = model_width // blk_count

    def vectors(first):
        block = flat[first : first + 8 * tiles_each].reshape(tiles_each, 8, LANES)
        return jnp.transpose(block, (1, 0, 2)).reshape(8, model_width)

    each = lax.dynamic_slice_in_dim(vectors(0), me * rows, rows, 1)
    grad_b_up = lax.dynamic_slice_in_dim(vectors(8 * tiles_each), me, 1, 0)[0]
    table_rows = bucket_total // blk_count
    table_out = []
    for number in range(3):
        first = 16 * tiles_each + number * bucket_total + me * table_rows
        table_out.append(lax.dynamic_slice_in_dim(flat, first, table_rows, 0)[:, :head_count])
    small_out = [each[7], each[6], each[5], each[3], each[4], grad_b_up, each[2], each[0], each[1], *table_out]
    return (
        output,
        grad_tokens,
        grad_w_query,
        small_out[0],
        grad_w_key,
        grad_w_value,
        small_out[1],
        grad_w_out,
        small_out[2],
        small_out[3],
        small_out[4],
        grad_w_up,
        small_out[5],
        grad_w_down,
        small_out[6],
        small_out[7],
        small_out[8],
        small_out[9],
        small_out[10],
        small_out[11],
    )


def solution(mesh):
    return jax.shard_map(
        body,
        mesh=mesh,
        in_specs=(
            P("docs", "blk", None),
            P(None, "docs", "blk"),
            P("docs", "blk", None),
            P(),
            P(),
            P(),
            P(),
            P(),
            P(),
            P(),
            P(),
            P(),
            P(),
            P(),
            P(),
            P(),
            P(),
            P(),
            P(),
            P(),
            P(),
        ),
        out_specs=(
            P("docs", "blk", None),
            P("docs", "blk", None),
            P("blk", None),
            P("blk"),
            P("blk", None),
            P("blk", None),
            P("blk"),
            P("blk", None),
            P("blk"),
            P("blk"),
            P("blk"),
            P("blk", None),
            P("blk"),
            P("blk", None),
            P("blk"),
            P("blk"),
            P("blk"),
            P("blk", None),
            P("blk", None),
            P("blk", None),
        ),
        check_vma=False,
    )
```

```python
import functools
import math

import jax
import jax.numpy as jnp
from jax import lax
from jax.experimental import pallas as pl
from jax.experimental.pallas import tpu as pltpu
from jax.sharding import PartitionSpec as P

ORDER_LIMITS = (1, 2, 3, 4, 5, 6, 7, 8, 12, 16, 23, 32, 45, 64, 91)
BOX_LIMITS = (2, 4, 6, 8, 12, 16, 24, 32, 48, 64, 96, 128, 192, 256, 384)
EPSILON = 1e-05
LANES = 128
PAIR = 128
VMEM_LIMIT = 60 * 1024 * 1024
FIELD = 65536
LOG2E = 1.4426950408889634
UNIT = 2048.0

def forward_kernel(tile_ref, table_ref, near_ref, across_ref, down_ref, query_ref, key_ref, value_ref,
                   raised_ref, mixed_ref, inverse_ref, mixed_low_ref, score_ref, order_ref, value_sums_ref):
    keys, queries = across_ref.shape
    head_size = PAIR // 2
    rows = lax.broadcasted_iota(jnp.int32, (PAIR, queries), 0)
    query_pair = query_ref[...]
    zero = jnp.zeros_like(query_pair)
    both = jnp.concatenate(
        [jnp.where(rows < head_size, query_pair, zero), jnp.where(rows >= head_size, query_pair, zero)], axis=1
    )
    step = 16
    numbers = lax.GatherDimensionNumbers(
        offset_dims=(), collapsed_slice_dims=(1,), start_index_map=(1,),
        operand_batching_dims=(0,), start_indices_batching_dims=(0,),
    )

    def pick(places):
        table = jnp.broadcast_to(table_ref[0], places.shape)
        return lax.gather(table, places[..., None], numbers, (1, 1), mode=lax.GatherScatterMode.PROMISE_IN_BOUNDS)

    for at in range(0, near_ref.shape[0], step):
        order_ref[at : at + step, :] = pick(near_ref[at : at + step, :])
    value_sums_ref[0, :head_size, :] = value_ref[:head_size, :]
    value_sums_ref[1, :head_size, :] = value_ref[head_size:, :]
    value_sums_ref[:, head_size:, :] = jnp.ones((2, 16, keys), jnp.bfloat16)

    peaks = [jnp.full((8, LANES), -jnp.inf, jnp.float32) for _ in range(2 * queries // LANES)]
    for at in range(0, keys, step):
        raw = jnp.dot(key_ref[at : at + step, :], both, preferred_element_type=jnp.float32)
        for lane in range(0, queries, LANES):
            lanes = slice(lane, lane + LANES)
            start = pl.multiple_of(tile_ref[at // LANES, lane // LANES] + at % LANES, step)
            code = order_ref[pl.ds(start, step), :]
            code = code + pick(across_ref[at : at + step, lanes]) + pick(down_ref[at : at + step, lanes])
            for head, field in enumerate((lax.bitwise_and(code, FIELD - 1), lax.shift_right_logical(code, 16))):
                place = head * queries + lane
                score = raw[:, place : place + LANES] + field.astype(jnp.float32)
                score_ref[at : at + step, place : place + LANES] = score
                peaks[place // LANES] = jnp.maximum(peaks[place // LANES], jnp.max(score.reshape(step // 8, 8, LANES), axis=0))
    peak = jnp.max(jnp.concatenate(peaks, axis=1), axis=0, keepdims=True)
    for head in range(2):
        lanes = slice(head * queries, (head + 1) * queries)
        for at in range(0, keys, step):
            raised = jnp.exp2((score_ref[at : at + step, lanes] - peak[:, lanes]) * (LOG2E / UNIT)).astype(jnp.bfloat16)
            raised_ref[head, at : at + step, :] = raised
        sums = jnp.dot(value_sums_ref[head], raised_ref[head], preferred_element_type=jnp.float32)
        inverse = 1.0 / sums[head_size : head_size + 1, :]
        mixed = sums[:head_size, :] * inverse
        mixed_ref[head * head_size : (head + 1) * head_size, :] = mixed
        mixed_low_ref[head * head_size : (head + 1) * head_size, :] = mixed.astype(jnp.bfloat16)
        inverse_ref[head * head_size : (head + 1) * head_size, :] = jnp.broadcast_to(inverse, (head_size, queries))


def attention_forward(tiles, tables, near, across, down, query_t, keys, value_t):
    width, queries = query_t.shape
    length = keys.shape[0]
    pairs = width // PAIR
    whole = pl.BlockSpec((length, queries), lambda p: (0, 0))
    return pl.pallas_call(
        forward_kernel,
        grid=(pairs,),
        in_specs=[
            pl.BlockSpec(memory_space=pltpu.SMEM),
            pl.BlockSpec((1, 1, LANES), lambda p: (p, 0, 0)),
            pl.BlockSpec(near.shape, lambda p: (0, 0)),
            whole, whole,
            pl.BlockSpec((PAIR, queries), lambda p: (p, 0)),
            pl.BlockSpec((length, PAIR), lambda p: (0, p)),
            pl.BlockSpec((PAIR, length), lambda p: (p, 0)),
        ],
        out_specs=[
            pl.BlockSpec((2, length, queries), lambda p: (p, 0, 0)),
            pl.BlockSpec((PAIR, queries), lambda p: (p, 0)),
            pl.BlockSpec((PAIR, queries), lambda p: (p, 0)),
            pl.BlockSpec((PAIR, queries), lambda p: (p, 0)),
        ],
        out_shape=[
            jax.ShapeDtypeStruct((2 * pairs, length, queries), jnp.bfloat16),
            jax.ShapeDtypeStruct((width, queries), jnp.float32),
            jax.ShapeDtypeStruct((width, queries), jnp.float32),
            jax.ShapeDtypeStruct((width, queries), jnp.bfloat16),
        ],
        scratch_shapes=[
            pltpu.VMEM((length, 2 * queries), jnp.float32),
            pltpu.VMEM(near.shape, jnp.int32),
            pltpu.VMEM((2, PAIR // 2 + 16, length), jnp.bfloat16),
        ],
        compiler_params=pltpu.CompilerParams(vmem_limit_bytes=VMEM_LIMIT),
        cost_estimate=pl.CostEstimate(flops=4 * width * queries * length, bytes_accessed=16 << 20, transcendentals=0),
        name="attention_forward",
    )(tiles, tables, near, across, down, query_t, keys, value_t)


ERF_P = 0.3275911
ERF_A = (0.254829592, -0.284496736, 1.421413741, -1.453152027, 1.061405429)
TN = (((0,), (0,)), ((), ()))
NT = (((1,), (1,)), ((), ()))


def dot(left, right, numbers=(((1,), (0,)), ((), ()))):
    return lax.dot_general(left, right, numbers, preferred_element_type=jnp.float32)


def gelu_and_slope(values):
    size = jnp.abs(values) * (0.5**0.5)
    near = 1.0 / (1.0 + ERF_P * size)
    series = ERF_A[4]
    for term in ERF_A[3::-1]:
        series = series * near + term
    bell = jnp.exp(-(size * size))
    tail = 0.5 * (series * near) * bell
    share = jnp.where(values >= 0, 1.0 - tail, tail)
    return (values * share, share + values * bell * (0.5 / math.pi) ** 0.5)


def normalized(values):
    centred = values - jnp.mean(values, axis=1, keepdims=True)
    scale = lax.rsqrt(jnp.mean(centred * centred, axis=1, keepdims=True) + EPSILON)
    return (centred * scale, scale)


def norm_back(normal, scale, grad, gain):
    scaled = grad * gain
    inner = jnp.mean(scaled * normal, axis=1, keepdims=True)
    return scale * (scaled - jnp.mean(scaled, axis=1, keepdims=True) - normal * inner)


def column_sum(values):
    return jnp.sum(values, axis=0, keepdims=True)


def put_rows(out, me_ref, full):
    rows = full.shape[0] // 4
    for x in range(2):
        for a in range(2):
            part = full[(2 * x + a) * rows : (2 * x + a + 1) * rows, :]
            out[lax.bitwise_xor(me_ref[1], x), lax.bitwise_xor(me_ref[2], a), :, : full.shape[1]] = part


def upper_kernel(me_ref, mixed_ref, tokens_ref, cotangent_ref, w_out_ref, w_up_ref, w_down_ref, vectors_ref, b_up_ref,
                 output_ref, grad_ref, normal_ref, scale_ref, low_ref, slope_ref, sent_ref, kept_ref, sums_ref,
                 active_ref):
    me = me_ref[0]
    width = tokens_ref.shape[1]
    hidden = w_up_ref.shape[1]
    step = width
    b_out, gain_first, shift_first, b_down, gain_second, shift_second = [vectors_ref[n : n + 1, :] for n in range(6)]
    branch = dot(mixed_ref[...], w_out_ref[...], TN) + b_out
    normal, scale = normalized(tokens_ref[...].astype(jnp.float32) + branch)
    normal_ref[...] = normal
    scale_ref[...] = jnp.broadcast_to(scale, scale_ref.shape)
    first_norm = normal * gain_first + shift_first
    first_low = first_norm.astype(jnp.bfloat16)
    low_ref[...] = first_low.T
    second = first_norm + b_down
    for at in range(0, hidden, step):
        columns = slice(at, at + step)
        active, slope = gelu_and_slope(dot(first_low, w_up_ref[:, columns]) + b_up_ref[:, columns])
        slope_ref[:, columns] = slope.astype(jnp.bfloat16)
        active = active.astype(jnp.bfloat16)
        active_ref[:, columns] = active
        second = second + dot(active, w_down_ref[columns, :])
    normal, scale = normalized(second)
    output_ref[...] = (normal * gain_second + shift_second).astype(jnp.bfloat16)
    upstream = cotangent_ref[...].astype(jnp.float32)
    grad = norm_back(normal, scale, upstream, gain_second)
    grad_ref[...] = grad
    grad_second = grad.astype(jnp.bfloat16)
    sums_ref[...] = jnp.zeros_like(sums_ref)
    sums_ref[0:1, :] = column_sum(upstream * normal)
    sums_ref[1:2, :] = column_sum(upstream)
    sums_ref[2:3, :] = column_sum(grad_second.astype(jnp.float32))
    rows = hidden // 4
    for distance, out in ((1, sent_ref.at[0]), (3, sent_ref.at[1]), (0, kept_ref.at[0]), (2, kept_ref.at[1])):
        place = pl.multiple_of(lax.bitwise_xor(me, distance) * rows, LANES)
        put_rows(out, me_ref, dot(active_ref[:, pl.ds(place, rows)], grad_second, TN).astype(jnp.bfloat16))


def upper(me, mixed_low, tokens, cotangent, w_out, w_up, w_down, vectors, b_up):
    length, width = tokens.shape
    hidden = w_up.shape[1]
    bf16, f32 = jnp.bfloat16, jnp.float32
    shapes = [
        ((length, width), bf16),
        ((length, width), f32),
        ((length, width), f32),
        ((length, LANES), f32),
        ((width, length), bf16),
        ((length, hidden), bf16),
        ((2, 2, 2, hidden // 16, width), bf16),
        ((2, 2, 2, hidden // 16, width), bf16),
        ((8, width), f32),
    ]
    return pl.pallas_call(
        upper_kernel,
        in_specs=[pl.BlockSpec(memory_space=pltpu.SMEM)]
        + [pl.BlockSpec(memory_space=pltpu.VMEM)] * 3
        + [pl.BlockSpec(memory_space=pltpu.VMEM)] * 3
        + [pl.BlockSpec(memory_space=pltpu.VMEM)] * 2,
        out_shape=[jax.ShapeDtypeStruct(shape, dtype) for shape, dtype in shapes],
        scratch_shapes=[pltpu.VMEM((length, hidden), bf16)],
        compiler_params=pltpu.CompilerParams(vmem_limit_bytes=VMEM_LIMIT),
        cost_estimate=pl.CostEstimate(flops=8 * length * width * hidden, bytes_accessed=24 << 20, transcendentals=0),
        name="upper",
    )(me, mixed_low, tokens, cotangent, w_out, w_up, w_down, vectors, b_up[None, :])


def lower_kernel(me_ref, grad_ref, normal_ref, scale_ref, low_ref, slope_ref, mixed_ref, w_out_ref, w_up_ref, w_down_ref, vectors_ref,
                 sent_up_ref, kept_up_ref, sent_out_ref, kept_out_ref, grad_first_ref, upstream_ref, sums_ref, up_sums_ref,
                 hidden_ref):
    me = me_ref[0]
    width = grad_ref.shape[1]
    hidden = w_up_ref.shape[1]
    step = width
    rows = width // 4
    grad_first = grad_ref[...]
    grad_second = grad_first.astype(jnp.bfloat16)
    up_sums_ref[...] = jnp.zeros_like(up_sums_ref)
    for at in range(0, hidden, step):
        columns = slice(at, at + step)
        grad_hidden = dot(grad_second, w_down_ref[columns, :], NT) * slope_ref[:, columns].astype(jnp.float32)
        grad_hidden = grad_hidden.astype(jnp.bfloat16)
        hidden_ref[:, columns] = grad_hidden
        up_sums_ref[at // step : at // step + 1, :] = column_sum(grad_hidden.astype(jnp.float32))
        grad_first = grad_first + dot(grad_hidden, w_up_ref[:, columns], NT)

    def places(sent, kept):
        for distance, out in ((1, sent.at[0]), (3, sent.at[1]), (0, kept.at[0]), (2, kept.at[1])):
            place = lax.bitwise_xor(me, distance) * rows
            yield (pl.ds(pl.multiple_of(place, rows), rows), out)

    for place, out in places(sent_up_ref, kept_up_ref):
        put_rows(out, me_ref, dot(low_ref[place, :], hidden_ref[...]).astype(jnp.bfloat16))
    normal = normal_ref[...]
    grad = norm_back(normal, scale_ref[:, :1], grad_first, vectors_ref[1:2, :])
    grad_first_ref[...] = grad
    grad_branch = grad.astype(jnp.bfloat16)
    sums_ref[...] = jnp.zeros_like(sums_ref)
    sums_ref[0:1, :] = column_sum(grad_first * normal)
    sums_ref[1:2, :] = column_sum(grad_first)
    sums_ref[2:3, :] = column_sum(grad_branch.astype(jnp.float32))
    upstream_ref[...] = dot(w_out_ref[...], grad_branch, NT).astype(jnp.bfloat16)
    for place, out in places(sent_out_ref, kept_out_ref):
        put_rows(out, me_ref, dot(mixed_ref[place, :], grad_branch).astype(jnp.bfloat16))


def lower(me, grad, normal, scale, low_t, slope, mixed_low, w_out, w_up, w_down, vectors):
    length, width = grad.shape
    hidden = w_up.shape[1]
    bf16, f32 = jnp.bfloat16, jnp.float32
    shapes = [
        ((2, 2, 2, width // 16, hidden), bf16),
        ((2, 2, 2, width // 16, hidden), bf16),
        ((2, 2, 2, width // 16, width), bf16),
        ((2, 2, 2, width // 16, width), bf16),
        ((length, width), f32),
        ((width, length), bf16),
        ((8, width), f32),
        ((8, width), f32),
    ]
    return pl.pallas_call(
        lower_kernel,
        in_specs=[pl.BlockSpec(memory_space=pltpu.SMEM)]
        + [pl.BlockSpec(memory_space=pltpu.VMEM)] * 6
        + [pl.BlockSpec(memory_space=pltpu.VMEM)] * 3
        + [pl.BlockSpec(memory_space=pltpu.VMEM)],
        out_shape=[jax.ShapeDtypeStruct(shape, dtype) for shape, dtype in shapes],
        scratch_shapes=[pltpu.VMEM((length, hidden), bf16)],
        compiler_params=pltpu.CompilerParams(vmem_limit_bytes=VMEM_LIMIT),
        cost_estimate=pl.CostEstimate(flops=8 * length * width * hidden, bytes_accessed=24 << 20, transcendentals=0),
        name="lower",
    )(me, grad, normal, scale, low_t, slope, mixed_low, w_out, w_up, w_down, vectors)


def project_kernel(*refs):
    one_ref, two_ref, w_key_ref, w_value_ref, b_value_ref = refs[:5]
    keys_ref, value_ref = refs[-2:]
    keys = one_ref.shape[0]
    for number, ref in enumerate((one_ref, two_ref)):
        at = slice(number * keys, (number + 1) * keys)
        keys_ref[at, :] = dot(ref[...], w_key_ref[...]).astype(jnp.bfloat16)
        values = dot(w_value_ref[...], ref[...], (((0,), (1,)), ((), ())))
        value_ref[:, at] = (values + b_value_ref[:, :1]).astype(jnp.bfloat16)


def project(one, two, w_key, w_value, b_value, before=()):
    length, width = one.shape
    half = 1 if before else 0
    return pl.pallas_call(
        project_kernel,
        grid=(1,),
        in_specs=[
            pl.BlockSpec((length, width), lambda i: (0, 0)),
            pl.BlockSpec((length, width), lambda i: (0, 0)),
            pl.BlockSpec((width, width), lambda i: (0, 0)),
            pl.BlockSpec((width, width), lambda i: (0, 0)),
            pl.BlockSpec((width, LANES), lambda i: (0, 0)),
        ]
        + [pl.BlockSpec(memory_space=pl.ANY)] * len(before),
        out_specs=[
            pl.BlockSpec((2 * length, width), lambda i: (half, 0)),
            pl.BlockSpec((width, 2 * length), lambda i: (0, half)),
        ],
        out_shape=[
            jax.ShapeDtypeStruct((4 * length, width), jnp.bfloat16),
            jax.ShapeDtypeStruct((width, 4 * length), jnp.bfloat16),
        ],
        input_output_aliases={5: 0, 6: 1} if before else {},
        compiler_params=pltpu.CompilerParams(vmem_limit_bytes=VMEM_LIMIT),
        cost_estimate=pl.CostEstimate(flops=8 * length * width * width, bytes_accessed=6 << 20, transcendentals=0),
        name="project",
    )(one, two, w_key, w_value, b_value, *before)


def project_back_kernel(grad_key_ref, grad_value_ref, w_key_ref, w_value_ref, sent_ref, near_ref, far_ref):
    keys = near_ref.shape[0]
    for slot, out in enumerate((near_ref, sent_ref.at[:keys], far_ref, sent_ref.at[keys:])):
        at = slice(slot * keys, (slot + 1) * keys)
        total = dot(grad_key_ref[at, :], w_key_ref[...], NT) + dot(grad_value_ref[at, :], w_value_ref[...], NT)
        out[...] = total.astype(jnp.bfloat16)


def project_back(grad_keys, grad_values, w_key, w_value):
    length, width = grad_keys.shape
    sizes = (length // 2, length // 4, length // 4)
    return pl.pallas_call(
        project_back_kernel,
        out_shape=[jax.ShapeDtypeStruct((size, width), jnp.bfloat16) for size in sizes],
        compiler_params=pltpu.CompilerParams(vmem_limit_bytes=VMEM_LIMIT),
        cost_estimate=pl.CostEstimate(flops=0, bytes_accessed=0, transcendentals=0),
        name="project_back",
    )(grad_keys, grad_values, w_key, w_value)


def backward_kernel(me_ref, far_ref, order_ref, across_ref, down_ref, raised_ref, query_ref, upstream_ref, inverse_ref, mixed_ref,
                    value_ref, key_ref, rows_a, rows_b, rows_c, rows_d, upper_sums_ref, lower_sums_ref, up_sums_ref,
                    grad_query_ref, grad_key_ref, grad_value_ref, sent_ref, kept_ref,
                    sum_ref, grad_ref, count_ref, scaled_ref, dot_ref, value_sum_ref, all_pairs_ref, all_rows_ref, small_ref,
                    *, heads, scale, key_scale):
    slot = pl.program_id(0)
    keys, queries = order_ref.shape
    width = query_ref.shape[0]
    head_size = PAIR // 2
    group = 16
    per_super = 4
    supers = keys // (group * per_super)
    buckets = count_ref.shape[1] // group

    @pl.when(slot == 0)
    def _():
        sum_ref[...] = jnp.zeros_like(sum_ref)
        count_ref[...] = jnp.zeros_like(count_ref)
        value_sum_ref[...] = jnp.zeros_like(value_sum_ref)
        for index, ref in enumerate((rows_a, rows_b, rows_c, rows_d)):
            all_rows_ref[index * keys : (index + 1) * keys, :] = ref[...]
        for head in range(heads):
            feature = slice(head * head_size, (head + 1) * head_size)
            scaled = (upstream_ref[feature, :].astype(jnp.float32) * inverse_ref[feature, :]).astype(jnp.bfloat16)
            scaled_ref[feature, :] = scaled
            dot_ref[head : head + 1, :] = jnp.sum(scaled.astype(jnp.float32) * mixed_ref[feature, :], axis=0, keepdims=True)

    rows = lax.broadcasted_iota(jnp.int32, (PAIR, queries), 0)
    here = pl.ds(pl.multiple_of(slot * keys, keys), keys)
    for pair in range(heads // 2):
        at = slice(pair * PAIR, (pair + 1) * PAIR)
        query_pair = query_ref[at, :]
        mixed_pair = scaled_ref[at, :]
        zero = jnp.zeros_like(query_pair)
        query_both = [jnp.where(rows < head_size, query_pair, zero), jnp.where(rows >= head_size, query_pair, zero)]
        mixed_both = [jnp.where(rows < head_size, mixed_pair, zero), jnp.where(rows >= head_size, mixed_pair, zero)]
        query_both = jnp.concatenate(query_both, axis=1)
        mixed_both = jnp.concatenate(mixed_both, axis=1)
        grad_probs = dot(value_ref[at, :], mixed_both, TN)
        raised = jnp.concatenate([raised_ref[2 * pair], raised_ref[2 * pair + 1]], axis=1)
        dots = jnp.concatenate([dot_ref[2 * pair : 2 * pair + 1, :], dot_ref[2 * pair + 1 : 2 * pair + 2, :]], axis=1)
        grad = (raised.astype(jnp.float32) * (grad_probs - dots)).astype(jnp.bfloat16)
        grad_values = dot(raised, mixed_both, NT).astype(jnp.bfloat16)
        grad_value_ref[:, at] = grad_values
        all_pairs_ref[here, width + pair * PAIR : width + (pair + 1) * PAIR] = grad_values
        value_sum_ref[:, at] += jnp.sum(grad_values.astype(jnp.float32).reshape(keys // 8, 8, PAIR), axis=0)
        grad_keys = (dot(grad, query_both, NT) * key_scale).astype(jnp.bfloat16)
        grad_key_ref[:, at] = grad_keys
        all_pairs_ref[here, at] = grad_keys
        both = dot(key_ref[:, at], grad, TN)
        sum_ref[at.start : at.start + head_size, :] += both[:head_size, :queries]
        sum_ref[at.start + head_size : at.stop, :] += both[head_size:, queries:]
        for one in range(2):
            head = 2 * pair + one
            mine = grad[:, one * queries : (one + 1) * queries]
            for g in range(keys // group):
                lanes = slice((g % per_super) * queries, (g % per_super + 1) * queries)
                grad_ref[g // per_super, head * group : (head + 1) * group, lanes] = mine[g * group : (g + 1) * group, :]

    def add_counts(number, ref, sup, grads):
        parts = []
        for sub in range(per_super):
            at = pl.multiple_of(sup * (group * per_super) + sub * group, group)
            ids = ref[pl.ds(at, group), :]
            hot = [jnp.where(ids == b + number * buckets, 1.0, 0.0).astype(jnp.bfloat16) for b in range(buckets)]
            parts.append(jnp.concatenate(hot, axis=0))
        count_ref[number] += dot(jnp.concatenate(parts, axis=1), grads, NT)

    def tally(sup, _):
        grads = grad_ref[sup]
        add_counts(1, across_ref, sup, grads)
        add_counts(2, down_ref, sup, grads)
        far = far_ref[slot * supers + sup]

        @pl.when(far == 0)
        def _():
            add_counts(0, order_ref, sup, grads)

        @pl.when(far > 0)
        def _():
            at = pl.ds(pl.multiple_of(far * group, group), group)
            count_ref[0, at, :] += dot(jnp.ones((group, per_super * queries), jnp.bfloat16), grads, NT)

        return 0

    lax.fori_loop(0, supers, tally, 0)

    @pl.when(slot == pl.num_programs(0) - 1)
    def _():
        grad_queries = (sum_ref[...] * scale).astype(jnp.bfloat16)
        grad_query_ref[...] = grad_queries
        bias_query = dot(jnp.ones((8, queries), jnp.bfloat16), grad_queries, NT)[:1]
        sums = [upper_sums_ref[:3, :], lower_sums_ref[:3, :], column_sum(value_sum_ref[...]), bias_query]
        for number, part in enumerate((jnp.concatenate(sums, axis=0), up_sums_ref[...])):
            for at in range(0, width, LANES):
                place = (number * width + at) // LANES * 8
                small_ref[place : place + 8, :] = part[:, at : at + LANES]
        used = 2 * width // LANES * 8
        place = lax.broadcasted_iota(jnp.int32, (buckets * group, heads * group), 0) % group
        other = lax.broadcasted_iota(jnp.int32, (buckets * group, heads * group), 1) % group
        owner = lax.broadcasted_iota(jnp.int32, (heads * group, LANES), 0) // group
        column = lax.broadcasted_iota(jnp.int32, (heads * group, LANES), 1)
        gather = jnp.where(owner == column, 1.0, 0.0)
        for number in range(3):
            kept = jnp.where(place == other, count_ref[number], 0.0)
            kept = jnp.sum(kept.reshape(buckets, group, heads * group), axis=1)
            table = jnp.dot(kept, gather, preferred_element_type=jnp.float32, precision=lax.Precision.HIGHEST)
            small_ref[used + number * buckets : used + (number + 1) * buckets, :] = table
        small = small_ref[...].astype(jnp.bfloat16)
        each = width // 4
        for side in range(2):
            for out in (sent_ref, kept_ref):
                for x in range(2):
                    for a in range(2):
                        part = small[(2 * x + a) * each // 4 : (2 * x + a + 1) * each // 4, :]
                        out[side, lax.bitwise_xor(me_ref[1], x), lax.bitwise_xor(me_ref[2], a), :, 3 * width :] = part
        parts = (
            (slice(0, width), dot(rows_a[...], grad_queries, (((0,), (1,)), ((), ())))),
            (slice(width, 3 * width), dot(all_rows_ref[...], all_pairs_ref[...], TN)),
        )
        for columns, full in parts:
            full = full.astype(jnp.bfloat16)
            for quarter in range(4):
                distance = lax.bitwise_xor(me_ref[0], quarter)
                for x in range(2):
                    for a in range(2):
                        first = quarter * each + (2 * x + a) * each // 4
                        part = full[first : first + each // 4, :]
                        at_x, at_a = lax.bitwise_xor(me_ref[1], x), lax.bitwise_xor(me_ref[2], a)

                        @pl.when(distance % 2 == 1)
                        def _():
                            sent_ref[distance // 2, at_x, at_a, :, columns] = part

                        @pl.when(distance % 2 == 0)
                        def _():
                            kept_ref[distance // 2, at_x, at_a, :, columns] = part


def attention_backward(me, far, order, across, down, raised, query_t, upstream_t, inverse_t, mixed_t, value_t, keys_in, row_slots,
                       small_sums, scale, key_scale):
    width, queries = query_t.shape
    heads = raised.shape[0]
    length = keys_in.shape[0]
    slots = len(row_slots)
    keys = length // slots
    buckets = 32
    group = 16
    ids = pl.BlockSpec((keys, queries), lambda s: (s, 0))
    full = pl.BlockSpec((width, queries), lambda s: (0, 0))
    rows = pl.BlockSpec((keys, width), lambda s: (s, 0))
    last = (2, 2, 2, width // 16, 3 * width + LANES)
    return pl.pallas_call(
        functools.partial(backward_kernel, heads=heads, scale=scale, key_scale=key_scale),
        grid=(slots,),
        in_specs=[
            pl.BlockSpec(memory_space=pltpu.SMEM),
            pl.BlockSpec(memory_space=pltpu.SMEM),
            ids, ids, ids,
            pl.BlockSpec((heads, keys, queries), lambda s: (0, s, 0)),
            full, full, full, full,
            pl.BlockSpec((width, keys), lambda s: (0, s)),
            rows,
        ]
        + [pl.BlockSpec((keys, width), lambda s: (0, 0))] * slots
        + [pl.BlockSpec((8, width), lambda s: (0, 0))] * len(small_sums),
        out_specs=[full, rows, rows] + [pl.BlockSpec(last, lambda s: (0, 0, 0, 0, 0))] * 2,
        out_shape=[
            jax.ShapeDtypeStruct((width, queries), jnp.bfloat16),
            jax.ShapeDtypeStruct((length, width), jnp.bfloat16),
            jax.ShapeDtypeStruct((length, width), jnp.bfloat16),
            jax.ShapeDtypeStruct(last, jnp.bfloat16),
            jax.ShapeDtypeStruct(last, jnp.bfloat16),
        ],
        scratch_shapes=[
            pltpu.VMEM((width, queries), jnp.float32),
            pltpu.VMEM((keys // (group * 4), heads * group, 4 * queries), jnp.bfloat16),
            pltpu.VMEM((3, buckets * group, heads * group), jnp.float32),
            pltpu.VMEM((width, queries), jnp.bfloat16),
            pltpu.VMEM((16, queries), jnp.float32),
            pltpu.VMEM((8, width), jnp.float32),
            pltpu.VMEM((length, 2 * width), jnp.bfloat16),
            pltpu.VMEM((length, width), jnp.bfloat16),
            pltpu.VMEM((width // slots, LANES), jnp.float32),
        ],
        compiler_params=pltpu.CompilerParams(vmem_limit_bytes=VMEM_LIMIT),
        cost_estimate=pl.CostEstimate(flops=0, bytes_accessed=0, transcendentals=0),
        name="attention_backward",
    )(me, far, order, across, down, raised, query_t, upstream_t, inverse_t, mixed_t, value_t, keys_in, *row_slots, *small_sums)


MARK_FLOPS = 20000000000


def bucketize(offsets, limits):
    magnitude = jnp.abs(offsets)

    def pick(bits, first, size):
        if not bits:
            return limits[first + size // 2]
        half = size // 2
        return jnp.where(bits[0], pick(bits[1:], first + half + 1, half), pick(bits[1:], first, half))

    bits = []
    total = 16 * (offsets > 0).astype(jnp.int32)
    weight = (len(limits) + 1) // 2
    while weight:
        bit = magnitude >= pick(bits, 0, len(limits))
        bits.append(bit)
        total = total + jnp.where(bit, weight, 0)
        weight = weight // 2
    return total


def einsum(spec, left, right):
    return jnp.einsum(spec, left, right, preferred_element_type=jnp.float32)


def exchange(array, axis_name, distance):
    pairs = [(i, i ^ distance) for i in range(lax.axis_size(axis_name))]
    return lax.ppermute(array, axis_name, pairs)


def in_blocks(sent, kept):
    return (kept, exchange(sent, "blk", 1))


def mark_kernel(array_ref, out_ref):
    out_ref[...] = jnp.zeros_like(out_ref)


def mark_of(array, flops):
    return pl.pallas_call(
        mark_kernel,
        in_specs=[pl.BlockSpec(memory_space=pl.ANY)],
        out_specs=pl.BlockSpec(memory_space=pltpu.VMEM),
        out_shape=jax.ShapeDtypeStruct((8, LANES), jnp.float32),
        compiler_params=pltpu.CompilerParams(has_side_effects=True),
        cost_estimate=pl.CostEstimate(flops=flops, bytes_accessed=4096, transcendentals=0),
        name="mark",
    )(array)


BITS = {"y": 0, "x": 1, "a": 2}


def add_low(left, right):
    return (left.astype(jnp.float32) + right.astype(jnp.float32)).astype(jnp.bfloat16)


def reduce_rows(kept, got, order, back, sides):
    distances = {"y": ("blk", 2), "x": ("docs", 1), "a": ("docs", 2)}
    for letter in order:
        bit = BITS[letter]
        near = [lax.slice_in_dim(array, 0, 1, axis=bit) for array in (kept, got)]
        away = [lax.slice_in_dim(array, 1, 2, axis=bit) for array in (kept, got)]
        got = yield (add_low(*away), *distances[letter])
        kept = add_low(*near)
    data = add_low(kept, got)
    distance = 4
    while distance < lax.axis_size("docs"):
        got = yield (data, "docs", distance)
        data = add_low(data, got)
        distance = distance * 2
    for letter in back:
        got = yield (data, *distances[letter])
        data = jnp.concatenate([data, got], axis=BITS[letter])
    for letter in back:
        bit = BITS[letter]
        near = lax.slice_in_dim(data, 0, 1, axis=bit)
        away = lax.slice_in_dim(data, 1, 2, axis=bit)
        halves = [jnp.where(sides[letter] == 0, near, away), jnp.where(sides[letter] == 0, away, near)]
        data = jnp.concatenate(halves, axis=bit)
    return data.reshape(-1, data.shape[4])


class Line:
    def __init__(self):
        self.last = None
        self.waiting = {}
        self.steps = {}
        self.results = {}

    def after(self, *arrays):
        if self.last is None:
            return arrays
        return lax.optimization_barrier((*arrays, self.last))[:-1]

    def mark(self, array):
        self.last = array

    def send(self, name):
        array, axis_name, distance = self.waiting[name]
        self.waiting[name] = exchange(array, axis_name, distance)
        self.mark(array)

    def begin(self, name, steps, marked):
        self.steps[name] = steps
        array, axis_name, distance = next(steps)
        self.waiting[name] = exchange(array, axis_name, distance)
        self.mark(mark_of(array, 20_000_000_000) if marked else array)

    def go(self, names):
        for name in names:
            if name in self.results:
                continue
            (got,) = self.after(self.waiting[name])
            try:
                self.waiting[name] = self.steps[name].send(got)
            except StopIteration as stop:
                self.results[name] = stop.value
                continue
            self.send(name)

    def finish(self, names):
        while any(name not in self.results for name in names):
            self.go(names)


def body(
    tokens,
    box_corners,
    cotangent,
    w_query,
    b_query,
    w_key,
    w_value,
    b_value,
    w_out,
    b_out,
    gain_first,
    shift_first,
    w_up,
    b_up,
    w_down,
    b_down,
    gain_second,
    shift_second,
    table_order,
    table_horizontal,
    table_vertical,
):
    docs_here, doc_length, model_width = tokens.shape
    bucket_total, head_count = table_order.shape
    head_size = model_width // head_count
    score_scale = head_size ** (-0.5)
    blk_count = lax.axis_size("blk")
    me = lax.axis_index("blk")
    rows_in = tokens.reshape(doc_length, model_width)

    centres = jnp.stack([box_corners[0, 0] + box_corners[2, 0], box_corners[1, 0] + box_corners[3, 0]])
    centres = centres.astype(jnp.float32)
    centre_slots = [centres] + [exchange(centres, "blk", s) for s in range(1, blk_count)]
    core_rows = exchange(rows_in, "blk", 1)
    far_rows = exchange(rows_in, "blk", 2)
    row_slots = [rows_in, core_rows, far_rows, exchange(far_rows, "blk", 1)]
    centres_all = jnp.concatenate(centre_slots, axis=1).astype(jnp.int32)
    centres_own = centres.astype(jnp.int32)

    inside = jnp.arange(doc_length, dtype=jnp.int32)
    key_place = jnp.concatenate([(me ^ s) * doc_length + inside for s in range(blk_count)])
    query_place = me * doc_length + inside
    order = bucketize(key_place[:, None] - query_place[None, :], ORDER_LIMITS)
    across = bucketize(centres_all[0][:, None] - centres_own[0][None, :], BOX_LIMITS) + bucket_total
    down = bucketize(centres_all[1][:, None] - centres_own[1][None, :], BOX_LIMITS) + 2 * bucket_total
    tile = jnp.arange(LANES, dtype=jnp.int32)
    near = [bucketize(t * LANES + tile[:, None] - tile[None, :], ORDER_LIMITS) for t in range(-2, 3)]
    near = jnp.concatenate(near, axis=0)
    tiles = (key_place[::LANES, None] - query_place[None, ::LANES]) // LANES
    tiles = (jnp.clip(tiles, -2, 2) + 2) * LANES
    first_key = key_place[::64]
    beyond = jnp.where(first_key > query_place[-1], first_key - query_place[-1], query_place[0] - (first_key + 63))
    far_order = jnp.where(beyond >= ORDER_LIMITS[-1], 15 + 16 * (first_key > query_place[-1]), 0).astype(jnp.int32)
    tables = jnp.concatenate([table_order, table_horizontal, table_vertical], axis=0).T
    tables = jnp.round((tables + 5.0) * UNIT).astype(jnp.int32)
    tables = tables[0::2] + FIELD * tables[1::2]
    tables = jnp.pad(tables, ((0, 0), (0, LANES - 3 * bucket_total)))[:, None, :]

    query_t = (einsum("df,td->ft", w_query, rows_in) + b_query[:, None]).astype(jnp.bfloat16)
    query_t = query_t * jnp.bfloat16(score_scale * UNIT)
    bias_column = jnp.broadcast_to(b_value[:, None], (model_width, LANES))
    vectors_in = jnp.stack([b_out, gain_first, shift_first, b_down, gain_second, shift_second, b_out, b_out])
    projected = project(rows_in, core_rows, w_key, w_value, bias_column)
    keys, value_t = project(row_slots[2], row_slots[3], w_key, w_value, bias_column, projected)
    keys, order, vectors_in, far_order = lax.optimization_barrier((keys, order, vectors_in, far_order))
    raised, mixed_t, inverse_t, mixed_low = attention_forward(
        tiles, tables, near, across, down, query_t, keys, value_t
    )

    here = lax.axis_index("docs")
    place = jnp.stack([me, here % 2, (here // 2) % 2]).astype(jnp.int32)
    cotangents = cotangent.reshape(doc_length, model_width)
    output, grad_pre2, normal, scale, low_t, slope, sent_down, kept_down, upper_sums = upper(
        place, mixed_low, rows_in, cotangents, w_out, w_up, w_down, vectors_in, b_up
    )
    parts_down = in_blocks(sent_down, kept_down)
    sent_up, kept_up, sent_out, kept_out, grad_pre1, upstream_t, lower_sums, up_sums = lower(
        place, grad_pre2, normal, scale, low_t, slope, mixed_low, w_out, w_up, w_down, vectors_in
    )
    parts_up = in_blocks(sent_up, kept_up)
    parts_out = in_blocks(sent_out, kept_out)
    output = output.reshape(tokens.shape)

    sides = {"y": 0, "x": here % 2, "a": (here // 2) % 2}
    line = Line()
    line.mark(upstream_t)
    def begin(name, parts, order, back):
        kept, got = parts
        (got,) = line.after(got)
        line.begin(name, reduce_rows(kept, got, order, back, sides), name == "last")

    begin("down", parts_down, "axy", "xa")
    begin("up", parts_up, "xay", "ax")
    begin("out", parts_out, "yxa", "xa")
    (upstream_t,) = line.after(upstream_t)
    grad_query_t, grad_keys, grad_values, sent_last, kept_last = attention_backward(
        place, far_order, order, across, down, raised, query_t, upstream_t, inverse_t, mixed_t, value_t, keys, row_slots,
        (upper_sums, lower_sums, up_sums), score_scale, 1.0 / UNIT
    )
    parts_last = in_blocks(sent_last, kept_last)
    line.mark(sent_last)
    line.mark(mark_of(line.last, 20000000000))
    line.go(["up"])
    begin("last", parts_last, "ayx", "ax")
    line.mark(mark_of(line.last, 20000000000))
    line.go(["down", "out", "up"])
    grad_keys, grad_values = line.after(grad_keys, grad_values)
    shared_sent, shared_near, shared_far = project_back(grad_keys, grad_values, w_key, w_value)
    line.mark(shared_sent)
    near = exchange(shared_sent, "blk", 1)
    line.mark(mark_of(line.last, 5000000000))
    line.go(["up", "out", "down"])
    line.mark(mark_of(line.last, 20000000000))
    line.go(["last", "out", "down", "up"])
    line.go(["last", "out"])
    (near,) = line.after(near)
    near = near.astype(jnp.float32)
    far_sent = (shared_far.astype(jnp.float32) + near[doc_length:]).astype(jnp.bfloat16)
    line.mark(far_sent)
    far = exchange(far_sent, "blk", 2)
    line.mark(mark_of(line.last, 20000000000))
    line.go(["last", "out", "down", "up", "out"])
    line.go(["last", "down"])
    line.go(["last", "up"])
    grad_query_t, far = line.after(grad_query_t, far)
    grad_inputs = grad_pre1 + einsum("ft,df->td", grad_query_t, w_query) + shared_near.astype(jnp.float32) + near[:doc_length]
    grad_tokens = (grad_inputs + far.astype(jnp.float32)).astype(jnp.bfloat16).reshape(tokens.shape)
    line.mark(grad_tokens)
    line.go(["down", "last"])
    line.finish(["down", "last", "up", "out"])

    (grad_w_down, grad_w_up, grad_w_out) = [line.results[name].astype(jnp.float32) for name in ("down", "up", "out")]
    last = line.results["last"]
    grads = [last[:, n * model_width : (n + 1) * model_width].astype(jnp.float32) for n in range(3)]
    grad_w_query, grad_w_key, grad_w_value = grads
    flat = last[:, 3 * model_width :].astype(jnp.float32)
    tiles_each = model_width // LANES
    rows = model_width // blk_count

    def vectors(first):
        block = flat[first : first + 8 * tiles_each].reshape(tiles_each, 8, LANES)
        return jnp.transpose(block, (1, 0, 2)).reshape(8, model_width)

    each = lax.dynamic_slice_in_dim(vectors(0), me * rows, rows, 1)
    grad_b_up = lax.dynamic_slice_in_dim(vectors(8 * tiles_each), me, 1, 0)[0]
    table_rows = bucket_total // blk_count
    table_out = []
    for number in range(3):
        first = 16 * tiles_each + number * bucket_total + me * table_rows
        table_out.append(lax.dynamic_slice_in_dim(flat, first, table_rows, 0)[:, :head_count])
    small_out = [each[7], each[6], each[5], each[3], each[4], grad_b_up, each[2], each[0], each[1], *table_out]
    return (
        output,
        grad_tokens,
        grad_w_query,
        small_out[0],
        grad_w_key,
        grad_w_value,
        small_out[1],
        grad_w_out,
        small_out[2],
        small_out[3],
        small_out[4],
        grad_w_up,
        small_out[5],
        grad_w_down,
        small_out[6],
        small_out[7],
        small_out[8],
        small_out[9],
        small_out[10],
        small_out[11],
    )


def solution(mesh):
    return jax.shard_map(
        body,
        mesh=mesh,
        in_specs=(
            P("docs", "blk", None),
            P(None, "docs", "blk"),
            P("docs", "blk", None),
            P(),
            P(),
            P(),
            P(),
            P(),
            P(),
            P(),
            P(),
            P(),
            P(),
            P(),
            P(),
            P(),
            P(),
            P(),
            P(),
            P(),
            P(),
        ),
        out_specs=(
            P("docs", "blk", None),
            P("docs", "blk", None),
            P("blk", None),
            P("blk"),
            P("blk", None),
            P("blk", None),
            P("blk"),
            P("blk", None),
            P("blk"),
            P("blk"),
            P("blk"),
            P("blk", None),
            P("blk"),
            P("blk", None),
            P("blk"),
            P("blk"),
            P("blk"),
            P("blk", None),
            P("blk", None),
            P("blk", None),
        ),
        check_vma=False,
    )
```

```python
import functools
import math

import jax
import jax.numpy as jnp
from jax import lax
from jax.experimental import pallas as pl
from jax.experimental.pallas import tpu as pltpu
from jax.sharding import PartitionSpec as P

ORDER_LIMITS = (1, 2, 3, 4, 5, 6, 7, 8, 12, 16, 23, 32, 45, 64, 91)
BOX_LIMITS = (2, 4, 6, 8, 12, 16, 24, 32, 48, 64, 96, 128, 192, 256, 384)
EPSILON = 1e-05
LANES = 128
PAIR = 128
VMEM_LIMIT = 60 * 1024 * 1024
FIELD = 65536
LOG2E = 1.4426950408889634
UNIT = 2048.0

def forward_kernel(tile_ref, table_ref, near_ref, across_ref, down_ref, query_ref, key_ref, value_ref,
                   raised_ref, mixed_ref, inverse_ref, mixed_low_ref, score_ref, order_ref, value_sums_ref):
    keys, queries = across_ref.shape
    head_size = PAIR // 2
    rows = lax.broadcasted_iota(jnp.int32, (PAIR, queries), 0)
    query_pair = query_ref[...]
    zero = jnp.zeros_like(query_pair)
    both = jnp.concatenate(
        [jnp.where(rows < head_size, query_pair, zero), jnp.where(rows >= head_size, query_pair, zero)], axis=1
    )
    step = 16
    numbers = lax.GatherDimensionNumbers(
        offset_dims=(), collapsed_slice_dims=(1,), start_index_map=(1,),
        operand_batching_dims=(0,), start_indices_batching_dims=(0,),
    )

    def pick(places):
        table = jnp.broadcast_to(table_ref[0], places.shape)
        return lax.gather(table, places[..., None], numbers, (1, 1), mode=lax.GatherScatterMode.PROMISE_IN_BOUNDS)

    for at in range(0, near_ref.shape[0], step):
        order_ref[at : at + step, :] = pick(near_ref[at : at + step, :])
    value_sums_ref[0, :head_size, :] = value_ref[:head_size, :]
    value_sums_ref[1, :head_size, :] = value_ref[head_size:, :]
    value_sums_ref[:, head_size:, :] = jnp.ones((2, 16, keys), jnp.bfloat16)

    peaks = [jnp.full((8, LANES), -jnp.inf, jnp.float32) for _ in range(2 * queries // LANES)]
    for at in range(0, keys, step):
        raw = jnp.dot(key_ref[at : at + step, :], both, preferred_element_type=jnp.float32)
        for lane in range(0, queries, LANES):
            lanes = slice(lane, lane + LANES)
            start = pl.multiple_of(tile_ref[at // LANES, lane // LANES] + at % LANES, step)
            code = order_ref[pl.ds(start, step), :]
            code = code + pick(across_ref[at : at + step, lanes]) + pick(down_ref[at : at + step, lanes])
            for head, field in enumerate((lax.bitwise_and(code, FIELD - 1), lax.shift_right_logical(code, 16))):
                place = head * queries + lane
                score = raw[:, place : place + LANES] + field.astype(jnp.float32)
                score_ref[at : at + step, place : place + LANES] = score
                peaks[place // LANES] = jnp.maximum(peaks[place // LANES], jnp.max(score.reshape(step // 8, 8, LANES), axis=0))
    peak = jnp.max(jnp.concatenate(peaks, axis=1), axis=0, keepdims=True)
    for head in range(2):
        lanes = slice(head * queries, (head + 1) * queries)
        for at in range(0, keys, step):
            raised = jnp.exp2((score_ref[at : at + step, lanes] - peak[:, lanes]) * (LOG2E / UNIT)).astype(jnp.bfloat16)
            raised_ref[head, at : at + step, :] = raised
        sums = jnp.dot(value_sums_ref[head], raised_ref[head], preferred_element_type=jnp.float32)
        inverse = 1.0 / sums[head_size : head_size + 1, :]
        mixed = sums[:head_size, :] * inverse
        mixed_ref[head * head_size : (head + 1) * head_size, :] = mixed
        mixed_low_ref[head * head_size : (head + 1) * head_size, :] = mixed.astype(jnp.bfloat16)
        inverse_ref[head * head_size : (head + 1) * head_size, :] = jnp.broadcast_to(inverse, (head_size, queries))


def attention_forward(tiles, tables, near, across, down, query_t, keys, value_t):
    width, queries = query_t.shape
    length = keys.shape[0]
    pairs = width // PAIR
    whole = pl.BlockSpec((length, queries), lambda p: (0, 0))
    return pl.pallas_call(
        forward_kernel,
        grid=(pairs,),
        in_specs=[
            pl.BlockSpec(memory_space=pltpu.SMEM),
            pl.BlockSpec((1, 1, LANES), lambda p: (p, 0, 0)),
            pl.BlockSpec(near.shape, lambda p: (0, 0)),
            whole, whole,
            pl.BlockSpec((PAIR, queries), lambda p: (p, 0)),
            pl.BlockSpec((length, PAIR), lambda p: (0, p)),
            pl.BlockSpec((PAIR, length), lambda p: (p, 0)),
        ],
        out_specs=[
            pl.BlockSpec((2, length, queries), lambda p: (p, 0, 0)),
            pl.BlockSpec((PAIR, queries), lambda p: (p, 0)),
            pl.BlockSpec((PAIR, queries), lambda p: (p, 0)),
            pl.BlockSpec((PAIR, queries), lambda p: (p, 0)),
        ],
        out_shape=[
            jax.ShapeDtypeStruct((2 * pairs, length, queries), jnp.bfloat16),
            jax.ShapeDtypeStruct((width, queries), jnp.float32),
            jax.ShapeDtypeStruct((width, queries), jnp.float32),
            jax.ShapeDtypeStruct((width, queries), jnp.bfloat16),
        ],
        scratch_shapes=[
            pltpu.VMEM((length, 2 * queries), jnp.float32),
            pltpu.VMEM(near.shape, jnp.int32),
            pltpu.VMEM((2, PAIR // 2 + 16, length), jnp.bfloat16),
        ],
        compiler_params=pltpu.CompilerParams(vmem_limit_bytes=VMEM_LIMIT),
        cost_estimate=pl.CostEstimate(flops=4 * width * queries * length, bytes_accessed=16 << 20, transcendentals=0),
        name="attention_forward",
    )(tiles, tables, near, across, down, query_t, keys, value_t)


ERF_P = 0.3275911
ERF_A = (0.254829592, -0.284496736, 1.421413741, -1.453152027, 1.061405429)
TN = (((0,), (0,)), ((), ()))
NT = (((1,), (1,)), ((), ()))


def dot(left, right, numbers=(((1,), (0,)), ((), ()))):
    return lax.dot_general(left, right, numbers, preferred_element_type=jnp.float32)


def gelu_and_slope(values):
    size = jnp.abs(values) * (0.5**0.5)
    near = 1.0 / (1.0 + ERF_P * size)
    series = ERF_A[4]
    for term in ERF_A[3::-1]:
        series = series * near + term
    bell = jnp.exp(-(size * size))
    tail = 0.5 * (series * near) * bell
    share = jnp.where(values >= 0, 1.0 - tail, tail)
    return (values * share, share + values * bell * (0.5 / math.pi) ** 0.5)


def normalized(values):
    centred = values - jnp.mean(values, axis=1, keepdims=True)
    scale = lax.rsqrt(jnp.mean(centred * centred, axis=1, keepdims=True) + EPSILON)
    return (centred * scale, scale)


def norm_back(normal, scale, grad, gain):
    scaled = grad * gain
    inner = jnp.mean(scaled * normal, axis=1, keepdims=True)
    return scale * (scaled - jnp.mean(scaled, axis=1, keepdims=True) - normal * inner)


def column_sum(values):
    return jnp.sum(values, axis=0, keepdims=True)


def put_rows(out, me_ref, full):
    rows = full.shape[0] // 4
    for x in range(2):
        for a in range(2):
            part = full[(2 * x + a) * rows : (2 * x + a + 1) * rows, :]
            out[lax.bitwise_xor(me_ref[1], x), lax.bitwise_xor(me_ref[2], a), :, : full.shape[1]] = part


def upper_kernel(me_ref, mixed_ref, tokens_ref, cotangent_ref, w_out_ref, w_up_ref, w_down_ref, vectors_ref, b_up_ref,
                 output_ref, grad_ref, normal_ref, scale_ref, low_ref, slope_ref, sent_ref, kept_ref, sums_ref,
                 active_ref):
    me = me_ref[0]
    width = tokens_ref.shape[1]
    hidden = w_up_ref.shape[1]
    step = width
    b_out, gain_first, shift_first, b_down, gain_second, shift_second = [vectors_ref[n : n + 1, :] for n in range(6)]
    branch = dot(mixed_ref[...], w_out_ref[...], TN) + b_out
    normal, scale = normalized(tokens_ref[...].astype(jnp.float32) + branch)
    normal_ref[...] = normal
    scale_ref[...] = jnp.broadcast_to(scale, scale_ref.shape)
    first_norm = normal * gain_first + shift_first
    first_low = first_norm.astype(jnp.bfloat16)
    low_ref[...] = first_low.T
    second = first_norm + b_down
    for at in range(0, hidden, step):
        columns = slice(at, at + step)
        active, slope = gelu_and_slope(dot(first_low, w_up_ref[:, columns]) + b_up_ref[:, columns])
        slope_ref[:, columns] = slope.astype(jnp.bfloat16)
        active = active.astype(jnp.bfloat16)
        active_ref[:, columns] = active
        second = second + dot(active, w_down_ref[columns, :])
    normal, scale = normalized(second)
    output_ref[...] = (normal * gain_second + shift_second).astype(jnp.bfloat16)
    upstream = cotangent_ref[...].astype(jnp.float32)
    grad = norm_back(normal, scale, upstream, gain_second)
    grad_ref[...] = grad
    grad_second = grad.astype(jnp.bfloat16)
    sums_ref[...] = jnp.zeros_like(sums_ref)
    sums_ref[0:1, :] = column_sum(upstream * normal)
    sums_ref[1:2, :] = column_sum(upstream)
    sums_ref[2:3, :] = column_sum(grad_second.astype(jnp.float32))
    rows = hidden // 4
    for distance, out in ((1, sent_ref.at[0]), (3, sent_ref.at[1]), (0, kept_ref.at[0]), (2, kept_ref.at[1])):
        place = pl.multiple_of(lax.bitwise_xor(me, distance) * rows, LANES)
        put_rows(out, me_ref, dot(active_ref[:, pl.ds(place, rows)], grad_second, TN).astype(jnp.bfloat16))


def upper(me, mixed_low, tokens, cotangent, w_out, w_up, w_down, vectors, b_up):
    length, width = tokens.shape
    hidden = w_up.shape[1]
    bf16, f32 = jnp.bfloat16, jnp.float32
    shapes = [
        ((length, width), bf16),
        ((length, width), f32),
        ((length, width), f32),
        ((length, LANES), f32),
        ((width, length), bf16),
        ((length, hidden), bf16),
        ((2, 2, 2, hidden // 16, width), bf16),
        ((2, 2, 2, hidden // 16, width), bf16),
        ((8, width), f32),
    ]
    return pl.pallas_call(
        upper_kernel,
        in_specs=[pl.BlockSpec(memory_space=pltpu.SMEM)]
        + [pl.BlockSpec(memory_space=pltpu.VMEM)] * 3
        + [pl.BlockSpec(memory_space=pltpu.VMEM)] * 3
        + [pl.BlockSpec(memory_space=pltpu.VMEM)] * 2,
        out_shape=[jax.ShapeDtypeStruct(shape, dtype) for shape, dtype in shapes],
        scratch_shapes=[pltpu.VMEM((length, hidden), bf16)],
        compiler_params=pltpu.CompilerParams(vmem_limit_bytes=VMEM_LIMIT),
        cost_estimate=pl.CostEstimate(flops=8 * length * width * hidden, bytes_accessed=24 << 20, transcendentals=0),
        name="upper",
    )(me, mixed_low, tokens, cotangent, w_out, w_up, w_down, vectors, b_up[None, :])


def lower_kernel(me_ref, grad_ref, normal_ref, scale_ref, low_ref, slope_ref, mixed_ref, w_out_ref, w_up_ref, w_down_ref, vectors_ref,
                 sent_up_ref, kept_up_ref, sent_out_ref, kept_out_ref, grad_first_ref, upstream_ref, sums_ref, up_sums_ref,
                 hidden_ref):
    me = me_ref[0]
    width = grad_ref.shape[1]
    hidden = w_up_ref.shape[1]
    step = width
    rows = width // 4
    grad_first = grad_ref[...]
    grad_second = grad_first.astype(jnp.bfloat16)
    up_sums_ref[...] = jnp.zeros_like(up_sums_ref)
    for at in range(0, hidden, step):
        columns = slice(at, at + step)
        grad_hidden = dot(grad_second, w_down_ref[columns, :], NT) * slope_ref[:, columns].astype(jnp.float32)
        grad_hidden = grad_hidden.astype(jnp.bfloat16)
        hidden_ref[:, columns] = grad_hidden
        up_sums_ref[at // step : at // step + 1, :] = column_sum(grad_hidden.astype(jnp.float32))
        grad_first = grad_first + dot(grad_hidden, w_up_ref[:, columns], NT)

    def places(sent, kept):
        for distance, out in ((1, sent.at[0]), (3, sent.at[1]), (0, kept.at[0]), (2, kept.at[1])):
            place = lax.bitwise_xor(me, distance) * rows
            yield (pl.ds(pl.multiple_of(place, rows), rows), out)

    for place, out in places(sent_up_ref, kept_up_ref):
        put_rows(out, me_ref, dot(low_ref[place, :], hidden_ref[...]).astype(jnp.bfloat16))
    normal = normal_ref[...]
    grad = norm_back(normal, scale_ref[:, :1], grad_first, vectors_ref[1:2, :])
    grad_first_ref[...] = grad
    grad_branch = grad.astype(jnp.bfloat16)
    sums_ref[...] = jnp.zeros_like(sums_ref)
    sums_ref[0:1, :] = column_sum(grad_first * normal)
    sums_ref[1:2, :] = column_sum(grad_first)
    sums_ref[2:3, :] = column_sum(grad_branch.astype(jnp.float32))
    upstream_ref[...] = dot(w_out_ref[...], grad_branch, NT).astype(jnp.bfloat16)
    for place, out in places(sent_out_ref, kept_out_ref):
        put_rows(out, me_ref, dot(mixed_ref[place, :], grad_branch).astype(jnp.bfloat16))


def lower(me, grad, normal, scale, low_t, slope, mixed_low, w_out, w_up, w_down, vectors):
    length, width = grad.shape
    hidden = w_up.shape[1]
    bf16, f32 = jnp.bfloat16, jnp.float32
    shapes = [
        ((2, 2, 2, width // 16, hidden), bf16),
        ((2, 2, 2, width // 16, hidden), bf16),
        ((2, 2, 2, width // 16, width), bf16),
        ((2, 2, 2, width // 16, width), bf16),
        ((length, width), f32),
        ((width, length), bf16),
        ((8, width), f32),
        ((8, width), f32),
    ]
    return pl.pallas_call(
        lower_kernel,
        in_specs=[pl.BlockSpec(memory_space=pltpu.SMEM)]
        + [pl.BlockSpec(memory_space=pltpu.VMEM)] * 6
        + [pl.BlockSpec(memory_space=pltpu.VMEM)] * 3
        + [pl.BlockSpec(memory_space=pltpu.VMEM)],
        out_shape=[jax.ShapeDtypeStruct(shape, dtype) for shape, dtype in shapes],
        scratch_shapes=[pltpu.VMEM((length, hidden), bf16)],
        compiler_params=pltpu.CompilerParams(vmem_limit_bytes=VMEM_LIMIT),
        cost_estimate=pl.CostEstimate(flops=8 * length * width * hidden, bytes_accessed=24 << 20, transcendentals=0),
        name="lower",
    )(me, grad, normal, scale, low_t, slope, mixed_low, w_out, w_up, w_down, vectors)


def project_kernel(*refs):
    one_ref, two_ref, w_key_ref, w_value_ref, b_value_ref = refs[:5]
    keys_ref, value_ref = refs[-2:]
    keys = one_ref.shape[0]
    for number, ref in enumerate((one_ref, two_ref)):
        at = slice(number * keys, (number + 1) * keys)
        keys_ref[at, :] = dot(ref[...], w_key_ref[...]).astype(jnp.bfloat16)
        values = dot(w_value_ref[...], ref[...], (((0,), (1,)), ((), ())))
        value_ref[:, at] = (values + b_value_ref[:, :1]).astype(jnp.bfloat16)


def project(one, two, w_key, w_value, b_value, before=()):
    length, width = one.shape
    half = 1 if before else 0
    return pl.pallas_call(
        project_kernel,
        grid=(1,),
        in_specs=[
            pl.BlockSpec((length, width), lambda i: (0, 0)),
            pl.BlockSpec((length, width), lambda i: (0, 0)),
            pl.BlockSpec((width, width), lambda i: (0, 0)),
            pl.BlockSpec((width, width), lambda i: (0, 0)),
            pl.BlockSpec((width, LANES), lambda i: (0, 0)),
        ]
        + [pl.BlockSpec(memory_space=pl.ANY)] * len(before),
        out_specs=[
            pl.BlockSpec((2 * length, width), lambda i: (half, 0)),
            pl.BlockSpec((width, 2 * length), lambda i: (0, half)),
        ],
        out_shape=[
            jax.ShapeDtypeStruct((4 * length, width), jnp.bfloat16),
            jax.ShapeDtypeStruct((width, 4 * length), jnp.bfloat16),
        ],
        input_output_aliases={5: 0, 6: 1} if before else {},
        compiler_params=pltpu.CompilerParams(vmem_limit_bytes=VMEM_LIMIT),
        cost_estimate=pl.CostEstimate(flops=8 * length * width * width, bytes_accessed=6 << 20, transcendentals=0),
        name="project",
    )(one, two, w_key, w_value, b_value, *before)


def project_back_kernel(grad_key_ref, grad_value_ref, w_key_ref, w_value_ref, sent_ref, near_ref, far_ref):
    keys = near_ref.shape[0]
    for slot, out in enumerate((near_ref, sent_ref.at[:keys], far_ref, sent_ref.at[keys:])):
        at = slice(slot * keys, (slot + 1) * keys)
        total = dot(grad_key_ref[at, :], w_key_ref[...], NT) + dot(grad_value_ref[at, :], w_value_ref[...], NT)
        out[...] = total.astype(jnp.bfloat16)


def project_back(grad_keys, grad_values, w_key, w_value):
    length, width = grad_keys.shape
    sizes = (length // 2, length // 4, length // 4)
    return pl.pallas_call(
        project_back_kernel,
        out_shape=[jax.ShapeDtypeStruct((size, width), jnp.bfloat16) for size in sizes],
        compiler_params=pltpu.CompilerParams(vmem_limit_bytes=VMEM_LIMIT),
        cost_estimate=pl.CostEstimate(flops=0, bytes_accessed=0, transcendentals=0),
        name="project_back",
    )(grad_keys, grad_values, w_key, w_value)


def backward_kernel(me_ref, far_ref, order_ref, across_ref, down_ref, raised_ref, query_ref, upstream_ref, inverse_ref, mixed_ref,
                    value_ref, key_ref, rows_a, rows_b, rows_c, rows_d, upper_sums_ref, lower_sums_ref, up_sums_ref,
                    grad_query_ref, grad_key_ref, grad_value_ref, sent_ref, kept_ref,
                    sum_ref, grad_ref, count_ref, scaled_ref, dot_ref, value_sum_ref, all_pairs_ref, all_rows_ref, small_ref,
                    *, heads, scale, key_scale):
    slot = pl.program_id(0)
    keys, queries = order_ref.shape
    width = query_ref.shape[0]
    head_size = PAIR // 2
    group = 16
    per_super = 4
    supers = keys // (group * per_super)
    buckets = count_ref.shape[1] // group

    @pl.when(slot == 0)
    def _():
        sum_ref[...] = jnp.zeros_like(sum_ref)
        count_ref[...] = jnp.zeros_like(count_ref)
        value_sum_ref[...] = jnp.zeros_like(value_sum_ref)
        for index, ref in enumerate((rows_a, rows_b, rows_c, rows_d)):
            all_rows_ref[index * keys : (index + 1) * keys, :] = ref[...]
        for head in range(heads):
            feature = slice(head * head_size, (head + 1) * head_size)
            scaled = (upstream_ref[feature, :].astype(jnp.float32) * inverse_ref[feature, :]).astype(jnp.bfloat16)
            scaled_ref[feature, :] = scaled
            dot_ref[head : head + 1, :] = jnp.sum(scaled.astype(jnp.float32) * mixed_ref[feature, :], axis=0, keepdims=True)

    rows = lax.broadcasted_iota(jnp.int32, (PAIR, queries), 0)
    here = pl.ds(pl.multiple_of(slot * keys, keys), keys)
    for pair in range(heads // 2):
        at = slice(pair * PAIR, (pair + 1) * PAIR)
        query_pair = query_ref[at, :]
        mixed_pair = scaled_ref[at, :]
        zero = jnp.zeros_like(query_pair)
        query_both = [jnp.where(rows < head_size, query_pair, zero), jnp.where(rows >= head_size, query_pair, zero)]
        mixed_both = [jnp.where(rows < head_size, mixed_pair, zero), jnp.where(rows >= head_size, mixed_pair, zero)]
        query_both = jnp.concatenate(query_both, axis=1)
        mixed_both = jnp.concatenate(mixed_both, axis=1)
        grad_probs = dot(value_ref[at, :], mixed_both, TN)
        raised = jnp.concatenate([raised_ref[2 * pair], raised_ref[2 * pair + 1]], axis=1)
        dots = jnp.concatenate([dot_ref[2 * pair : 2 * pair + 1, :], dot_ref[2 * pair + 1 : 2 * pair + 2, :]], axis=1)
        grad = (raised.astype(jnp.float32) * (grad_probs - dots)).astype(jnp.bfloat16)
        grad_values = dot(raised, mixed_both, NT).astype(jnp.bfloat16)
        grad_value_ref[:, at] = grad_values
        all_pairs_ref[here, width + pair * PAIR : width + (pair + 1) * PAIR] = grad_values
        value_sum_ref[:, at] += jnp.sum(grad_values.astype(jnp.float32).reshape(keys // 8, 8, PAIR), axis=0)
        grad_keys = (dot(grad, query_both, NT) * key_scale).astype(jnp.bfloat16)
        grad_key_ref[:, at] = grad_keys
        all_pairs_ref[here, at] = grad_keys
        both = dot(key_ref[:, at], grad, TN)
        sum_ref[at.start : at.start + head_size, :] += both[:head_size, :queries]
        sum_ref[at.start + head_size : at.stop, :] += both[head_size:, queries:]
        for one in range(2):
            head = 2 * pair + one
            mine = grad[:, one * queries : (one + 1) * queries]
            for g in range(keys // group):
                lanes = slice((g % per_super) * queries, (g % per_super + 1) * queries)
                grad_ref[g // per_super, head * group : (head + 1) * group, lanes] = mine[g * group : (g + 1) * group, :]

    def add_counts(number, ref, sup, grads):
        parts = []
        for sub in range(per_super):
            at = pl.multiple_of(sup * (group * per_super) + sub * group, group)
            ids = ref[pl.ds(at, group), :]
            hot = [jnp.where(ids == b + number * buckets, 1.0, 0.0).astype(jnp.bfloat16) for b in range(buckets)]
            parts.append(jnp.concatenate(hot, axis=0))
        count_ref[number] += dot(jnp.concatenate(parts, axis=1), grads, NT)

    def tally(sup, _):
        grads = grad_ref[sup]
        add_counts(1, across_ref, sup, grads)
        add_counts(2, down_ref, sup, grads)
        far = far_ref[slot * supers + sup]

        @pl.when(far == 0)
        def _():
            add_counts(0, order_ref, sup, grads)

        @pl.when(far > 0)
        def _():
            at = pl.ds(pl.multiple_of(far * group, group), group)
            count_ref[0, at, :] += dot(jnp.ones((group, per_super * queries), jnp.bfloat16), grads, NT)

        return 0

    lax.fori_loop(0, supers, tally, 0)

    @pl.when(slot == pl.num_programs(0) - 1)
    def _():
        grad_queries = (sum_ref[...] * scale).astype(jnp.bfloat16)
        grad_query_ref[...] = grad_queries
        bias_query = dot(jnp.ones((8, queries), jnp.bfloat16), grad_queries, NT)[:1]
        sums = [upper_sums_ref[:3, :], lower_sums_ref[:3, :], column_sum(value_sum_ref[...]), bias_query]
        for number, part in enumerate((jnp.concatenate(sums, axis=0), up_sums_ref[...])):
            for at in range(0, width, LANES):
                place = (number * width + at) // LANES * 8
                small_ref[place : place + 8, :] = part[:, at : at + LANES]
        used = 2 * width // LANES * 8
        place = lax.broadcasted_iota(jnp.int32, (buckets * group, heads * group), 0) % group
        other = lax.broadcasted_iota(jnp.int32, (buckets * group, heads * group), 1) % group
        owner = lax.broadcasted_iota(jnp.int32, (heads * group, LANES), 0) // group
        column = lax.broadcasted_iota(jnp.int32, (heads * group, LANES), 1)
        gather = jnp.where(owner == column, 1.0, 0.0)
        for number in range(3):
            kept = jnp.where(place == other, count_ref[number], 0.0)
            kept = jnp.sum(kept.reshape(buckets, group, heads * group), axis=1)
            table = jnp.dot(kept, gather, preferred_element_type=jnp.float32, precision=lax.Precision.HIGHEST)
            small_ref[used + number * buckets : used + (number + 1) * buckets, :] = table
        small = small_ref[...].astype(jnp.bfloat16)
        each = width // 4
        for side in range(2):
            for out in (sent_ref, kept_ref):
                for x in range(2):
                    for a in range(2):
                        part = small[(2 * x + a) * each // 4 : (2 * x + a + 1) * each // 4, :]
                        out[side, lax.bitwise_xor(me_ref[1], x), lax.bitwise_xor(me_ref[2], a), :, 3 * width :] = part
        parts = (
            (slice(0, width), dot(rows_a[...], grad_queries, (((0,), (1,)), ((), ())))),
            (slice(width, 3 * width), dot(all_rows_ref[...], all_pairs_ref[...], TN)),
        )
        for columns, full in parts:
            full = full.astype(jnp.bfloat16)
            for quarter in range(4):
                distance = lax.bitwise_xor(me_ref[0], quarter)
                for x in range(2):
                    for a in range(2):
                        first = quarter * each + (2 * x + a) * each // 4
                        part = full[first : first + each // 4, :]
                        at_x, at_a = lax.bitwise_xor(me_ref[1], x), lax.bitwise_xor(me_ref[2], a)

                        @pl.when(distance % 2 == 1)
                        def _():
                            sent_ref[distance // 2, at_x, at_a, :, columns] = part

                        @pl.when(distance % 2 == 0)
                        def _():
                            kept_ref[distance // 2, at_x, at_a, :, columns] = part


def attention_backward(me, far, order, across, down, raised, query_t, upstream_t, inverse_t, mixed_t, value_t, keys_in, row_slots,
                       small_sums, scale, key_scale):
    width, queries = query_t.shape
    heads = raised.shape[0]
    length = keys_in.shape[0]
    slots = len(row_slots)
    keys = length // slots
    buckets = 32
    group = 16
    ids = pl.BlockSpec((keys, queries), lambda s: (s, 0))
    full = pl.BlockSpec((width, queries), lambda s: (0, 0))
    rows = pl.BlockSpec((keys, width), lambda s: (s, 0))
    last = (2, 2, 2, width // 16, 3 * width + LANES)
    return pl.pallas_call(
        functools.partial(backward_kernel, heads=heads, scale=scale, key_scale=key_scale),
        grid=(slots,),
        in_specs=[
            pl.BlockSpec(memory_space=pltpu.SMEM),
            pl.BlockSpec(memory_space=pltpu.SMEM),
            ids, ids, ids,
            pl.BlockSpec((heads, keys, queries), lambda s: (0, s, 0)),
            full, full, full, full,
            pl.BlockSpec((width, keys), lambda s: (0, s)),
            rows,
        ]
        + [pl.BlockSpec((keys, width), lambda s: (0, 0))] * slots
        + [pl.BlockSpec((8, width), lambda s: (0, 0))] * len(small_sums),
        out_specs=[full, rows, rows] + [pl.BlockSpec(last, lambda s: (0, 0, 0, 0, 0))] * 2,
        out_shape=[
            jax.ShapeDtypeStruct((width, queries), jnp.bfloat16),
            jax.ShapeDtypeStruct((length, width), jnp.bfloat16),
            jax.ShapeDtypeStruct((length, width), jnp.bfloat16),
            jax.ShapeDtypeStruct(last, jnp.bfloat16),
            jax.ShapeDtypeStruct(last, jnp.bfloat16),
        ],
        scratch_shapes=[
            pltpu.VMEM((width, queries), jnp.float32),
            pltpu.VMEM((keys // (group * 4), heads * group, 4 * queries), jnp.bfloat16),
            pltpu.VMEM((3, buckets * group, heads * group), jnp.float32),
            pltpu.VMEM((width, queries), jnp.bfloat16),
            pltpu.VMEM((16, queries), jnp.float32),
            pltpu.VMEM((8, width), jnp.float32),
            pltpu.VMEM((length, 2 * width), jnp.bfloat16),
            pltpu.VMEM((length, width), jnp.bfloat16),
            pltpu.VMEM((width // slots, LANES), jnp.float32),
        ],
        compiler_params=pltpu.CompilerParams(vmem_limit_bytes=VMEM_LIMIT),
        cost_estimate=pl.CostEstimate(flops=0, bytes_accessed=0, transcendentals=0),
        name="attention_backward",
    )(me, far, order, across, down, raised, query_t, upstream_t, inverse_t, mixed_t, value_t, keys_in, *row_slots, *small_sums)


MARK_FLOPS = 20000000000


def bucketize(offsets, limits):
    magnitude = jnp.abs(offsets)

    def pick(bits, first, size):
        if not bits:
            return limits[first + size // 2]
        half = size // 2
        return jnp.where(bits[0], pick(bits[1:], first + half + 1, half), pick(bits[1:], first, half))

    bits = []
    total = 16 * (offsets > 0).astype(jnp.int32)
    weight = (len(limits) + 1) // 2
    while weight:
        bit = magnitude >= pick(bits, 0, len(limits))
        bits.append(bit)
        total = total + jnp.where(bit, weight, 0)
        weight = weight // 2
    return total


def einsum(spec, left, right):
    return jnp.einsum(spec, left, right, preferred_element_type=jnp.float32)


def exchange(array, axis_name, distance):
    pairs = [(i, i ^ distance) for i in range(lax.axis_size(axis_name))]
    return lax.ppermute(array, axis_name, pairs)


def in_blocks(sent, kept):
    return (kept, exchange(sent, "blk", 1))


def mark_kernel(array_ref, out_ref):
    out_ref[...] = jnp.zeros_like(out_ref)


def mark_of(array, flops):
    return pl.pallas_call(
        mark_kernel,
        in_specs=[pl.BlockSpec(memory_space=pl.ANY)],
        out_specs=pl.BlockSpec(memory_space=pltpu.VMEM),
        out_shape=jax.ShapeDtypeStruct((8, LANES), jnp.float32),
        compiler_params=pltpu.CompilerParams(has_side_effects=True),
        cost_estimate=pl.CostEstimate(flops=flops, bytes_accessed=4096, transcendentals=0),
        name="mark",
    )(array)


BITS = {"y": 0, "x": 1, "a": 2}


def add_low(left, right):
    return (left.astype(jnp.float32) + right.astype(jnp.float32)).astype(jnp.bfloat16)


def reduce_rows(kept, got, order, back, sides):
    distances = {"y": ("blk", 2), "x": ("docs", 1), "a": ("docs", 2)}
    for letter in order:
        bit = BITS[letter]
        near = [lax.slice_in_dim(array, 0, 1, axis=bit) for array in (kept, got)]
        away = [lax.slice_in_dim(array, 1, 2, axis=bit) for array in (kept, got)]
        got = yield (add_low(*away), *distances[letter])
        kept = add_low(*near)
    data = add_low(kept, got)
    distance = 4
    while distance < lax.axis_size("docs"):
        got = yield (data, "docs", distance)
        data = add_low(data, got)
        distance = distance * 2
    for letter in back:
        got = yield (data, *distances[letter])
        data = jnp.concatenate([data, got], axis=BITS[letter])
    for letter in back:
        bit = BITS[letter]
        near = lax.slice_in_dim(data, 0, 1, axis=bit)
        away = lax.slice_in_dim(data, 1, 2, axis=bit)
        halves = [jnp.where(sides[letter] == 0, near, away), jnp.where(sides[letter] == 0, away, near)]
        data = jnp.concatenate(halves, axis=bit)
    return data.reshape(-1, data.shape[4])


class Line:
    def __init__(self):
        self.last = None
        self.waiting = {}
        self.steps = {}
        self.results = {}

    def after(self, *arrays):
        if self.last is None:
            return arrays
        return lax.optimization_barrier((*arrays, self.last))[:-1]

    def mark(self, array):
        self.last = array

    def send(self, name):
        array, axis_name, distance = self.waiting[name]
        self.waiting[name] = exchange(array, axis_name, distance)
        self.mark(array)

    def begin(self, name, steps, marked):
        self.steps[name] = steps
        array, axis_name, distance = next(steps)
        self.waiting[name] = exchange(array, axis_name, distance)
        self.mark(mark_of(array, 20_000_000_000) if marked else array)

    def go(self, names):
        for name in names:
            if name in self.results:
                continue
            (got,) = self.after(self.waiting[name])
            try:
                self.waiting[name] = self.steps[name].send(got)
            except StopIteration as stop:
                self.results[name] = stop.value
                continue
            self.send(name)

    def finish(self, names):
        while any(name not in self.results for name in names):
            self.go(names)


def body(
    tokens,
    box_corners,
    cotangent,
    w_query,
    b_query,
    w_key,
    w_value,
    b_value,
    w_out,
    b_out,
    gain_first,
    shift_first,
    w_up,
    b_up,
    w_down,
    b_down,
    gain_second,
    shift_second,
    table_order,
    table_horizontal,
    table_vertical,
):
    docs_here, doc_length, model_width = tokens.shape
    bucket_total, head_count = table_order.shape
    head_size = model_width // head_count
    score_scale = head_size ** (-0.5)
    blk_count = lax.axis_size("blk")
    me = lax.axis_index("blk")
    rows_in = tokens.reshape(doc_length, model_width)

    centres = jnp.stack([box_corners[0, 0] + box_corners[2, 0], box_corners[1, 0] + box_corners[3, 0]])
    centres = centres.astype(jnp.float32)
    centre_slots = [centres] + [exchange(centres, "blk", s) for s in range(1, blk_count)]
    core_rows = exchange(rows_in, "blk", 1)
    far_rows = exchange(rows_in, "blk", 2)
    row_slots = [rows_in, core_rows, far_rows, exchange(far_rows, "blk", 1)]
    centres_all = jnp.concatenate(centre_slots, axis=1).astype(jnp.int32)
    centres_own = centres.astype(jnp.int32)

    inside = jnp.arange(doc_length, dtype=jnp.int32)
    key_place = jnp.concatenate([(me ^ s) * doc_length + inside for s in range(blk_count)])
    query_place = me * doc_length + inside
    order = bucketize(key_place[:, None] - query_place[None, :], ORDER_LIMITS)
    across = bucketize(centres_all[0][:, None] - centres_own[0][None, :], BOX_LIMITS) + bucket_total
    down = bucketize(centres_all[1][:, None] - centres_own[1][None, :], BOX_LIMITS) + 2 * bucket_total
    tile = jnp.arange(LANES, dtype=jnp.int32)
    near = [bucketize(t * LANES + tile[:, None] - tile[None, :], ORDER_LIMITS) for t in range(-2, 3)]
    near = jnp.concatenate(near, axis=0)
    tiles = (key_place[::LANES, None] - query_place[None, ::LANES]) // LANES
    tiles = (jnp.clip(tiles, -2, 2) + 2) * LANES
    first_key = key_place[::64]
    beyond = jnp.where(first_key > query_place[-1], first_key - query_place[-1], query_place[0] - (first_key + 63))
    far_order = jnp.where(beyond >= ORDER_LIMITS[-1], 15 + 16 * (first_key > query_place[-1]), 0).astype(jnp.int32)
    tables = jnp.concatenate([table_order, table_horizontal, table_vertical], axis=0).T
    tables = jnp.round((tables + 5.0) * UNIT).astype(jnp.int32)
    tables = tables[0::2] + FIELD * tables[1::2]
    tables = jnp.pad(tables, ((0, 0), (0, LANES - 3 * bucket_total)))[:, None, :]

    query_t = (einsum("df,td->ft", w_query, rows_in) + b_query[:, None]).astype(jnp.bfloat16)
    query_t = query_t * jnp.bfloat16(score_scale * UNIT)
    bias_column = jnp.broadcast_to(b_value[:, None], (model_width, LANES))
    vectors_in = jnp.stack([b_out, gain_first, shift_first, b_down, gain_second, shift_second, b_out, b_out])
    projected = project(rows_in, core_rows, w_key, w_value, bias_column)
    keys, value_t = project(row_slots[2], row_slots[3], w_key, w_value, bias_column, projected)
    keys, order, vectors_in, far_order = lax.optimization_barrier((keys, order, vectors_in, far_order))
    raised, mixed_t, inverse_t, mixed_low = attention_forward(
        tiles, tables, near, across, down, query_t, keys, value_t
    )

    here = lax.axis_index("docs")
    place = jnp.stack([me, here % 2, (here // 2) % 2]).astype(jnp.int32)
    cotangents = cotangent.reshape(doc_length, model_width)
    output, grad_pre2, normal, scale, low_t, slope, sent_down, kept_down, upper_sums = upper(
        place, mixed_low, rows_in, cotangents, w_out, w_up, w_down, vectors_in, b_up
    )
    parts_down = in_blocks(sent_down, kept_down)
    sent_up, kept_up, sent_out, kept_out, grad_pre1, upstream_t, lower_sums, up_sums = lower(
        place, grad_pre2, normal, scale, low_t, slope, mixed_low, w_out, w_up, w_down, vectors_in
    )
    parts_up = in_blocks(sent_up, kept_up)
    parts_out = in_blocks(sent_out, kept_out)
    output = output.reshape(tokens.shape)

    sides = {"y": 0, "x": here % 2, "a": (here // 2) % 2}
    line = Line()
    line.mark(upstream_t)
    def begin(name, parts, order, back):
        kept, got = parts
        (got,) = line.after(got)
        line.begin(name, reduce_rows(kept, got, order, back, sides), name == "last")

    begin("down", parts_down, "axy", "xa")
    begin("up", parts_up, "xay", "ax")
    begin("out", parts_out, "yxa", "xa")
    (upstream_t,) = line.after(upstream_t)
    grad_query_t, grad_keys, grad_values, sent_last, kept_last = attention_backward(
        place, far_order, order, across, down, raised, query_t, upstream_t, inverse_t, mixed_t, value_t, keys, row_slots,
        (upper_sums, lower_sums, up_sums), score_scale, 1.0 / UNIT
    )
    parts_last = in_blocks(sent_last, kept_last)
    line.mark(sent_last)
    line.mark(mark_of(line.last, 20000000000))
    line.go(["up"])
    begin("last", parts_last, "ayx", "ax")
    line.go(["down", "out", "up"])
    grad_keys, grad_values = line.after(grad_keys, grad_values)
    shared_sent, shared_near, shared_far = project_back(grad_keys, grad_values, w_key, w_value)
    line.mark(shared_sent)
    near = exchange(shared_sent, "blk", 1)
    line.mark(mark_of(line.last, 5000000000))
    line.go(["up", "out", "down"])
    line.mark(mark_of(line.last, 20000000000))
    line.go(["last", "out", "down", "up"])
    line.go(["last", "out"])
    (near,) = line.after(near)
    near = near.astype(jnp.float32)
    far_sent = (shared_far.astype(jnp.float32) + near[doc_length:]).astype(jnp.bfloat16)
    line.mark(far_sent)
    far = exchange(far_sent, "blk", 2)
    line.mark(mark_of(line.last, 20000000000))
    line.go(["last", "out", "down", "up", "out"])
    line.go(["last", "down"])
    line.go(["last", "up"])
    grad_query_t, far = line.after(grad_query_t, far)
    grad_inputs = grad_pre1 + einsum("ft,df->td", grad_query_t, w_query) + shared_near.astype(jnp.float32) + near[:doc_length]
    grad_tokens = (grad_inputs + far.astype(jnp.float32)).astype(jnp.bfloat16).reshape(tokens.shape)
    line.mark(grad_tokens)
    line.go(["down", "last"])
    line.finish(["down", "last", "up", "out"])

    (grad_w_down, grad_w_up, grad_w_out) = [line.results[name].astype(jnp.float32) for name in ("down", "up", "out")]
    last = line.results["last"]
    grads = [last[:, n * model_width : (n + 1) * model_width].astype(jnp.float32) for n in range(3)]
    grad_w_query, grad_w_key, grad_w_value = grads
    flat = last[:, 3 * model_width :].astype(jnp.float32)
    tiles_each = model_width // LANES
    rows = model_width // blk_count

    def vectors(first):
        block = flat[first : first + 8 * tiles_each].reshape(tiles_each, 8, LANES)
        return jnp.transpose(block, (1, 0, 2)).reshape(8, model_width)

    each = lax.dynamic_slice_in_dim(vectors(0), me * rows, rows, 1)
    grad_b_up = lax.dynamic_slice_in_dim(vectors(8 * tiles_each), me, 1, 0)[0]
    table_rows = bucket_total // blk_count
    table_out = []
    for number in range(3):
        first = 16 * tiles_each + number * bucket_total + me * table_rows
        table_out.append(lax.dynamic_slice_in_dim(flat, first, table_rows, 0)[:, :head_count])
    small_out = [each[7], each[6], each[5], each[3], each[4], grad_b_up, each[2], each[0], each[1], *table_out]
    return (
        output,
        grad_tokens,
        grad_w_query,
        small_out[0],
        grad_w_key,
        grad_w_value,
        small_out[1],
        grad_w_out,
        small_out[2],
        small_out[3],
        small_out[4],
        grad_w_up,
        small_out[5],
        grad_w_down,
        small_out[6],
        small_out[7],
        small_out[8],
        small_out[9],
        small_out[10],
        small_out[11],
    )


def solution(mesh):
    return jax.shard_map(
        body,
        mesh=mesh,
        in_specs=(
            P("docs", "blk", None),
            P(None, "docs", "blk"),
            P("docs", "blk", None),
            P(),
            P(),
            P(),
            P(),
            P(),
            P(),
            P(),
            P(),
            P(),
            P(),
            P(),
            P(),
            P(),
            P(),
            P(),
            P(),
            P(),
            P(),
        ),
        out_specs=(
            P("docs", "blk", None),
            P("docs", "blk", None),
            P("blk", None),
            P("blk"),
            P("blk", None),
            P("blk", None),
            P("blk"),
            P("blk", None),
            P("blk"),
            P("blk"),
            P("blk"),
            P("blk", None),
            P("blk"),
            P("blk", None),
            P("blk"),
            P("blk"),
            P("blk"),
            P("blk", None),
            P("blk", None),
            P("blk", None),
        ),
        check_vma=False,
    )
```
